32 devices in a mesh: dp: 2 (over core), fsdp: 16 (over z, y, x).
Axes of the slice: x: 2, y: 2, z: 4, core: 2. Of those that a mesh axis runs over, the one named last changes fastest.
Arguments:
- patches: bfloat16 [64, 4, 117, 128], P(('dp', 'fsdp')), may hold values from -6 to 6
- prompts: bfloat16 [8, 10, 128], replicated, may hold values from -6 to 6
- cls_token: bfloat16 [128], replicated, may hold values from -6 to 6
- attention_input_weights: bfloat16 [2, 2, 128, 384], P(None, None, 'fsdp'), may hold values from -0.5 to 0.5
- attention_output_weights: bfloat16 [2, 2, 128, 128], P(None, None, 'fsdp'), may hold values from -2 to 2
- feed_input_weights: bfloat16 [2, 128, 1024], P(None, 'fsdp'), may hold values from -0.5 to 0.5
- feed_output_weights: bfloat16 [2, 512, 128], P(None, 'fsdp'), may hold values from -0.25 to 0.25
- token_operator: bfloat16 [2, 128, 128], replicated, may hold values from -0.5 to 0.5
- norm_gains: float32 [2, 4, 128], replicated, may hold values from 0.5 to 1.5
- branch_scales: float32 [2, 4, 128], replicated, may hold values from 0.1 to 1.9
- var_counts: int32 [8], replicated, may hold values from 1 to 4, as said below
- dataset_ids: int32 [64], P(('dp', 'fsdp')), may hold values from 0 to 7
- cotangent: bfloat16 [64, 4, 128, 128], P(('dp', 'fsdp')), may hold values from -40 to 40
- adjust_cotangent: bfloat16 [64, 4, 128, 128], P(('dp', 'fsdp')), may hold values from -40 to 40
Outputs:
- output: bfloat16 [64, 4, 128, 128], P(('dp', 'fsdp'))
- patch_grad: float32 [64, 4, 117, 128], P(('dp', 'fsdp'))
- prompt_grad: float32 [8, 10, 128], replicated
- cls_grad: float32 [128], replicated
- attn_in_grad: float32 [2, 2, 128, 384], P(None, None, 'fsdp')
- attn_out_grad: float32 [2, 2, 128, 128], P(None, None, 'fsdp')
- mix_in_grad: float32 [2, 128, 1024], P(None, 'fsdp')
- mix_out_grad: float32 [2, 512, 128], P(None, 'fsdp')
- token_mix_grad: float32 [2, 128, 128], replicated
- gains_grad: float32 [2, 4, 128], replicated
- scales_grad: float32 [2, 4, 128], replicated
- adjust_prompt_grad: float32 [8, 10, 128], replicated
- adjust_cls_grad: float32 [128], replicated
The draws below stay inside these ranges and needn't reach their ends.
Inputs may be any that keep to these rules, and one draw needn't show every extreme that they name: `var_counts`: some dataset has exactly 4 variables and another exactly 1.
All inputs are finite; a program needn't handle non-finite values.
Results may differ from the reference program's by a relative error of at most 0.02.
Values may be sent and summed in bfloat16 or wider, within the bound.
No kernel may reach another device: no remote copies, remote signals or barrier semaphores. Data moves between devices by JAX's collectives and lax.ppermute only.
A program may use at most 192 MiB of HBM per device.

```python
import math
import jax
import jax.numpy as jnp
from jax import lax

D = 128
HEADS = 8
FF = 512
PROMPT = 10
PATCHES = 117
VMAX = 4
ITEMS_DEV = 2
NDATA = 8
LAYERS = 2
LEN = 128
ITEMS = 64


def draw_var_counts(key, part):
    key = jax.random.fold_in(key, 11)
    first_key, second_key, third_key = jax.random.split(key, 3)
    counts = jax.random.randint(first_key, (NDATA,), 1, VMAX + 1)
    widest = jax.random.randint(second_key, (), 0, NDATA)
    narrow = (widest + 1 + jax.random.randint(third_key, (), 0, NDATA - 1)) % NDATA
    slots = jnp.arange(NDATA)
    counts = jnp.where(slots == widest, VMAX, counts)
    counts = jnp.where(slots == narrow, 1, counts)
    return counts.astype(jnp.int32)


def rising_field(key):
    first_key = jax.random.fold_in(key, 0)
    third_key = jax.random.fold_in(key, 2)
    shape = (ITEMS, VMAX, LEN, D)
    rising = jnp.exp(math.log(3.0) * jnp.arange(ITEMS, dtype=jnp.float32) / max(ITEMS - 1, 1))
    base = jax.random.normal(first_key, shape, jnp.float32)
    channel = jnp.exp(jax.random.uniform(third_key, (D,), jnp.float32, 0.0, math.log(2.0)))
    return base * channel * rising[:, None, None, None]


def draw_cotangent(key, part):
    key = jax.random.fold_in(key, 23)
    return rising_field(key).astype(jnp.bfloat16)


def draw_adjust_cotangent(key, part):
    key = jax.random.fold_in(key, 37)
    return rising_field(key).astype(jnp.bfloat16)


def place_ends(values, rng, least, top_value):
    shape = values.shape
    index_at = [jax.random.randint(jax.random.fold_in(rng, axis), (), 0, shape[axis]) for axis in range(len(shape))]
    values = values.at[tuple(index_at)].set(least)
    longest = shape.index(max(shape))
    index_at[longest] = (index_at[longest] + 1) % shape[longest]
    return values.at[tuple(index_at)].set(top_value)


def level_of(own_key, dims, shards, low, top_value):
    loudness = 1.0
    for axis_at, blocks in shards:
        heights = jax.random.uniform(jax.random.fold_in(jax.random.fold_in(own_key, 6), axis_at), (blocks,), jnp.float32, low / len(shards), top_value / len(shards))
        loudness = loudness * jnp.repeat(jnp.exp(heights), dims[axis_at] // blocks).reshape((-1,) + (1,) * (len(dims) - 1 - axis_at))
    return loudness


def centred(own_key, dims, deviation, reach, shards=(), kind=jnp.bfloat16):
    array = deviation * jax.random.normal(own_key, dims, jnp.float32)
    if shards:
        array = array * level_of(own_key, dims, shards, -0.22, 0.18)
    return jnp.clip(array, -reach, reach).astype(kind)


def setup_inputs(seed: int = 0) -> dict:
    key_of = jax.random.split(jax.random.key(seed), 15)
    return {
        "patches": centred(key_of[0], (ITEMS, VMAX, PATCHES, D), 1.0, 6.0, ((0, 32),)),
        "prompts": centred(key_of[1], (NDATA, PROMPT, D), 1.0, 6.0),
        "cls_token": centred(key_of[2], (D,), 1.0, 6.0),
        "attention_input_weights": centred(key_of[3], (LAYERS, 2, D, 3 * D), D ** -0.5, 0.5, ((2, 16),)),
        "attention_output_weights": centred(key_of[4], (LAYERS, 2, D, D), (D // 16) ** -0.5, 2.0, ((2, 16),)),
        "feed_input_weights": centred(key_of[5], (LAYERS, D, 2 * FF), D ** -0.5, 0.5, ((1, 16),)),
        "feed_output_weights": centred(key_of[6], (LAYERS, FF, D), FF ** -0.5, 0.25, ((1, 16),)),
        "token_operator": centred(key_of[7], (LAYERS, LEN, LEN), LEN ** -0.5, 0.5),
        "norm_gains": jnp.clip(1.0 + 0.1 * jax.random.normal(key_of[8], (LAYERS, 4, D), jnp.float32), 0.5, 1.5),
        "branch_scales": jnp.clip(1.0 + 0.18 * jax.random.normal(key_of[9], (LAYERS, 4, D), jnp.float32), 0.1, 1.9),
        "var_counts": draw_var_counts(jax.random.fold_in(key_of[14], 71), 0),
        "dataset_ids": place_ends(jax.random.randint(key_of[11], (ITEMS,), 0, NDATA), jax.random.fold_in(key_of[11], 1), 0, NDATA - 1).astype(jnp.int32),
        "cotangent": draw_cotangent(jax.random.fold_in(key_of[14], 71), 0),
        "adjust_cotangent": draw_adjust_cotangent(jax.random.fold_in(key_of[14], 71), 0),
    }


EPSILON = 1e-05
NEG_FILL = -1000000000.0
PRECISE_MODE = lax.Precision.HIGHEST

@jax.custom_vjp
def reduced_cast(v):
    return lax.optimization_barrier(v.astype(jnp.bfloat16)).astype(jnp.float32)

@jax.custom_vjp
def reduced_cast_backward(v):
    return v

def low_keep(v):
    return (reduced_cast(v), None)

def low_pass(kept, grad):
    return (grad,)

def back_keep(v):
    return (v, None)

def back_low(kept, grad):
    return (reduced_cast(grad),)
reduced_cast.defvjp(low_keep, low_pass)
reduced_cast_backward.defvjp(back_keep, back_low)

def norm_rows(stream, gain_vec):
    centered = stream - lax.optimization_barrier(jnp.mean(stream, axis=-1, keepdims=True))
    variance = lax.optimization_barrier(jnp.mean(centered * centered, axis=-1, keepdims=True))
    return centered * lax.rsqrt(variance + EPSILON) * gain_vec

def split_heads(block):
    return block.reshape(block.shape[:-1] + (HEADS, D // HEADS))

def layer_forward(stream, attention_input_weights, attention_output_weights, feed_input_weights, feed_output_weights, token_operator, gain_vec, scale_vec, key_mask):
    factor = (D // HEADS) ** (-0.5)
    normalized_rows = reduced_cast(norm_rows(stream, gain_vec[0]))
    query_key_value_rows = reduced_cast(reduced_cast_backward(jnp.einsum('mfxu,uz->mfxz', normalized_rows, attention_input_weights[0], precision=PRECISE_MODE)))
    queries = split_heads(query_key_value_rows[..., :D])
    key_rows = split_heads(query_key_value_rows[..., D:2 * D])
    value_rows = split_heads(query_key_value_rows[..., 2 * D:])
    scores = reduced_cast_backward(jnp.einsum('bvqhc,bvkhc->bvhqk', queries, key_rows, precision=PRECISE_MODE) * factor)
    attn_prob = reduced_cast(jax.nn.softmax(scores, axis=-1))
    mixed_state = reduced_cast(reduced_cast_backward(jnp.einsum('bvhqk,bvkhc->bvqhc', attn_prob, value_rows, precision=PRECISE_MODE)))
    mixed_state = mixed_state.reshape(stream.shape)
    branch_output = reduced_cast_backward(jnp.einsum('mfxu,uz->mfxz', mixed_state, attention_output_weights[0], precision=PRECISE_MODE))
    stream = stream + scale_vec[0] * branch_output
    normalized_rows = reduced_cast(norm_rows(stream, gain_vec[1]))
    query_key_value_rows = reduced_cast(reduced_cast_backward(jnp.einsum('mfxu,uz->mfxz', normalized_rows, attention_input_weights[1], precision=PRECISE_MODE)))
    queries = split_heads(query_key_value_rows[..., :D])
    key_rows = split_heads(query_key_value_rows[..., D:2 * D])
    value_rows = split_heads(query_key_value_rows[..., 2 * D:])
    scores = reduced_cast_backward(jnp.einsum('bqlhc,bklhc->blhqk', queries, key_rows, precision=PRECISE_MODE) * factor)
    scores = jnp.where(key_mask[:, None, None, None, :], scores, NEG_FILL)
    attn_prob = reduced_cast(jax.nn.softmax(scores, axis=-1))
    mixed_state = reduced_cast(reduced_cast_backward(jnp.einsum('blhqk,bklhc->bqlhc', attn_prob, value_rows, precision=PRECISE_MODE)))
    mixed_state = mixed_state.reshape(stream.shape)
    branch_output = reduced_cast_backward(jnp.einsum('mfxu,uz->mfxz', mixed_state, attention_output_weights[1], precision=PRECISE_MODE))
    stream = stream + scale_vec[1] * branch_output
    normalized_rows = reduced_cast(norm_rows(stream, gain_vec[2]))
    branch_output = reduced_cast_backward(jnp.einsum('xf,pyfi->pyxi', token_operator, normalized_rows, precision=PRECISE_MODE))
    stream = stream + scale_vec[2] * branch_output
    normalized_rows = reduced_cast(norm_rows(stream, gain_vec[3]))
    joint_rows = reduced_cast_backward(jnp.einsum('mfxu,uz->mfxz', normalized_rows, feed_input_weights, precision=PRECISE_MODE))
    hidden_state = reduced_cast(jax.nn.silu(joint_rows[..., :FF]) * joint_rows[..., FF:])
    branch_output = reduced_cast_backward(jnp.einsum('mkni,ix->mknx', hidden_state, feed_output_weights, precision=PRECISE_MODE))
    return stream + scale_vec[3] * branch_output

def forward(patch_vals, params, group_ids, var_counts):
    prompt_vals, cls_vals, attention_input_weights, attention_output_weights, feed_input_weights, feed_output_weights, token_operator, norm_gains, branch_scales = params
    group_size = patch_vals.shape[0]
    prompt_rows = jnp.broadcast_to(prompt_vals[group_ids][:, None], (group_size, VMAX, PROMPT, D))
    cls_rows = jnp.broadcast_to(cls_vals, (group_size, VMAX, 1, D))
    stream = jnp.concatenate([prompt_rows, patch_vals, cls_rows], axis=2)
    key_mask = jnp.arange(VMAX, dtype=jnp.int32)[None, :] < var_counts[group_ids][:, None]
    for layer_idx in range(LAYERS):
        stream = layer_forward(stream, attention_input_weights[layer_idx], attention_output_weights[layer_idx], feed_input_weights[layer_idx], feed_output_weights[layer_idx], token_operator[layer_idx], norm_gains[layer_idx], branch_scales[layer_idx], key_mask)
    return stream

def reference(patches, prompts, cls_token, attention_input_weights, attention_output_weights, feed_input_weights, feed_output_weights, token_operator, norm_gains, branch_scales, var_counts, dataset_ids, cotangent, adjust_cotangent):
    params = (prompts.astype(jnp.float32), cls_token.astype(jnp.float32), attention_input_weights.astype(jnp.float32), attention_output_weights.astype(jnp.float32), feed_input_weights.astype(jnp.float32), feed_output_weights.astype(jnp.float32), token_operator.astype(jnp.float32), norm_gains, branch_scales)
    group_count = ITEMS // ITEMS_DEV

    def group_step(running, group_idx):
        totals_now, adjust_prompt_now, adjust_cls_now = running
        offset = (group_idx * ITEMS_DEV).astype(jnp.int32)
        patch_vals = lax.dynamic_slice_in_dim(patches, offset, ITEMS_DEV, 0).astype(jnp.float32)
        group_ids = lax.dynamic_slice_in_dim(dataset_ids, offset, ITEMS_DEV, 0)
        group_cot = lax.dynamic_slice_in_dim(cotangent, offset, ITEMS_DEV, 0).astype(jnp.float32)
        group_adjust = lax.dynamic_slice_in_dim(adjust_cotangent, offset, ITEMS_DEV, 0).astype(jnp.float32)

        def run_group(patch_in, param_in):
            return forward(patch_in, param_in, group_ids, var_counts)
        result, pullback = jax.vjp(run_group, patch_vals, params)
        grad_patch, grad_params = pullback(group_cot)
        adjust_grads = pullback(group_adjust)[1]
        totals_now = jax.tree.map(jnp.add, totals_now, grad_params)
        adjust_prompt_now = adjust_prompt_now + adjust_grads[0]
        adjust_cls_now = adjust_cls_now + adjust_grads[1]
        return ((totals_now, adjust_prompt_now, adjust_cls_now), (result.astype(jnp.bfloat16), grad_patch))
    zeros = jax.tree.map(jnp.zeros_like, params)
    start = (zeros, jnp.zeros((NDATA, PROMPT, D), jnp.float32), jnp.zeros((D,), jnp.float32))
    (totals, adjust_prompt, adjust_cls), (results, patch_grads) = lax.scan(group_step, start, jnp.arange(group_count, dtype=jnp.int32))
    output = results.reshape(ITEMS, VMAX, LEN, D)
    patch_grad = patch_grads.reshape(ITEMS, VMAX, PATCHES, D)
    return (output, patch_grad, totals[0], totals[1], totals[2], totals[3], totals[4], totals[5], totals[6], totals[7], totals[8], adjust_prompt, adjust_cls)
```

```python
import functools

import jax
import jax.numpy as jnp
from jax import lax
from jax.experimental import pallas as pl
from jax.experimental.pallas import tpu as pltpu
from jax.sharding import PartitionSpec as P

HEADS = 8
EPSILON = 1e-05
NEG_FILL = -1000000000.0
BF = jnp.bfloat16
F32 = jnp.float32

COL_IN = (0, 384)
COL_OUT = (768, 896)
COL_FEED = 1024
COL_DOWN = 2048
COLS = 2560
SHARDS = 16
STEP_BITS = (2, 3, 0, 1)


def dot_nn(a, b):
    return lax.dot_general(a, b, (((1,), (0,)), ((), ())), preferred_element_type=F32)


def dot_nt(a, b):
    return lax.dot_general(a, b, (((1,), (1,)), ((), ())), preferred_element_type=F32)


def norm_cols(x):
    centered = x - jnp.mean(x, axis=0, keepdims=True)
    inv = lax.rsqrt(jnp.mean(centered * centered, axis=0, keepdims=True) + EPSILON)
    return centered * inv, inv


def norm_cols_back(dn, gain, xhat, inv):
    e = dn * gain
    m1 = jnp.mean(e, axis=0, keepdims=True)
    m2 = jnp.mean(e * xhat, axis=0, keepdims=True)
    return inv * (e - m1 - xhat * m2)


def fold(part):
    return part[:, :128] + part[:, 128:]


def dp_of(split):
    return lax.axis_index("dp") if split else 0


def pack_kernel(attn_in_ref, attn_out_ref, feed_in_ref, feed_out_ref, out_ref):
    l = lax.axis_index("dp")
    down = feed_out_ref[l].astype(F32)
    parts = [attn_in_ref[l, 0], attn_in_ref[l, 1], attn_out_ref[l, 0], attn_out_ref[l, 1], feed_in_ref[l]]
    parts = [part.astype(F32) for part in parts] + [down[8 * a : 8 * a + 8] for a in range(4)]
    row = jnp.concatenate(parts, axis=1).astype(BF)
    for f in range(SHARDS):
        out_ref[f] = row


def tower_kernel(
    split,
    ids_ref, counts_ref, wmine_ref, wother_ref, tok_ref, gains_ref, scales_ref, patches_ref, prompts_ref,
    cls_ref, cot_ref, adj_ref,
    out_ref, pgrad_ref, gbig_ref, gsmall_ref,
    w_ref, wd_ref, wt_ref, wdt_ref, colb_ref, tokscr_ref, h_ref, g_ref, xh_ref, inv_ref,
    qkvt_ref, pb_ref, ot_ref, qkvv_ref, pv_ref, ov_ref, qbd_ref, dob_ref, hid_ref, du_ref, dqkv_ref,
    dov_ref, ga_ref, gd_ref, gt_ref, gacc_ref,
):
    dp = dp_of(split)
    layers = 2
    chunks = 4
    items = 2

    for l in range(layers):
        for pair in range(SHARDS // 2):
            lo = jnp.where(dp == l, wmine_ref[2 * pair].astype(F32), wother_ref[2 * pair].astype(F32))
            hi = jnp.where(dp == l, wmine_ref[2 * pair + 1].astype(F32), wother_ref[2 * pair + 1].astype(F32))
            w_ref[l, 16 * pair : 16 * pair + 16, :] = jnp.concatenate([lo[:, :COL_DOWN], hi[:, :COL_DOWN]], axis=0).astype(BF)
            for half, part in enumerate((lo, hi)):
                base = 64 * pair + 32 * half
                wd_ref[l, base : base + 32, :] = jnp.concatenate(
                    [part[:, COL_DOWN + 128 * a : COL_DOWN + 128 * a + 128] for a in range(4)], axis=0
                ).astype(BF)
        for block in range(COL_DOWN // 128):
            wt_ref[l, 128 * block : 128 * block + 128, :] = w_ref[l, :, 128 * block : 128 * block + 128].T
        for block in range(4):
            wdt_ref[l, :, 128 * block : 128 * block + 128] = wd_ref[l, 128 * block : 128 * block + 128, :].T
        for k in range(4):
            for offset, rows in ((0, gains_ref), (4, scales_ref)):
                col = jnp.broadcast_to(rows[l, k : k + 1, :], (128, 128)).T
                colb_ref[l * 8 + offset + k, :, 0:128] = col
                colb_ref[l * 8 + offset + k, :, 128:256] = col

    for b in range(items):
        ident = ids_ref[b]
        for v in range(4):
            bv = 4 * b + v
            tokscr_ref[bv, 0:10, :] = prompts_ref[ident].astype(F32)
            tokscr_ref[bv, 10:127, :] = patches_ref[b, v].astype(F32)
            tokscr_ref[bv, 127:128, :] = cls_ref[...].astype(F32)
            lanes = slice(128 * (v % 2), 128 * (v % 2) + 128)
            h_ref[2 * b + v // 2, :, lanes] = tokscr_ref[bv].T
            g_ref[0, 2 * b + v // 2, :, lanes] = cot_ref[b, v].astype(F32).T
            g_ref[1, 2 * b + v // 2, :, lanes] = adj_ref[b, v].astype(F32).T

    qbd_ref[...] = jnp.zeros_like(qbd_ref)
    dob_ref[...] = jnp.zeros_like(dob_ref)

    head_row = lax.broadcasted_iota(jnp.int32, (8, 256), 0)
    head_col = (lax.broadcasted_iota(jnp.int32, (8, 256), 1) % 128) // 16
    gather_heads = jnp.where(head_row == head_col, 1.0, 0.0).astype(BF)
    spread_row = lax.broadcasted_iota(jnp.int32, (128, 8), 0) // 16
    spread_col = lax.broadcasted_iota(jnp.int32, (128, 8), 1)
    spread_heads = jnp.where(spread_row == spread_col, 1.0, 0.0).astype(BF)

    def head_sums(left, rights):
        his, los = [], []
        for right in rights:
            prod = left * right
            hi = prod.astype(BF)
            his.append(hi)
            los.append((prod - hi.astype(F32)).astype(BF))
        both = jnp.concatenate([jnp.concatenate(his, axis=1), jnp.concatenate(los, axis=1)], axis=0)
        return dot_nn(gather_heads, both)

    def diag_heads(target_ref, s, rows):
        for head in range(HEADS):
            target_ref[s, 16 * head : 16 * head + 16, 128 * head : 128 * head + 128] = rows[16 * head : 16 * head + 16]

    def gain(l, k):
        return colb_ref[l * 8 + k]

    def scale(l, k):
        return colb_ref[l * 8 + 4 + k]

    def keep_norm(l, k, c, x):
        xhat, inv = norm_cols(x)
        xh_ref[l * 4 + k, c] = xhat
        inv_ref[l * 4 + k, c] = inv
        return (xhat * gain(l, k)).astype(BF)

    def time_forward(l, c):
        x = h_ref[c]
        n = keep_norm(l, 0, c, x)
        qkv = dot_nn(wt_ref[l, 0:384, :], n)
        queries = (qkv[:128] * 0.25).astype(BF)
        keys = qkv[128:256].astype(BF)
        values = qkv[256:].astype(BF)
        qkvt_ref[l, c, 0:128, :] = queries
        qkvt_ref[l, c, 128:256, :] = keys
        qkvt_ref[l, c, 256:384, :] = values
        for s in range(2):
            lanes = slice(128 * s, 128 * s + 128)
            diag_heads(qbd_ref, s, queries[:, lanes])
            key_rows = keys[:, lanes].T
            for hp in range(4):
                span = slice(256 * hp, 256 * hp + 256)
                rows = slice(32 * hp, 32 * hp + 32)
                scores = dot_nn(key_rows, qbd_ref[s, :, span])
                shifted = jnp.exp(scores - jnp.max(scores, axis=0, keepdims=True))
                prob = (shifted * (1.0 / jnp.sum(shifted, axis=0, keepdims=True))).astype(BF)
                pb_ref[l, 2 * c + s, :, span] = prob
                mixed = dot_nn(values[rows, lanes], prob)
                ot_ref[l, c, 32 * hp : 32 * hp + 16, lanes] = mixed[:16, :128].astype(BF)
                ot_ref[l, c, 32 * hp + 16 : 32 * hp + 32, lanes] = mixed[16:, 128:].astype(BF)
        branch = dot_nn(wt_ref[l, COL_OUT[0] : COL_OUT[0] + 128, :], ot_ref[l, c])
        h_ref[c] = x + scale(l, 0) * branch

    def var_forward(l, b):
        for cc in range(2):
            c = 2 * b + cc
            n = keep_norm(l, 1, c, h_ref[c])
            qkv = dot_nn(wt_ref[l, COL_IN[1] : COL_IN[1] + 384, :], n)
            qkvv_ref[l, c, 0:128, :] = (qkv[:128] * 0.25).astype(BF)
            qkvv_ref[l, c, 128:384, :] = qkv[128:].astype(BF)
        count = counts_ref[ids_ref[b]]

        def slot(first, i):
            lanes = slice(128 * (i % 2), 128 * (i % 2) + 128)
            return qkvv_ref[l, 2 * b + i // 2, first : first + 128, lanes].astype(F32)

        key_slots = [slot(128, j) for j in range(4)]
        value_slots = [slot(256, j) for j in range(4)]
        for i in range(4):
            scores = head_sums(slot(0, i), key_slots)
            parts = [scores[:, 128 * j : 128 * j + 128] for j in range(4)]
            parts = [jnp.where(jnp.full((8, 128), count, jnp.int32) > j, parts[j], NEG_FILL) for j in range(4)]
            top = jnp.maximum(jnp.maximum(parts[0], parts[1]), jnp.maximum(parts[2], parts[3]))
            shifted = [jnp.exp(part - top) for part in parts]
            total = 1.0 / ((shifted[0] + shifted[1]) + (shifted[2] + shifted[3]))
            prob = jnp.concatenate([part * total for part in shifted], axis=1)
            pv_ref[l, b, i] = prob
            spread = dot_nn(spread_heads, prob.astype(BF))
            mixed = spread[:, :128] * value_slots[0]
            for j in range(1, 4):
                mixed = mixed + spread[:, 128 * j : 128 * j + 128] * value_slots[j]
            lanes = slice(128 * (i % 2), 128 * (i % 2) + 128)
            ov_ref[l, 2 * b + i // 2, :, lanes] = mixed.astype(BF)
        for cc in range(2):
            c = 2 * b + cc
            branch = dot_nn(wt_ref[l, COL_OUT[1] : COL_OUT[1] + 128, :], ov_ref[l, c])
            h_ref[c] = h_ref[c] + scale(l, 1) * branch

    def tail_forward(l, c):
        x = h_ref[c]
        n = keep_norm(l, 2, c, x)
        mix = [dot_nt(n[:, 128 * s : 128 * s + 128], tok_ref[l]) for s in range(2)]
        x = x + scale(l, 2) * jnp.concatenate(mix, axis=1)
        n = keep_norm(l, 3, c, x)
        for z in range(4):
            gate = dot_nn(wt_ref[l, COL_FEED + 128 * z : COL_FEED + 128 * z + 128, :], n)
            up = dot_nn(wt_ref[l, COL_FEED + 512 + 128 * z : COL_FEED + 640 + 128 * z, :], n)
            sig = 0.5 * jnp.tanh(0.5 * gate) + 0.5
            hid_ref[128 * z : 128 * z + 128, :] = (gate * sig * up).astype(BF)
        h_ref[c] = x + scale(l, 3) * dot_nn(wdt_ref[l], hid_ref[...])

    def norm_of(l, k, c):
        xhat = xh_ref[l * 4 + k, c]
        return xhat, inv_ref[l * 4 + k, c], (xhat * gain(l, k)).astype(BF)

    def pass_on(l, k, c, x, dn, xhat, inv):
        if x == 0:
            gacc_ref[l * 4 + k] += fold(dn * xhat)
        g_ref[x, c] += norm_cols_back(dn, gain(l, k), xhat, inv)

    def feed_backward(l, c):
        xhat, inv, n = norm_of(l, 3, c)
        dz = [(scale(l, 3) * g_ref[x, c]).astype(BF) for x in range(2)]
        for z in range(4):
            rows = slice(128 * z, 128 * z + 128)
            gate = dot_nn(wt_ref[l, COL_FEED + 128 * z : COL_FEED + 128 * z + 128, :], n)
            up = dot_nn(wt_ref[l, COL_FEED + 512 + 128 * z : COL_FEED + 640 + 128 * z, :], n)
            sig = 0.5 * jnp.tanh(0.5 * gate) + 0.5
            act = gate * sig
            hid_ref[rows, :] = (act * up).astype(BF)
            slope = up * (sig * (1.0 + gate * (1.0 - sig)))
            for x in range(2):
                dhid = dot_nn(wd_ref[l, rows, :], dz[x])
                du_ref[x, 128 * z : 128 * z + 128, :] = (dhid * slope).astype(BF)
                du_ref[x, 512 + 128 * z : 640 + 128 * z, :] = (dhid * act).astype(BF)
        ga_ref[:, COL_FEED:COL_DOWN] += dot_nt(n, du_ref[0])
        gd_ref[...] += dot_nt(hid_ref[...], dz[0])
        for x in range(2):
            dn = dot_nn(w_ref[l, :, COL_FEED:COL_DOWN], du_ref[x])
            pass_on(l, 3, c, x, dn, xhat, inv)

    def token_backward(l, c):
        xhat, inv, n = norm_of(l, 2, c)
        for x in range(2):
            dy = (scale(l, 2) * g_ref[x, c]).astype(BF)
            dn = []
            for s in range(2):
                part = dy[:, 128 * s : 128 * s + 128]
                dn.append(dot_nn(part, tok_ref[l]))
                if x == 0:
                    gt_ref[l] += dot_nn(part.T, n[:, 128 * s : 128 * s + 128])
            pass_on(l, 2, c, x, jnp.concatenate(dn, axis=1), xhat, inv)

    def var_backward(l, b):
        def slot(first, i):
            lanes = slice(128 * (i % 2), 128 * (i % 2) + 128)
            return qkvv_ref[l, 2 * b + i // 2, first : first + 128, lanes].astype(F32)

        for x in range(2):
            for cc in range(2):
                c = 2 * b + cc
                dt = (scale(l, 1) * g_ref[x, c]).astype(BF)
                dov_ref[cc] = dot_nn(w_ref[l, :, COL_OUT[1] : COL_OUT[1] + 128], dt).astype(BF)
                if x == 0:
                    ga_ref[:, COL_OUT[1] : COL_OUT[1] + 128] += dot_nt(ov_ref[l, c], dt)
            value_slots = [slot(256, j) for j in range(4)]
            dkeys = [None] * 4
            dvalues = [None] * 4
            for i in range(4):
                lanes = slice(128 * (i % 2), 128 * (i % 2) + 128)
                grad = dov_ref[i // 2, :, lanes].astype(F32)
                query = slot(0, i)
                prob = pv_ref[l, b, i]
                weighted = prob * head_sums(grad, value_slots)
                total = (weighted[:, :128] + weighted[:, 128:256]) + (weighted[:, 256:384] + weighted[:, 384:])
                ds = weighted - prob * jnp.concatenate([total] * 4, axis=1)
                ds_wide = dot_nn(spread_heads, ds.astype(BF))
                p_wide = dot_nn(spread_heads, prob.astype(BF))
                dquery = None
                for j in range(4):
                    ds_j = ds_wide[:, 128 * j : 128 * j + 128]
                    p_j = p_wide[:, 128 * j : 128 * j + 128]
                    terms = (ds_j * slot(128, j), ds_j * query, p_j * grad)
                    dquery = terms[0] if dquery is None else dquery + terms[0]
                    dkeys[j] = terms[1] if dkeys[j] is None else dkeys[j] + terms[1]
                    dvalues[j] = terms[2] if dvalues[j] is None else dvalues[j] + terms[2]
                dqkv_ref[i // 2, 0:128, lanes] = (0.25 * dquery).astype(BF)
            for j in range(4):
                lanes = slice(128 * (j % 2), 128 * (j % 2) + 128)
                dqkv_ref[j // 2, 128:256, lanes] = dkeys[j].astype(BF)
                dqkv_ref[j // 2, 256:384, lanes] = dvalues[j].astype(BF)
            for cc in range(2):
                c = 2 * b + cc
                xhat, inv, n = norm_of(l, 1, c)
                dqkv = dqkv_ref[cc]
                if x == 0:
                    ga_ref[:, COL_IN[1] : COL_IN[1] + 384] += dot_nt(n, dqkv)
                pass_on(l, 1, c, x, dot_nn(w_ref[l, :, COL_IN[1] : COL_IN[1] + 384], dqkv), xhat, inv)

    def time_backward(l, c):
        xhat, inv, n = norm_of(l, 0, c)
        queries = qkvt_ref[l, c, 0:128, :]
        keys = qkvt_ref[l, c, 128:256, :]
        values = qkvt_ref[l, c, 256:384, :]
        grads = []
        for x in range(2):
            dt = (scale(l, 0) * g_ref[x, c]).astype(BF)
            grads.append(dot_nn(w_ref[l, :, COL_OUT[0] : COL_OUT[0] + 128], dt).astype(BF))
            if x == 0:
                ga_ref[:, COL_OUT[0] : COL_OUT[0] + 128] += dot_nt(ot_ref[l, c], dt)
        for s in range(2):
            lanes = slice(128 * s, 128 * s + 128)
            diag_heads(qbd_ref, s, queries[:, lanes])
            value_rows = values[:, lanes].T
            for x in range(2):
                diag_heads(dob_ref, 2 * x + s, grads[x][:, lanes])
            for hp in range(4):
                span = slice(256 * hp, 256 * hp + 256)
                rows = slice(32 * hp, 32 * hp + 32)
                prob_bf = pb_ref[l, 2 * c + s, :, span]
                prob = prob_bf.astype(F32)
                for x in range(2):
                    weighted = prob * dot_nn(value_rows, dob_ref[2 * x + s, :, span])
                    ds = (weighted - prob * jnp.sum(weighted, axis=0, keepdims=True)).astype(BF)
                    dvalue = dot_nt(dob_ref[2 * x + s, rows, span], prob_bf)
                    dquery = dot_nn(keys[rows, lanes], ds) * 0.25
                    dkey = dot_nt(qbd_ref[s, rows, span], ds)
                    dqkv_ref[x, 32 * hp : 32 * hp + 16, lanes] = dquery[:16, :128].astype(BF)
                    dqkv_ref[x, 32 * hp + 16 : 32 * hp + 32, lanes] = dquery[16:, 128:].astype(BF)
                    dqkv_ref[x, 128 + 32 * hp : 160 + 32 * hp, lanes] = dkey.astype(BF)
                    dqkv_ref[x, 256 + 32 * hp : 288 + 32 * hp, lanes] = dvalue.astype(BF)
        ga_ref[:, COL_IN[0] : COL_IN[0] + 384] += dot_nt(n, dqkv_ref[0])
        for x in range(2):
            pass_on(l, 0, c, x, dot_nn(w_ref[l, :, COL_IN[0] : COL_IN[0] + 384], dqkv_ref[x]), xhat, inv)

    def each(count, stage, l):
        lax.fori_loop(0, count, lambda i, carry: (stage(l, i), carry)[1], 0)

    def forward_layer(l, carry):
        each(chunks, time_forward, l)
        each(items, var_forward, l)
        each(chunks, tail_forward, l)
        return carry

    lax.fori_loop(0, layers, forward_layer, 0)
    for b in range(items):
        for v in range(4):
            lanes = slice(128 * (v % 2), 128 * (v % 2) + 128)
            out_ref[b, v] = h_ref[2 * b + v // 2, :, lanes].T.astype(BF)

    gacc_ref[...] = jnp.zeros_like(gacc_ref)
    gt_ref[...] = jnp.zeros_like(gt_ref)
    gsmall_ref[...] = jnp.zeros_like(gsmall_ref)
    rest = 1 ^ dp
    def backward_layer(step, carry):
        l = layers - 1 - step
        ga_ref[...] = jnp.zeros_like(ga_ref)
        gd_ref[...] = jnp.zeros_like(gd_ref)
        each(chunks, feed_backward, l)
        each(chunks, token_backward, l)
        each(items, var_backward, l)
        each(chunks, time_backward, l)
        l_at = l ^ dp
        for f in range(SHARDS):
            down = jnp.concatenate([gd_ref[32 * f + 8 * a : 32 * f + 8 * a + 8, :] for a in range(4)], axis=1)
            block = jnp.concatenate([ga_ref[8 * f : 8 * f + 8, :], down], axis=1)
            gbig_ref[l_at, f] = block.astype(BF)
        gains_rows = [jnp.sum(gacc_ref[l * 4 + k].T, axis=0, keepdims=True) for k in range(4)]
        sums = [
            jnp.sum(w_ref[l, :, COL_OUT[k] : COL_OUT[k] + 128].astype(F32) * ga_ref[:, COL_OUT[k] : COL_OUT[k] + 128], axis=0, keepdims=True)
            for k in range(2)
        ]
        sums.append(gains_ref[l, 2:3, :] * gains_rows[2])
        sums.append(jnp.sum(wd_ref[l].astype(F32) * gd_ref[...], axis=0, keepdims=True))
        for k in range(4):
            gsmall_ref[rest, l * 4 + k, 10:11, :] = gains_rows[k]
            gsmall_ref[rest, l * 4 + k, 11:12, :] = sums[k] / scales_ref[l, k : k + 1, :]
        for block in range(8):
            gsmall_ref[dp, 8 * l + block] = gt_ref[l, 16 * block : 16 * block + 16, :]
        return carry

    lax.fori_loop(0, layers, backward_layer, 0)

    for x in range(2):
        cls_sum = None
        for b in range(items):
            prompt_sum = None
            for v in range(4):
                lanes = slice(128 * (v % 2), 128 * (v % 2) + 128)
                tokscr_ref[4 * b + v] = g_ref[x, 2 * b + v // 2, :, lanes].T
                head = tokscr_ref[4 * b + v, 0:10, :]
                last = tokscr_ref[4 * b + v, 127:128, :]
                prompt_sum = head if prompt_sum is None else prompt_sum + head
                cls_sum = last if cls_sum is None else cls_sum + last
                if x == 0:
                    pgrad_ref[b, v] = tokscr_ref[4 * b + v, 10:127, :]
            gsmall_ref[rest, 8 * x + ids_ref[b], 0:10, :] += prompt_sum
        gsmall_ref[rest, 8 * x, 12:13, :] = cls_sum


def run_tower(split, *operands):
    vmem = pl.BlockSpec(memory_space=pltpu.VMEM)
    smem = pl.BlockSpec(memory_space=pltpu.SMEM)
    return pl.pallas_call(
        functools.partial(tower_kernel, split),
        out_shape=(
            jax.ShapeDtypeStruct((2, 4, 128, 128), BF),
            jax.ShapeDtypeStruct((2, 4, 117, 128), F32),
            jax.ShapeDtypeStruct((2, SHARDS, 8, COLS), BF),
            jax.ShapeDtypeStruct((2, 16, 16, 128), F32),
        ),
        in_specs=[smem, smem] + [vmem] * 10,
        out_specs=[vmem] * 4,
        scratch_shapes=[
            pltpu.VMEM((2, 128, COL_DOWN), BF),
            pltpu.VMEM((2, 512, 128), BF),
            pltpu.VMEM((2, COL_DOWN, 128), BF),
            pltpu.VMEM((2, 128, 512), BF),
            pltpu.VMEM((16, 128, 256), F32),
            pltpu.VMEM((8, 128, 128), F32),
            pltpu.VMEM((4, 128, 256), F32),
            pltpu.VMEM((2, 4, 128, 256), F32),
            pltpu.VMEM((8, 4, 128, 256), F32),
            pltpu.VMEM((8, 4, 1, 256), F32),
            pltpu.VMEM((2, 4, 384, 256), BF),
            pltpu.VMEM((2, 8, 128, 1024), BF),
            pltpu.VMEM((2, 4, 128, 256), BF),
            pltpu.VMEM((2, 4, 384, 256), BF),
            pltpu.VMEM((2, 2, 4, 8, 512), F32),
            pltpu.VMEM((2, 4, 128, 256), BF),
            pltpu.VMEM((2, 128, 1024), BF),
            pltpu.VMEM((4, 128, 1024), BF),
            pltpu.VMEM((512, 256), BF),
            pltpu.VMEM((2, 1024, 256), BF),
            pltpu.VMEM((2, 384, 256), BF),
            pltpu.VMEM((2, 128, 256), BF),
            pltpu.VMEM((128, COL_DOWN), F32),
            pltpu.VMEM((512, 128), F32),
            pltpu.VMEM((2, 128, 128), F32),
            pltpu.VMEM((8, 128, 128), F32),
        ],
        compiler_params=pltpu.CompilerParams(vmem_limit_bytes=56 * 1024 * 1024),
        name="tower",
    )(*operands)


def pack_rows(attn_in, attn_out, feed_in, feed_out):
    layers, _, rows, _ = attn_in.shape
    down = feed_out.reshape(layers, 4, rows, 128)
    return jnp.concatenate(
        [attn_in[:, 0], attn_in[:, 1], attn_out[:, 0], attn_out[:, 1], feed_in] + [down[:, a] for a in range(4)], axis=2
    )


def unpack_rows(packed):
    layers, rows, _ = packed.shape
    attn_in = jnp.stack([packed[:, :, at : at + 384] for at in COL_IN], axis=1)
    attn_out = jnp.stack([packed[:, :, at : at + 128] for at in COL_OUT], axis=1)
    feed_in = packed[:, :, COL_FEED:COL_DOWN]
    feed_out = jnp.stack([packed[:, :, COL_DOWN + 128 * a : COL_DOWN + 128 * a + 128] for a in range(4)], axis=1)
    return attn_in, attn_out, feed_in, feed_out.reshape(layers, 4 * rows, 128)


def flip(array, axis, bit, size):
    return lax.ppermute(array, axis, [(i, i ^ (1 << bit)) for i in range(size)])


def gather_rows(attn_in, attn_out, feed_in, feed_out):
    vmem = pl.BlockSpec(memory_space=pltpu.VMEM)
    row = pl.pallas_call(
        pack_kernel, out_shape=jax.ShapeDtypeStruct((SHARDS, 8, COLS), BF), in_specs=[vmem] * 4, out_specs=vmem, name="pack",
    )(attn_in, attn_out, feed_in, feed_out)
    mine = lax.all_to_all(row, "fsdp", 0, 0, tiled=True)
    return mine, flip(mine, "dp", 0, 2)


def reduce_big(big):
    held = big[0].astype(F32) + flip(big[1], "dp", 0, 2).astype(F32)
    parts = lax.all_to_all(held.astype(BF), "fsdp", 0, 0, tiled=True)
    return jnp.sum(parts.astype(F32), axis=0)


def reduce_small(small):
    held = small[0] + flip(small[1].astype(BF), "dp", 0, 2).astype(F32)
    for bit in STEP_BITS[::-1]:
        mine = held.astype(BF)
        held = mine.astype(F32) + flip(mine, "fsdp", bit, SHARDS).astype(F32)
    return held


def both_cores(mine, dp):
    other = flip(mine, "dp", 0, 2)
    return jnp.where(dp == 0, mine, other), jnp.where(dp == 0, other, mine)


def per_device(shard_count, patches, prompts, cls_token, attn_in, attn_out, feed_in, feed_out, token_operator,
               norm_gains, branch_scales, var_counts, dataset_ids, cotangent, adjust_cotangent):
    dp = lax.axis_index("dp")
    fast = shard_count == SHARDS
    if fast:
        mine, other = gather_rows(attn_in, attn_out, feed_in, feed_out)
    else:
        whole_down = lax.all_gather(feed_out, "fsdp", axis=1, tiled=True)
        whole_down = whole_down.reshape(2, SHARDS, 4, 8, 128).transpose(0, 2, 1, 3, 4).reshape(2, 512, 128)
        rows = pack_rows(
            lax.all_gather(attn_in, "fsdp", axis=2, tiled=True),
            lax.all_gather(attn_out, "fsdp", axis=2, tiled=True),
            lax.all_gather(feed_in, "fsdp", axis=1, tiled=True),
            whole_down,
        )
        rows = rows.reshape(2, SHARDS, 8, COLS).transpose(1, 0, 2, 3)
        mine, other = rows[:, 0], rows[:, 1]
    output, patch_grad, big, small = run_tower(
        fast, dataset_ids, var_counts, mine, other, token_operator, norm_gains, branch_scales, patches, prompts,
        cls_token.reshape(1, -1), cotangent, adjust_cotangent,
    )
    if fast:
        layer_grads = both_cores(reduce_big(big), dp)
        grads = unpack_rows(jnp.stack(layer_grads))
        tokens, rest = both_cores(reduce_small(small), dp)
    else:
        rows = big.astype(F32).reshape(2, 128, COLS)
        attn_in_g, attn_out_g, feed_in_g, feed_out_g = unpack_rows(rows)
        feed_out_g = feed_out_g.reshape(2, 4, SHARDS, 8, 128).transpose(0, 2, 1, 3, 4).reshape(2, 512, 128)
        grads = (
            lax.psum_scatter(lax.psum(attn_in_g, "dp"), "fsdp", scatter_dimension=2, tiled=True),
            lax.psum_scatter(lax.psum(attn_out_g, "dp"), "fsdp", scatter_dimension=2, tiled=True),
            lax.psum_scatter(lax.psum(feed_in_g, "dp"), "fsdp", scatter_dimension=1, tiled=True),
            lax.psum_scatter(lax.psum(feed_out_g, "dp"), "fsdp", scatter_dimension=1, tiled=True),
        )
        tokens, rest = lax.psum(small, ("dp", "fsdp"))
    token_grad = tokens.reshape(2, 128, 128)
    gains_grad = rest[:8, 10].reshape(2, 4, 128)
    scales_grad = rest[:8, 11].reshape(2, 4, 128)
    return (
        output, patch_grad, rest[:8, :10], rest[0, 12], *grads, token_grad, gains_grad, scales_grad,
        rest[8:, :10], rest[8, 12],
    )


def solution(mesh):
    batch = P(("dp", "fsdp"), None, None, None)
    wide = P(None, None, "fsdp", None)
    tall = P(None, "fsdp", None)
    return jax.shard_map(
        functools.partial(per_device, mesh.shape["fsdp"]),
        mesh=mesh,
        in_specs=(batch, P(), P(), wide, wide, tall, tall, P(), P(), P(), P(), P(("dp", "fsdp")), batch, batch),
        out_specs=(batch, batch, P(), P(), wide, wide, tall, tall, P(), P(), P(), P(), P()),
        check_vma=False,
    )
```

```python
import functools

import jax
import jax.numpy as jnp
from jax import lax
from jax.experimental import pallas as pl
from jax.experimental.pallas import tpu as pltpu
from jax.sharding import PartitionSpec as P

HEADS = 8
EPSILON = 1e-05
NEG_FILL = -1000000000.0
BF = jnp.bfloat16
F32 = jnp.float32

COL_IN = (0, 384)
COL_OUT = (768, 896)
COL_FEED = 1024
COL_DOWN = 2048
COLS = 2560
SHARDS = 16
STEP_BITS = (2, 3, 0, 1)


def dot_nn(a, b):
    return lax.dot_general(a, b, (((1,), (0,)), ((), ())), preferred_element_type=F32)


def dot_nt(a, b):
    return lax.dot_general(a, b, (((1,), (1,)), ((), ())), preferred_element_type=F32)


def norm_cols(x):
    centered = x - jnp.mean(x, axis=0, keepdims=True)
    inv = lax.rsqrt(jnp.mean(centered * centered, axis=0, keepdims=True) + EPSILON)
    return centered * inv, inv


def norm_cols_back(dn, gain, xhat, inv):
    e = dn * gain
    m1 = jnp.mean(e, axis=0, keepdims=True)
    m2 = jnp.mean(e * xhat, axis=0, keepdims=True)
    return inv * (e - m1 - xhat * m2)


def fold(part):
    return part[:, :128] + part[:, 128:]


def dp_of(split):
    return lax.axis_index("dp") if split else 0


def pack_kernel(attn_in_ref, attn_out_ref, feed_in_ref, feed_out_ref, out_ref):
    l = lax.axis_index("dp")
    down = feed_out_ref[l].astype(F32)
    parts = [attn_in_ref[l, 0], attn_in_ref[l, 1], attn_out_ref[l, 0], attn_out_ref[l, 1], feed_in_ref[l]]
    parts = [part.astype(F32) for part in parts] + [down[8 * a : 8 * a + 8] for a in range(4)]
    row = jnp.concatenate(parts, axis=1).astype(BF)
    for f in range(SHARDS):
        out_ref[f] = row


def tower_kernel(
    split,
    ids_ref, counts_ref, wmine_ref, wother_ref, tok_ref, gains_ref, scales_ref, patches_ref, prompts_ref,
    cls_ref, cot_ref, adj_ref,
    out_ref, pgrad_ref, gbig_ref, gsmall_ref,
    w_ref, wd_ref, wt_ref, wdt_ref, colb_ref, tokscr_ref, h_ref, g_ref, xh_ref, inv_ref,
    qkvt_ref, pb_ref, ot_ref, qkvv_ref, pv_ref, ov_ref, pw_ref, hid_ref, du_ref, dqkv_ref,
    dov_ref, ga_ref, gd_ref, gt_ref, gacc_ref,
):
    dp = dp_of(split)
    layers = 2
    chunks = 4
    items = 2

    for l in range(layers):
        for pair in range(SHARDS // 2):
            lo = jnp.where(dp == l, wmine_ref[2 * pair].astype(F32), wother_ref[2 * pair].astype(F32))
            hi = jnp.where(dp == l, wmine_ref[2 * pair + 1].astype(F32), wother_ref[2 * pair + 1].astype(F32))
            w_ref[l, 16 * pair : 16 * pair + 16, :] = jnp.concatenate([lo[:, :COL_DOWN], hi[:, :COL_DOWN]], axis=0).astype(BF)
            for half, part in enumerate((lo, hi)):
                base = 64 * pair + 32 * half
                wd_ref[l, base : base + 32, :] = jnp.concatenate(
                    [part[:, COL_DOWN + 128 * a : COL_DOWN + 128 * a + 128] for a in range(4)], axis=0
                ).astype(BF)
        for block in range(COL_DOWN // 128):
            target = block if block < 8 else 8 + (0, 1, 4, 5, 2, 3, 6, 7)[block - 8]
            wt_ref[l, 128 * target : 128 * target + 128, :] = w_ref[l, :, 128 * block : 128 * block + 128].T
        for block in range(4):
            wdt_ref[l, :, 128 * block : 128 * block + 128] = wd_ref[l, 128 * block : 128 * block + 128, :].T
        for k in range(4):
            for offset, rows in ((0, gains_ref), (4, scales_ref)):
                col = jnp.broadcast_to(rows[l, k : k + 1, :], (128, 128)).T
                colb_ref[l * 8 + offset + k, :, 0:128] = col
                colb_ref[l * 8 + offset + k, :, 128:256] = col

    for b in range(items):
        ident = ids_ref[b]
        for v in range(4):
            bv = 4 * b + v
            tokscr_ref[bv, 0:10, :] = prompts_ref[ident].astype(F32)
            tokscr_ref[bv, 10:127, :] = patches_ref[b, v].astype(F32)
            tokscr_ref[bv, 127:128, :] = cls_ref[...].astype(F32)
            lanes = slice(128 * (v % 2), 128 * (v % 2) + 128)
            h_ref[2 * b + v // 2, :, lanes] = tokscr_ref[bv].T
            g_ref[0, 2 * b + v // 2, :, lanes] = cot_ref[b, v].astype(F32).T
            g_ref[1, 2 * b + v // 2, :, lanes] = adj_ref[b, v].astype(F32).T

    head_row = lax.broadcasted_iota(jnp.int32, (8, 128), 0)
    head_col = lax.broadcasted_iota(jnp.int32, (8, 128), 1) // 16
    gather_heads = jnp.where(head_row == head_col, 1.0, 0.0).astype(BF)
    spread_row = lax.broadcasted_iota(jnp.int32, (128, 8), 0) // 16
    spread_col = lax.broadcasted_iota(jnp.int32, (128, 8), 1)
    spread_heads = jnp.where(spread_row == spread_col, 1.0, 0.0).astype(BF)

    def head_sums(left, rights):
        return dot_nn(gather_heads, jnp.concatenate([left * right for right in rights], axis=1))

    blank = jnp.zeros((16, 128), BF)

    def diag_pair(rows):
        upper = jnp.concatenate([rows[:16], blank], axis=1)
        return jnp.concatenate([upper, jnp.concatenate([blank, rows[16:]], axis=1)], axis=0)

    def diag_full(pair, hp):
        parts = [pair if at == hp else jnp.zeros_like(pair) for at in range(4)]
        return jnp.concatenate(parts, axis=0)

    def gain(l, k):
        return colb_ref[l * 8 + k]

    def scale(l, k):
        return colb_ref[l * 8 + 4 + k]

    def keep_norm(l, k, c, x):
        xhat, inv = norm_cols(x)
        xh_ref[l * 4 + k, c] = xhat
        inv_ref[l * 4 + k, c] = inv
        return (xhat * gain(l, k)).astype(BF)

    def time_forward(l, c):
        x = h_ref[c]
        n = keep_norm(l, 0, c, x)
        qkv = dot_nn(wt_ref[l, 0:384, :], n)
        queries = (qkv[:128] * 0.25).astype(BF)
        keys = qkv[128:256].astype(BF)
        values = qkv[256:].astype(BF)
        qkvt_ref[l, c, 0:128, :] = queries
        qkvt_ref[l, c, 128:256, :] = keys
        qkvt_ref[l, c, 256:384, :] = values
        for s in range(2):
            lanes = slice(128 * s, 128 * s + 128)
            key_rows = keys[:, lanes].T
            for hp in range(4):
                span = slice(256 * hp, 256 * hp + 256)
                rows = slice(32 * hp, 32 * hp + 32)
                scores = dot_nn(key_rows, diag_full(diag_pair(queries[rows, lanes]), hp))
                shifted = jnp.exp(scores - jnp.max(scores, axis=0, keepdims=True))
                prob = (shifted * (1.0 / jnp.sum(shifted, axis=0, keepdims=True))).astype(BF)
                pb_ref[l, 2 * c + s, :, span] = prob
                mixed = dot_nn(values[rows, lanes], prob)
                ot_ref[l, c, 32 * hp : 32 * hp + 16, lanes] = mixed[:16, :128].astype(BF)
                ot_ref[l, c, 32 * hp + 16 : 32 * hp + 32, lanes] = mixed[16:, 128:].astype(BF)
        branch = dot_nn(wt_ref[l, COL_OUT[0] : COL_OUT[0] + 128, :], ot_ref[l, c])
        h_ref[c] = x + scale(l, 0) * branch

    def var_forward(l, b):
        for cc in range(2):
            c = 2 * b + cc
            n = keep_norm(l, 1, c, h_ref[c])
            qkv = dot_nn(wt_ref[l, COL_IN[1] : COL_IN[1] + 384, :], n)
            qkvv_ref[l, c, 0:128, :] = (qkv[:128] * 0.25).astype(BF)
            qkvv_ref[l, c, 128:384, :] = qkv[128:].astype(BF)
        count = counts_ref[ids_ref[b]]

        def slot(first, i):
            lanes = slice(128 * (i % 2), 128 * (i % 2) + 128)
            return qkvv_ref[l, 2 * b + i // 2, first : first + 128, lanes]

        key_slots = [slot(128, j) for j in range(4)]
        value_slots = [slot(256, j).astype(F32) for j in range(4)]
        for i in range(4):
            scores = head_sums(slot(0, i), key_slots)
            parts = [scores[:, 128 * j : 128 * j + 128] for j in range(4)]
            parts = [jnp.where(jnp.full((8, 128), count, jnp.int32) > j, parts[j], NEG_FILL) for j in range(4)]
            top = jnp.maximum(jnp.maximum(parts[0], parts[1]), jnp.maximum(parts[2], parts[3]))
            shifted = [jnp.exp(part - top) for part in parts]
            total = 1.0 / ((shifted[0] + shifted[1]) + (shifted[2] + shifted[3]))
            prob = jnp.concatenate([part * total for part in shifted], axis=1)
            pv_ref[l, b, i] = prob
            spread = dot_nn(spread_heads, prob.astype(BF))
            pw_ref[l, b, i] = spread.astype(BF)
            mixed = spread[:, :128] * value_slots[0]
            for j in range(1, 4):
                mixed = mixed + spread[:, 128 * j : 128 * j + 128] * value_slots[j]
            lanes = slice(128 * (i % 2), 128 * (i % 2) + 128)
            ov_ref[l, 2 * b + i // 2, :, lanes] = mixed.astype(BF)
        for cc in range(2):
            c = 2 * b + cc
            branch = dot_nn(wt_ref[l, COL_OUT[1] : COL_OUT[1] + 128, :], ov_ref[l, c])
            h_ref[c] = h_ref[c] + scale(l, 1) * branch

    def stacked(rows):
        return jnp.concatenate([rows[:, :128], rows[:, 128:]], axis=0)

    def unstacked(rows):
        return jnp.concatenate([rows[:128], rows[128:]], axis=1)

    def gate_and_up(l, z, n):
        joint = dot_nn(wt_ref[l, COL_FEED + 512 * z : COL_FEED + 512 * z + 512, :], n)
        gate, up = joint[:256], joint[256:]
        return gate, up, 0.5 * jnp.tanh(0.5 * gate) + 0.5

    def tail_forward(l, c):
        x = h_ref[c]
        n = keep_norm(l, 2, c, x)
        x = x + scale(l, 2) * unstacked(dot_nt(stacked(n), tok_ref[l]))
        n = keep_norm(l, 3, c, x)
        for z in range(2):
            gate, up, sig = gate_and_up(l, z, n)
            hid_ref[c % 2, 256 * z : 256 * z + 256, :] = (gate * sig * up).astype(BF)
        h_ref[c] = x + scale(l, 3) * dot_nn(wdt_ref[l], hid_ref[c % 2])

    def norm_of(l, k, c):
        xhat = xh_ref[l * 4 + k, c]
        return xhat, inv_ref[l * 4 + k, c], (xhat * gain(l, k)).astype(BF)

    def pass_on(l, k, c, x, dn, xhat, inv):
        if x == 0:
            gacc_ref[l * 4 + k] += fold(dn * xhat)
        g_ref[x, c] += norm_cols_back(dn, gain(l, k), xhat, inv)

    def feed_backward(l, c):
        xhat, inv, n = norm_of(l, 3, c)
        dz = [(scale(l, 3) * g_ref[x, c]).astype(BF) for x in range(2)]
        for z in range(2):
            rows = slice(256 * z, 256 * z + 256)
            gate, up, sig = gate_and_up(l, z, n)
            act = gate * sig
            hid_ref[c % 2, rows, :] = (act * up).astype(BF)
            slope = up * (sig * (1.0 + gate * (1.0 - sig)))
            for x in range(2):
                dhid = dot_nn(wd_ref[l, rows, :], dz[x])
                du_ref[2 * (c % 2) + x, 256 * z : 256 * z + 256, :] = (dhid * slope).astype(BF)
                du_ref[2 * (c % 2) + x, 512 + 256 * z : 768 + 256 * z, :] = (dhid * act).astype(BF)
        ga_ref[:, COL_FEED:COL_DOWN] += dot_nt(n, du_ref[2 * (c % 2)])
        gd_ref[...] += dot_nt(hid_ref[c % 2], dz[0])
        for x in range(2):
            dn = dot_nn(w_ref[l, :, COL_FEED:COL_DOWN], du_ref[2 * (c % 2) + x])
            pass_on(l, 3, c, x, dn, xhat, inv)

    def token_backward(l, c):
        xhat, inv, n = norm_of(l, 2, c)
        for x in range(2):
            dy = stacked((scale(l, 2) * g_ref[x, c]).astype(BF))
            if x == 0:
                turned = jnp.concatenate([dy[:128].T, dy[128:].T], axis=1)
                gt_ref[l] += dot_nn(turned, stacked(n))
            pass_on(l, 2, c, x, unstacked(dot_nn(dy, tok_ref[l])), xhat, inv)

    def var_backward(l, b):
        def slot(first, i):
            lanes = slice(128 * (i % 2), 128 * (i % 2) + 128)
            return qkvv_ref[l, 2 * b + i // 2, first : first + 128, lanes]

        for x in range(2):
            for cc in range(2):
                c = 2 * b + cc
                dt = (scale(l, 1) * g_ref[x, c]).astype(BF)
                dov_ref[4 * b + 2 * x + cc] = dot_nn(w_ref[l, :, COL_OUT[1] : COL_OUT[1] + 128], dt).astype(BF)
                if x == 0:
                    ga_ref[:, COL_OUT[1] : COL_OUT[1] + 128] += dot_nt(ov_ref[l, c], dt)
            value_slots = [slot(256, j) for j in range(4)]
            dkeys = [[] for _ in range(4)]
            dvalues = [[] for _ in range(4)]
            for i in range(4):
                lanes = slice(128 * (i % 2), 128 * (i % 2) + 128)
                grad = dov_ref[4 * b + 2 * x + i // 2, :, lanes]
                query = slot(0, i)
                prob = pv_ref[l, b, i]
                weighted = prob * head_sums(grad, value_slots)
                total = (weighted[:, :128] + weighted[:, 128:256]) + (weighted[:, 256:384] + weighted[:, 384:])
                ds = weighted - prob * jnp.concatenate([total] * 4, axis=1)
                ds_wide = dot_nn(spread_heads, ds.astype(BF)).astype(BF)
                ds_slots = [ds_wide[:, 128 * j : 128 * j + 128] for j in range(4)]
                terms = [ds_slots[j] * slot(128, j) for j in range(4)]
                dquery = (terms[0] + terms[1]) + (terms[2] + terms[3])
                for j in range(4):
                    dkeys[j].append(ds_slots[j] * query)
                    dvalues[j].append(pw_ref[l, b, i, :, 128 * j : 128 * j + 128] * grad)
                dqkv_ref[4 * b + 2 * x + i // 2, 0:128, lanes] = dquery * jnp.asarray(0.25, BF)
            for j in range(4):
                lanes = slice(128 * (j % 2), 128 * (j % 2) + 128)
                dqkv_ref[4 * b + 2 * x + j // 2, 128:256, lanes] = (dkeys[j][0] + dkeys[j][1]) + (dkeys[j][2] + dkeys[j][3])
                dqkv_ref[4 * b + 2 * x + j // 2, 256:384, lanes] = (dvalues[j][0] + dvalues[j][1]) + (dvalues[j][2] + dvalues[j][3])
            for cc in range(2):
                c = 2 * b + cc
                xhat, inv, n = norm_of(l, 1, c)
                dqkv = dqkv_ref[4 * b + 2 * x + cc]
                if x == 0:
                    ga_ref[:, COL_IN[1] : COL_IN[1] + 384] += dot_nt(n, dqkv)
                pass_on(l, 1, c, x, dot_nn(w_ref[l, :, COL_IN[1] : COL_IN[1] + 384], dqkv), xhat, inv)

    def time_backward(l, c):
        xhat, inv, n = norm_of(l, 0, c)
        queries = qkvt_ref[l, c, 0:128, :]
        keys = qkvt_ref[l, c, 128:256, :]
        values = qkvt_ref[l, c, 256:384, :]
        grads = []
        for x in range(2):
            dt = (scale(l, 0) * g_ref[x, c]).astype(BF)
            grads.append(dot_nn(w_ref[l, :, COL_OUT[0] : COL_OUT[0] + 128], dt).astype(BF))
            if x == 0:
                ga_ref[:, COL_OUT[0] : COL_OUT[0] + 128] += dot_nt(ot_ref[l, c], dt)
        for s in range(2):
            lanes = slice(128 * s, 128 * s + 128)
            value_rows = values[:, lanes].T
            for hp in range(4):
                span = slice(256 * hp, 256 * hp + 256)
                rows = slice(32 * hp, 32 * hp + 32)
                prob_bf = pb_ref[l, 2 * c + s, :, span]
                prob = prob_bf.astype(F32)
                query_pair = diag_pair(queries[rows, lanes])
                for x in range(2):
                    grad_pair = diag_pair(grads[x][rows, lanes])
                    weighted = prob * dot_nn(value_rows, diag_full(grad_pair, hp))
                    ds = (weighted - prob * jnp.sum(weighted, axis=0, keepdims=True)).astype(BF)
                    dvalue = dot_nt(grad_pair, prob_bf)
                    dquery = dot_nn(keys[rows, lanes], ds) * 0.25
                    dkey = dot_nt(query_pair, ds)
                    dqkv_ref[2 * c + x, 32 * hp : 32 * hp + 16, lanes] = dquery[:16, :128].astype(BF)
                    dqkv_ref[2 * c + x, 32 * hp + 16 : 32 * hp + 32, lanes] = dquery[16:, 128:].astype(BF)
                    dqkv_ref[2 * c + x, 128 + 32 * hp : 160 + 32 * hp, lanes] = dkey.astype(BF)
                    dqkv_ref[2 * c + x, 256 + 32 * hp : 288 + 32 * hp, lanes] = dvalue.astype(BF)
        ga_ref[:, COL_IN[0] : COL_IN[0] + 384] += dot_nt(n, dqkv_ref[2 * c])
        for x in range(2):
            pass_on(l, 0, c, x, dot_nn(w_ref[l, :, COL_IN[0] : COL_IN[0] + 384], dqkv_ref[2 * c + x]), xhat, inv)

    def each(count, stage, l):
        for i in range(count):
            stage(l, i)

    def forward_layer(l, carry):
        each(chunks, time_forward, l)
        each(items, var_forward, l)
        each(chunks, tail_forward, l)
        return carry

    lax.fori_loop(0, layers, forward_layer, 0)
    for b in range(items):
        for v in range(4):
            lanes = slice(128 * (v % 2), 128 * (v % 2) + 128)
            out_ref[b, v] = h_ref[2 * b + v // 2, :, lanes].T.astype(BF)

    gacc_ref[...] = jnp.zeros_like(gacc_ref)
    gt_ref[...] = jnp.zeros_like(gt_ref)
    gsmall_ref[...] = jnp.zeros_like(gsmall_ref)
    rest = 1 ^ dp
    def backward_layer(step, carry):
        l = layers - 1 - step
        ga_ref[...] = jnp.zeros_like(ga_ref)
        gd_ref[...] = jnp.zeros_like(gd_ref)
        each(chunks, feed_backward, l)
        each(chunks, token_backward, l)
        each(items, var_backward, l)
        each(chunks, time_backward, l)
        l_at = l ^ dp
        for f in range(SHARDS):
            down = jnp.concatenate([gd_ref[32 * f + 8 * a : 32 * f + 8 * a + 8, :] for a in range(4)], axis=1)
            block = jnp.concatenate([ga_ref[8 * f : 8 * f + 8, :], down], axis=1)
            gbig_ref[l_at, f] = block.astype(BF)
        gains_rows = [jnp.sum(gacc_ref[l * 4 + k].T, axis=0, keepdims=True) for k in range(4)]
        sums = [
            jnp.sum(w_ref[l, :, COL_OUT[k] : COL_OUT[k] + 128].astype(F32) * ga_ref[:, COL_OUT[k] : COL_OUT[k] + 128], axis=0, keepdims=True)
            for k in range(2)
        ]
        sums.append(gains_ref[l, 2:3, :] * gains_rows[2])
        sums.append(jnp.sum(wd_ref[l].astype(F32) * gd_ref[...], axis=0, keepdims=True))
        for k in range(4):
            gsmall_ref[rest, l * 4 + k, 10:11, :] = gains_rows[k]
            gsmall_ref[rest, l * 4 + k, 11:12, :] = sums[k] / scales_ref[l, k : k + 1, :]
        for block in range(8):
            gsmall_ref[dp, 8 * l + block] = gt_ref[l, 16 * block : 16 * block + 16, :]
        return carry

    lax.fori_loop(0, layers, backward_layer, 0)

    for x in range(2):
        cls_sum = None
        for b in range(items):
            prompt_sum = None
            for v in range(4):
                lanes = slice(128 * (v % 2), 128 * (v % 2) + 128)
                tokscr_ref[4 * b + v] = g_ref[x, 2 * b + v // 2, :, lanes].T
                head = tokscr_ref[4 * b + v, 0:10, :]
                last = tokscr_ref[4 * b + v, 127:128, :]
                prompt_sum = head if prompt_sum is None else prompt_sum + head
                cls_sum = last if cls_sum is None else cls_sum + last
                if x == 0:
                    pgrad_ref[b, v] = tokscr_ref[4 * b + v, 10:127, :]
            gsmall_ref[rest, 8 * x + ids_ref[b], 0:10, :] += prompt_sum
        gsmall_ref[rest, 8 * x, 12:13, :] = cls_sum


def run_tower(split, *operands):
    vmem = pl.BlockSpec(memory_space=pltpu.VMEM)
    smem = pl.BlockSpec(memory_space=pltpu.SMEM)
    return pl.pallas_call(
        functools.partial(tower_kernel, split),
        out_shape=(
            jax.ShapeDtypeStruct((2, 4, 128, 128), BF),
            jax.ShapeDtypeStruct((2, 4, 117, 128), F32),
            jax.ShapeDtypeStruct((2, SHARDS, 8, COLS), BF),
            jax.ShapeDtypeStruct((2, 16, 16, 128), F32),
        ),
        in_specs=[smem, smem] + [vmem] * 10,
        out_specs=[vmem] * 4,
        scratch_shapes=[
            pltpu.VMEM((2, 128, COL_DOWN), BF),
            pltpu.VMEM((2, 512, 128), BF),
            pltpu.VMEM((2, COL_DOWN, 128), BF),
            pltpu.VMEM((2, 128, 512), BF),
            pltpu.VMEM((16, 128, 256), F32),
            pltpu.VMEM((8, 128, 128), F32),
            pltpu.VMEM((4, 128, 256), F32),
            pltpu.VMEM((2, 4, 128, 256), F32),
            pltpu.VMEM((8, 4, 128, 256), F32),
            pltpu.VMEM((8, 4, 1, 256), F32),
            pltpu.VMEM((2, 4, 384, 256), BF),
            pltpu.VMEM((2, 8, 128, 1024), BF),
            pltpu.VMEM((2, 4, 128, 256), BF),
            pltpu.VMEM((2, 4, 384, 256), BF),
            pltpu.VMEM((2, 2, 4, 8, 512), F32),
            pltpu.VMEM((2, 4, 128, 256), BF),
            pltpu.VMEM((2, 2, 4, 128, 512), BF),
            pltpu.VMEM((2, 512, 256), BF),
            pltpu.VMEM((4, 1024, 256), BF),
            pltpu.VMEM((8, 384, 256), BF),
            pltpu.VMEM((8, 128, 256), BF),
            pltpu.VMEM((128, COL_DOWN), F32),
            pltpu.VMEM((512, 128), F32),
            pltpu.VMEM((2, 128, 128), F32),
            pltpu.VMEM((8, 128, 128), F32),
        ],
        compiler_params=pltpu.CompilerParams(vmem_limit_bytes=56 * 1024 * 1024),
        name="tower",
    )(*operands)


def pack_rows(attn_in, attn_out, feed_in, feed_out):
    layers, _, rows, _ = attn_in.shape
    down = feed_out.reshape(layers, 4, rows, 128)
    return jnp.concatenate(
        [attn_in[:, 0], attn_in[:, 1], attn_out[:, 0], attn_out[:, 1], feed_in] + [down[:, a] for a in range(4)], axis=2
    )


def unpack_rows(packed):
    layers, rows, _ = packed.shape
    attn_in = jnp.stack([packed[:, :, at : at + 384] for at in COL_IN], axis=1)
    attn_out = jnp.stack([packed[:, :, at : at + 128] for at in COL_OUT], axis=1)
    feed_in = packed[:, :, COL_FEED:COL_DOWN]
    feed_out = jnp.stack([packed[:, :, COL_DOWN + 128 * a : COL_DOWN + 128 * a + 128] for a in range(4)], axis=1)
    return attn_in, attn_out, feed_in, feed_out.reshape(layers, 4 * rows, 128)


def flip(array, axis, bit, size):
    return lax.ppermute(array, axis, [(i, i ^ (1 << bit)) for i in range(size)])


def gather_rows(attn_in, attn_out, feed_in, feed_out):
    vmem = pl.BlockSpec(memory_space=pltpu.VMEM)
    row = pl.pallas_call(
        pack_kernel, out_shape=jax.ShapeDtypeStruct((SHARDS, 8, COLS), BF), in_specs=[vmem] * 4, out_specs=vmem, name="pack",
    )(attn_in, attn_out, feed_in, feed_out)
    mine = lax.all_to_all(row, "fsdp", 0, 0, tiled=True)
    return mine, flip(mine, "dp", 0, 2)


def reduce_big(big):
    held = big[0].astype(F32) + flip(big[1], "dp", 0, 2).astype(F32)
    parts = lax.all_to_all(held.astype(BF), "fsdp", 0, 0, tiled=True)
    return jnp.sum(parts.astype(F32), axis=0)


def reduce_small(small):
    held = small[0] + flip(small[1].astype(BF), "dp", 0, 2).astype(F32)
    for bit in STEP_BITS[::-1]:
        mine = held.astype(BF)
        held = mine.astype(F32) + flip(mine, "fsdp", bit, SHARDS).astype(F32)
    return held


def both_cores(mine, dp):
    other = flip(mine, "dp", 0, 2)
    return jnp.where(dp == 0, mine, other), jnp.where(dp == 0, other, mine)


def per_device(shard_count, patches, prompts, cls_token, attn_in, attn_out, feed_in, feed_out, token_operator,
               norm_gains, branch_scales, var_counts, dataset_ids, cotangent, adjust_cotangent):
    dp = lax.axis_index("dp")
    fast = shard_count == SHARDS
    if fast:
        mine, other = gather_rows(attn_in, attn_out, feed_in, feed_out)
    else:
        whole_down = lax.all_gather(feed_out, "fsdp", axis=1, tiled=True)
        whole_down = whole_down.reshape(2, SHARDS, 4, 8, 128).transpose(0, 2, 1, 3, 4).reshape(2, 512, 128)
        rows = pack_rows(
            lax.all_gather(attn_in, "fsdp", axis=2, tiled=True),
            lax.all_gather(attn_out, "fsdp", axis=2, tiled=True),
            lax.all_gather(feed_in, "fsdp", axis=1, tiled=True),
            whole_down,
        )
        rows = rows.reshape(2, SHARDS, 8, COLS).transpose(1, 0, 2, 3)
        mine, other = rows[:, 0], rows[:, 1]
    output, patch_grad, big, small = run_tower(
        fast, dataset_ids, var_counts, mine, other, token_operator, norm_gains, branch_scales, patches, prompts,
        cls_token.reshape(1, -1), cotangent, adjust_cotangent,
    )
    if fast:
        layer_grads = both_cores(reduce_big(big), dp)
        grads = unpack_rows(jnp.stack(layer_grads))
        tokens, rest = both_cores(reduce_small(small), dp)
    else:
        rows = big.astype(F32).reshape(2, 128, COLS)
        attn_in_g, attn_out_g, feed_in_g, feed_out_g = unpack_rows(rows)
        feed_out_g = feed_out_g.reshape(2, 4, SHARDS, 8, 128).transpose(0, 2, 1, 3, 4).reshape(2, 512, 128)
        grads = (
            lax.psum_scatter(lax.psum(attn_in_g, "dp"), "fsdp", scatter_dimension=2, tiled=True),
            lax.psum_scatter(lax.psum(attn_out_g, "dp"), "fsdp", scatter_dimension=2, tiled=True),
            lax.psum_scatter(lax.psum(feed_in_g, "dp"), "fsdp", scatter_dimension=1, tiled=True),
            lax.psum_scatter(lax.psum(feed_out_g, "dp"), "fsdp", scatter_dimension=1, tiled=True),
        )
        tokens, rest = lax.psum(small, ("dp", "fsdp"))
    token_grad = tokens.reshape(2, 128, 128)
    gains_grad = rest[:8, 10].reshape(2, 4, 128)
    scales_grad = rest[:8, 11].reshape(2, 4, 128)
    return (
        output, patch_grad, rest[:8, :10], rest[0, 12], *grads, token_grad, gains_grad, scales_grad,
        rest[8:, :10], rest[8, 12],
    )


def solution(mesh):
    batch = P(("dp", "fsdp"), None, None, None)
    wide = P(None, None, "fsdp", None)
    tall = P(None, "fsdp", None)
    return jax.shard_map(
        functools.partial(per_device, mesh.shape["fsdp"]),
        mesh=mesh,
        in_specs=(batch, P(), P(), wide, wide, tall, tall, P(), P(), P(), P(), P(("dp", "fsdp")), batch, batch),
        out_specs=(batch, batch, P(), P(), wide, wide, tall, tall, P(), P(), P(), P(), P()),
        check_vma=False,
    )
```

```python
import functools

import jax
import jax.numpy as jnp
from jax import lax
from jax.experimental import pallas as pl
from jax.experimental.pallas import tpu as pltpu
from jax.sharding import PartitionSpec as P

HEADS = 8
EPSILON = 1e-05
NEG_FILL = -1000000000.0
BF = jnp.bfloat16
F32 = jnp.float32

COL_IN = (0, 384)
COL_OUT = (768, 896)
COL_FEED = 1024
COL_DOWN = 2048
COLS = 2560
SHARDS = 16
STEP_BITS = (2, 3, 0, 1)


def dot_nn(a, b):
    return lax.dot_general(a, b, (((1,), (0,)), ((), ())), preferred_element_type=F32)


def dot_nt(a, b):
    return lax.dot_general(a, b, (((1,), (1,)), ((), ())), preferred_element_type=F32)


def norm_cols(x):
    centered = x - jnp.mean(x, axis=0, keepdims=True)
    inv = lax.rsqrt(jnp.mean(centered * centered, axis=0, keepdims=True) + EPSILON)
    return centered * inv, inv


def norm_cols_back(dn, gain, xhat, inv):
    e = dn * gain
    m1 = jnp.mean(e, axis=0, keepdims=True)
    m2 = jnp.mean(e * xhat, axis=0, keepdims=True)
    return inv * (e - m1 - xhat * m2)


def fold(part):
    return part[:, :128] + part[:, 128:]


def pack_kernel(attn_in_ref, attn_out_ref, feed_in_ref, feed_out_ref, out_ref):
    l = lax.axis_index("dp")
    down = feed_out_ref[l].astype(F32)
    parts = [attn_in_ref[l, 0], attn_in_ref[l, 1], attn_out_ref[l, 0], attn_out_ref[l, 1], feed_in_ref[l]]
    parts = [part.astype(F32) for part in parts] + [down[8 * a : 8 * a + 8] for a in range(4)]
    out_ref[0] = jnp.concatenate(parts, axis=1).astype(BF)


def tower_kernel(
    split,
    ids_ref, counts_ref, wmine0_ref, wmine1_ref, wmine2_ref, wmine3_ref, wother0_ref, wother1_ref, wother2_ref, wother3_ref,
    tok_ref, gains_ref, scales_ref, patches_ref, prompts_ref,
    cls_ref, cot_ref, adj_ref,
    out_ref, pgrad_ref, gbig_ref, gsmall_ref,
    stage_ref, w_ref, wd_ref, wt_ref, wdt_ref, colb_ref, tokscr_ref, h_ref, g_ref, xh_ref, inv_ref,
    qkvt_ref, pb_ref, ot_ref, qkvv_ref, pv_ref, ov_ref, pw_ref, hid_ref, du_ref, dqkv_ref,
    dov_ref, ga_ref, gd_ref, gt_ref, gacc_ref,
):
    dp = lax.axis_index("dp") if split else 0
    me = lax.axis_index("fsdp") if split else 0
    layers = 2
    chunks = 4
    items = 2

    for rel in range(SHARDS):
        rows = pl.ds(pl.multiple_of(8 * (me ^ rel), 8), 8)
        mine_ref = (wmine0_ref, wmine1_ref, wmine2_ref, wmine3_ref)[rel % 4]
        other_ref = (wother0_ref, wother1_ref, wother2_ref, wother3_ref)[rel % 4]
        stage_ref[dp, rows, :] = mine_ref[rel // 4].astype(F32)
        stage_ref[1 - dp, rows, :] = other_ref[rel // 4].astype(F32)
    for l in range(layers):
        for pair in range(SHARDS // 2):
            lo = stage_ref[l, 16 * pair : 16 * pair + 8, :]
            hi = stage_ref[l, 16 * pair + 8 : 16 * pair + 16, :]
            w_ref[l, 16 * pair : 16 * pair + 16, :] = jnp.concatenate([lo[:, :COL_DOWN], hi[:, :COL_DOWN]], axis=0).astype(BF)
            for half, part in enumerate((lo, hi)):
                base = 64 * pair + 32 * half
                wd_ref[l, base : base + 32, :] = jnp.concatenate(
                    [part[:, COL_DOWN + 128 * a : COL_DOWN + 128 * a + 128] for a in range(4)], axis=0
                ).astype(BF)
        for block in range(COL_DOWN // 128):
            wt_ref[l, 128 * block : 128 * block + 128, :] = w_ref[l, :, 128 * block : 128 * block + 128].T
        for block in range(4):
            wdt_ref[l, :, 128 * block : 128 * block + 128] = wd_ref[l, 128 * block : 128 * block + 128, :].T
        for k in range(4):
            for offset, rows in ((0, gains_ref), (4, scales_ref)):
                col = jnp.broadcast_to(rows[l, k : k + 1, :], (128, 128)).T
                colb_ref[l * 8 + offset + k, :, 0:128] = col
                colb_ref[l * 8 + offset + k, :, 128:256] = col

    for b in range(items):
        ident = ids_ref[b]
        for v in range(4):
            bv = 4 * b + v
            tokscr_ref[bv, 0:10, :] = prompts_ref[ident].astype(F32)
            tokscr_ref[bv, 10:127, :] = patches_ref[b, v].astype(F32)
            tokscr_ref[bv, 127:128, :] = cls_ref[...].astype(F32)
            lanes = slice(128 * (v % 2), 128 * (v % 2) + 128)
            h_ref[2 * b + v // 2, :, lanes] = tokscr_ref[bv].T
            g_ref[0, 2 * b + v // 2, :, lanes] = cot_ref[b, v].astype(F32).T
            g_ref[1, 2 * b + v // 2, :, lanes] = adj_ref[b, v].astype(F32).T

    head_row = lax.broadcasted_iota(jnp.int32, (8, 128), 0)
    head_col = lax.broadcasted_iota(jnp.int32, (8, 128), 1) // 16
    gather_heads = jnp.where(head_row == head_col, 1.0, 0.0).astype(BF)
    spread_row = lax.broadcasted_iota(jnp.int32, (128, 8), 0) // 16
    spread_col = lax.broadcasted_iota(jnp.int32, (128, 8), 1)
    spread_heads = jnp.where(spread_row == spread_col, 1.0, 0.0).astype(BF)

    def head_sums(left, rights):
        return dot_nn(gather_heads, jnp.concatenate([(left * right).astype(BF) for right in rights], axis=1))

    blank = jnp.zeros((16, 128), BF)

    def diag_pair(rows):
        upper = jnp.concatenate([rows[:16], blank], axis=1)
        return jnp.concatenate([upper, jnp.concatenate([blank, rows[16:]], axis=1)], axis=0)

    def diag_full(pair, hp):
        parts = [pair if at == hp else jnp.zeros_like(pair) for at in range(4)]
        return jnp.concatenate(parts, axis=0)

    def gain(l, k):
        return colb_ref[l * 8 + k]

    def scale(l, k):
        return colb_ref[l * 8 + 4 + k]

    def keep_norm(l, k, c, x):
        xhat, inv = norm_cols(x)
        xh_ref[l * 4 + k, c] = xhat
        inv_ref[l * 4 + k, c] = inv
        return (xhat * gain(l, k)).astype(BF)

    def time_forward(l, c):
        x = h_ref[c]
        n = keep_norm(l, 0, c, x)
        qkv = dot_nn(wt_ref[l, 0:384, :], n)
        queries = (qkv[:128] * 0.25).astype(BF)
        keys = qkv[128:256].astype(BF)
        values = qkv[256:].astype(BF)
        qkvt_ref[l, c, 0:128, :] = queries
        qkvt_ref[l, c, 128:256, :] = keys
        qkvt_ref[l, c, 256:384, :] = values
        for s in range(2):
            lanes = slice(128 * s, 128 * s + 128)
            key_rows = keys[:, lanes].T
            for hp in range(4):
                span = slice(256 * hp, 256 * hp + 256)
                rows = slice(32 * hp, 32 * hp + 32)
                scores = dot_nn(key_rows, diag_full(diag_pair(queries[rows, lanes]), hp))
                shifted = jnp.exp(scores - jnp.max(scores, axis=0, keepdims=True))
                prob = (shifted * (1.0 / jnp.sum(shifted, axis=0, keepdims=True))).astype(BF)
                pb_ref[l, 2 * c + s, :, span] = prob
                mixed = dot_nn(values[rows, lanes], prob)
                ot_ref[l, c, 32 * hp : 32 * hp + 16, lanes] = mixed[:16, :128].astype(BF)
                ot_ref[l, c, 32 * hp + 16 : 32 * hp + 32, lanes] = mixed[16:, 128:].astype(BF)
        branch = dot_nn(wt_ref[l, COL_OUT[0] : COL_OUT[0] + 128, :], ot_ref[l, c])
        h_ref[c] = x + scale(l, 0) * branch

    def var_forward(l, b):
        for cc in range(2):
            c = 2 * b + cc
            n = keep_norm(l, 1, c, h_ref[c])
            qkv = dot_nn(wt_ref[l, COL_IN[1] : COL_IN[1] + 384, :], n)
            qkvv_ref[l, c, 0:128, :] = (qkv[:128] * 0.25).astype(BF)
            qkvv_ref[l, c, 128:384, :] = qkv[128:].astype(BF)
        count = counts_ref[ids_ref[b]]

        def slot(first, i):
            lanes = slice(128 * (i % 2), 128 * (i % 2) + 128)
            return qkvv_ref[l, 2 * b + i // 2, first : first + 128, lanes].astype(F32)

        key_slots = [slot(128, j) for j in range(4)]
        value_slots = [slot(256, j) for j in range(4)]
        for i in range(4):
            scores = head_sums(slot(0, i), key_slots)
            parts = [scores[:, 128 * j : 128 * j + 128] for j in range(4)]
            parts = [jnp.where(jnp.full((8, 128), count, jnp.int32) > j, parts[j], NEG_FILL) for j in range(4)]
            top = jnp.maximum(jnp.maximum(parts[0], parts[1]), jnp.maximum(parts[2], parts[3]))
            shifted = [jnp.exp(part - top) for part in parts]
            total = 1.0 / ((shifted[0] + shifted[1]) + (shifted[2] + shifted[3]))
            prob = jnp.concatenate([part * total for part in shifted], axis=1)
            pv_ref[l, b, i] = prob
            spread = dot_nn(spread_heads, prob.astype(BF))
            pw_ref[l, b, i] = spread.astype(BF)
            mixed = spread[:, :128] * value_slots[0]
            for j in range(1, 4):
                mixed = mixed + spread[:, 128 * j : 128 * j + 128] * value_slots[j]
            lanes = slice(128 * (i % 2), 128 * (i % 2) + 128)
            ov_ref[l, 2 * b + i // 2, :, lanes] = mixed.astype(BF)
        for cc in range(2):
            c = 2 * b + cc
            branch = dot_nn(wt_ref[l, COL_OUT[1] : COL_OUT[1] + 128, :], ov_ref[l, c])
            h_ref[c] = h_ref[c] + scale(l, 1) * branch

    def tail_forward(l, c):
        x = h_ref[c]
        n = keep_norm(l, 2, c, x)
        mix = [dot_nt(n[:, 128 * s : 128 * s + 128], tok_ref[l]) for s in range(2)]
        x = x + scale(l, 2) * jnp.concatenate(mix, axis=1)
        n = keep_norm(l, 3, c, x)
        for z in range(4):
            gate = dot_nn(wt_ref[l, COL_FEED + 128 * z : COL_FEED + 128 * z + 128, :], n)
            up = dot_nn(wt_ref[l, COL_FEED + 512 + 128 * z : COL_FEED + 640 + 128 * z, :], n)
            sig = 0.5 * jnp.tanh(0.5 * gate) + 0.5
            hid_ref[c % 2, 128 * z : 128 * z + 128, :] = (gate * sig * up).astype(BF)
        h_ref[c] = x + scale(l, 3) * dot_nn(wdt_ref[l], hid_ref[c % 2])

    def norm_of(l, k, c):
        xhat = xh_ref[l * 4 + k, c]
        return xhat, inv_ref[l * 4 + k, c], (xhat * gain(l, k)).astype(BF)

    def pass_on(l, k, c, x, dn, xhat, inv):
        if x == 0:
            gacc_ref[l * 4 + k] += fold(dn * xhat)
        g_ref[x, c] += norm_cols_back(dn, gain(l, k), xhat, inv)

    def feed_backward(l, c):
        xhat, inv, n = norm_of(l, 3, c)
        dz = [(scale(l, 3) * g_ref[x, c]).astype(BF) for x in range(2)]
        for z in range(4):
            rows = slice(128 * z, 128 * z + 128)
            gate = dot_nn(wt_ref[l, COL_FEED + 128 * z : COL_FEED + 128 * z + 128, :], n)
            up = dot_nn(wt_ref[l, COL_FEED + 512 + 128 * z : COL_FEED + 640 + 128 * z, :], n)
            sig = 0.5 * jnp.tanh(0.5 * gate) + 0.5
            act = gate * sig
            hid_ref[c % 2, rows, :] = (act * up).astype(BF)
            slope = up * (sig * (1.0 + gate * (1.0 - sig)))
            for x in range(2):
                dhid = dot_nn(wd_ref[l, rows, :], dz[x])
                du_ref[2 * (c % 2) + x, 128 * z : 128 * z + 128, :] = (dhid * slope).astype(BF)
                du_ref[2 * (c % 2) + x, 512 + 128 * z : 640 + 128 * z, :] = (dhid * act).astype(BF)
        ga_ref[:, COL_FEED:COL_DOWN] += dot_nt(n, du_ref[2 * (c % 2)])
        gd_ref[...] += dot_nt(hid_ref[c % 2], dz[0])
        for x in range(2):
            dn = dot_nn(w_ref[l, :, COL_FEED:COL_DOWN], du_ref[2 * (c % 2) + x])
            pass_on(l, 3, c, x, dn, xhat, inv)

    def token_backward(l, c):
        xhat, inv, n = norm_of(l, 2, c)
        for x in range(2):
            dy = (scale(l, 2) * g_ref[x, c]).astype(BF)
            dn = []
            for s in range(2):
                part = dy[:, 128 * s : 128 * s + 128]
                dn.append(dot_nn(part, tok_ref[l]))
                if x == 0:
                    gt_ref[l] += dot_nn(part.T, n[:, 128 * s : 128 * s + 128])
            pass_on(l, 2, c, x, jnp.concatenate(dn, axis=1), xhat, inv)

    def var_backward(l, b):
        def slot(first, i):
            lanes = slice(128 * (i % 2), 128 * (i % 2) + 128)
            return qkvv_ref[l, 2 * b + i // 2, first : first + 128, lanes].astype(F32)

        for x in range(2):
            for cc in range(2):
                c = 2 * b + cc
                dt = (scale(l, 1) * g_ref[x, c]).astype(BF)
                dov_ref[4 * b + 2 * x + cc] = dot_nn(w_ref[l, :, COL_OUT[1] : COL_OUT[1] + 128], dt).astype(BF)
                if x == 0:
                    ga_ref[:, COL_OUT[1] : COL_OUT[1] + 128] += dot_nt(ov_ref[l, c], dt)
            value_slots = [slot(256, j) for j in range(4)]
            dkeys = [0.0] * 4
            dvalues = [0.0] * 4
            for i in range(4):
                lanes = slice(128 * (i % 2), 128 * (i % 2) + 128)
                grad = dov_ref[4 * b + 2 * x + i // 2, :, lanes].astype(F32)
                query = slot(0, i)
                prob = pv_ref[l, b, i]
                weighted = prob * head_sums(grad, value_slots)
                total = (weighted[:, :128] + weighted[:, 128:256]) + (weighted[:, 256:384] + weighted[:, 384:])
                ds = weighted - prob * jnp.concatenate([total] * 4, axis=1)
                ds_wide = dot_nn(spread_heads, ds.astype(BF))
                ds_slots = [ds_wide[:, 128 * j : 128 * j + 128] for j in range(4)]
                terms = [ds_slots[j] * slot(128, j) for j in range(4)]
                dquery = (terms[0] + terms[1]) + (terms[2] + terms[3])
                for j in range(4):
                    dkeys[j] = dkeys[j] + ds_slots[j] * query
                    dvalues[j] = dvalues[j] + pw_ref[l, b, i, :, 128 * j : 128 * j + 128].astype(F32) * grad
                dqkv_ref[4 * b + 2 * x + i // 2, 0:128, lanes] = (dquery * 0.25).astype(BF)
            for j in range(4):
                lanes = slice(128 * (j % 2), 128 * (j % 2) + 128)
                dqkv_ref[4 * b + 2 * x + j // 2, 128:256, lanes] = dkeys[j].astype(BF)
                dqkv_ref[4 * b + 2 * x + j // 2, 256:384, lanes] = dvalues[j].astype(BF)
            for cc in range(2):
                c = 2 * b + cc
                xhat, inv, n = norm_of(l, 1, c)
                dqkv = dqkv_ref[4 * b + 2 * x + cc]
                if x == 0:
                    ga_ref[:, COL_IN[1] : COL_IN[1] + 384] += dot_nt(n, dqkv)
                pass_on(l, 1, c, x, dot_nn(w_ref[l, :, COL_IN[1] : COL_IN[1] + 384], dqkv), xhat, inv)

    def time_backward(l, c):
        xhat, inv, n = norm_of(l, 0, c)
        queries = qkvt_ref[l, c, 0:128, :]
        keys = qkvt_ref[l, c, 128:256, :]
        values = qkvt_ref[l, c, 256:384, :]
        grads = []
        for x in range(2):
            dt = (scale(l, 0) * g_ref[x, c]).astype(BF)
            grads.append(dot_nn(w_ref[l, :, COL_OUT[0] : COL_OUT[0] + 128], dt).astype(BF))
            if x == 0:
                ga_ref[:, COL_OUT[0] : COL_OUT[0] + 128] += dot_nt(ot_ref[l, c], dt)
        for s in range(2):
            lanes = slice(128 * s, 128 * s + 128)
            value_rows = values[:, lanes].T
            for hp in range(4):
                span = slice(256 * hp, 256 * hp + 256)
                rows = slice(32 * hp, 32 * hp + 32)
                prob_bf = pb_ref[l, 2 * c + s, :, span]
                prob = prob_bf.astype(F32)
                query_pair = diag_pair(queries[rows, lanes])
                for x in range(2):
                    grad_pair = diag_pair(grads[x][rows, lanes])
                    weighted = prob * dot_nn(value_rows, diag_full(grad_pair, hp))
                    ds = (weighted - prob * jnp.sum(weighted, axis=0, keepdims=True)).astype(BF)
                    dvalue = dot_nt(grad_pair, prob_bf)
                    dquery = dot_nn(keys[rows, lanes], ds) * 0.25
                    dkey = dot_nt(query_pair, ds)
                    dqkv_ref[2 * c + x, 32 * hp : 32 * hp + 16, lanes] = dquery[:16, :128].astype(BF)
                    dqkv_ref[2 * c + x, 32 * hp + 16 : 32 * hp + 32, lanes] = dquery[16:, 128:].astype(BF)
                    dqkv_ref[2 * c + x, 128 + 32 * hp : 160 + 32 * hp, lanes] = dkey.astype(BF)
                    dqkv_ref[2 * c + x, 256 + 32 * hp : 288 + 32 * hp, lanes] = dvalue.astype(BF)
        ga_ref[:, COL_IN[0] : COL_IN[0] + 384] += dot_nt(n, dqkv_ref[2 * c])
        for x in range(2):
            pass_on(l, 0, c, x, dot_nn(w_ref[l, :, COL_IN[0] : COL_IN[0] + 384], dqkv_ref[2 * c + x]), xhat, inv)

    def each(count, stage, l):
        for i in range(count):
            stage(l, i)

    def forward_layer(l, carry):
        each(chunks, time_forward, l)
        each(items, var_forward, l)
        each(chunks, tail_forward, l)
        return carry

    lax.fori_loop(0, layers, forward_layer, 0)
    for b in range(items):
        for v in range(4):
            lanes = slice(128 * (v % 2), 128 * (v % 2) + 128)
            out_ref[b, v] = h_ref[2 * b + v // 2, :, lanes].T.astype(BF)

    gacc_ref[...] = jnp.zeros_like(gacc_ref)
    gt_ref[...] = jnp.zeros_like(gt_ref)
    gsmall_ref[...] = jnp.zeros_like(gsmall_ref)
    rest = 1 ^ dp
    def backward_layer(step, carry):
        l = layers - 1 - step
        ga_ref[...] = jnp.zeros_like(ga_ref)
        gd_ref[...] = jnp.zeros_like(gd_ref)
        each(chunks, feed_backward, l)
        each(chunks, token_backward, l)
        each(items, var_backward, l)
        each(chunks, time_backward, l)
        l_at = l ^ dp
        for f in range(SHARDS):
            down = jnp.concatenate([gd_ref[32 * f + 8 * a : 32 * f + 8 * a + 8, :] for a in range(4)], axis=1)
            block = jnp.concatenate([ga_ref[8 * f : 8 * f + 8, :], down], axis=1)
            gbig_ref[l_at, f] = block.astype(BF)
        gains_rows = [jnp.sum(gacc_ref[l * 4 + k].T, axis=0, keepdims=True) for k in range(4)]
        sums = [
            jnp.sum(w_ref[l, :, COL_OUT[k] : COL_OUT[k] + 128].astype(F32) * ga_ref[:, COL_OUT[k] : COL_OUT[k] + 128], axis=0, keepdims=True)
            for k in range(2)
        ]
        sums.append(gains_ref[l, 2:3, :] * gains_rows[2])
        sums.append(jnp.sum(wd_ref[l].astype(F32) * gd_ref[...], axis=0, keepdims=True))
        for k in range(4):
            gsmall_ref[rest, l * 4 + k, 10:11, :] = gains_rows[k]
            gsmall_ref[rest, l * 4 + k, 11:12, :] = sums[k] / scales_ref[l, k : k + 1, :]
        for block in range(8):
            gsmall_ref[dp, 8 * l + block] = gt_ref[l, 16 * block : 16 * block + 16, :]
        return carry

    lax.fori_loop(0, layers, backward_layer, 0)

    for x in range(2):
        cls_sum = None
        for b in range(items):
            prompt_sum = None
            for v in range(4):
                lanes = slice(128 * (v % 2), 128 * (v % 2) + 128)
                tokscr_ref[4 * b + v] = g_ref[x, 2 * b + v // 2, :, lanes].T
                head = tokscr_ref[4 * b + v, 0:10, :]
                last = tokscr_ref[4 * b + v, 127:128, :]
                prompt_sum = head if prompt_sum is None else prompt_sum + head
                cls_sum = last if cls_sum is None else cls_sum + last
                if x == 0:
                    pgrad_ref[b, v] = tokscr_ref[4 * b + v, 10:127, :]
            gsmall_ref[rest, 8 * x + ids_ref[b], 0:10, :] += prompt_sum
        gsmall_ref[rest, 8 * x, 12:13, :] = cls_sum


def run_tower(split, *operands):
    vmem = pl.BlockSpec(memory_space=pltpu.VMEM)
    smem = pl.BlockSpec(memory_space=pltpu.SMEM)
    return pl.pallas_call(
        functools.partial(tower_kernel, split),
        out_shape=(
            jax.ShapeDtypeStruct((2, 4, 128, 128), BF),
            jax.ShapeDtypeStruct((2, 4, 117, 128), F32),
            jax.ShapeDtypeStruct((2, SHARDS, 8, COLS), BF),
            jax.ShapeDtypeStruct((2, 16, 16, 128), F32),
        ),
        in_specs=[smem, smem] + [vmem] * 16,
        out_specs=[vmem] * 4,
        scratch_shapes=[
            pltpu.VMEM((2, 128, COLS), F32),
            pltpu.VMEM((2, 128, COL_DOWN), BF),
            pltpu.VMEM((2, 512, 128), BF),
            pltpu.VMEM((2, COL_DOWN, 128), BF),
            pltpu.VMEM((2, 128, 512), BF),
            pltpu.VMEM((16, 128, 256), F32),
            pltpu.VMEM((8, 128, 128), F32),
            pltpu.VMEM((4, 128, 256), F32),
            pltpu.VMEM((2, 4, 128, 256), F32),
            pltpu.VMEM((8, 4, 128, 256), F32),
            pltpu.VMEM((8, 4, 1, 256), F32),
            pltpu.VMEM((2, 4, 384, 256), BF),
            pltpu.VMEM((2, 8, 128, 1024), BF),
            pltpu.VMEM((2, 4, 128, 256), BF),
            pltpu.VMEM((2, 4, 384, 256), BF),
            pltpu.VMEM((2, 2, 4, 8, 512), F32),
            pltpu.VMEM((2, 4, 128, 256), BF),
            pltpu.VMEM((2, 2, 4, 128, 512), BF),
            pltpu.VMEM((2, 512, 256), BF),
            pltpu.VMEM((4, 1024, 256), BF),
            pltpu.VMEM((8, 384, 256), BF),
            pltpu.VMEM((8, 128, 256), BF),
            pltpu.VMEM((128, COL_DOWN), F32),
            pltpu.VMEM((512, 128), F32),
            pltpu.VMEM((2, 128, 128), F32),
            pltpu.VMEM((8, 128, 128), F32),
        ],
        compiler_params=pltpu.CompilerParams(vmem_limit_bytes=56 * 1024 * 1024),
        name="tower",
    )(*operands)


def pack_rows(attn_in, attn_out, feed_in, feed_out):
    layers, _, rows, _ = attn_in.shape
    down = feed_out.reshape(layers, 4, rows, 128)
    return jnp.concatenate(
        [attn_in[:, 0], attn_in[:, 1], attn_out[:, 0], attn_out[:, 1], feed_in] + [down[:, a] for a in range(4)], axis=2
    )


def unpack_rows(packed):
    layers, rows, _ = packed.shape
    attn_in = jnp.stack([packed[:, :, at : at + 384] for at in COL_IN], axis=1)
    attn_out = jnp.stack([packed[:, :, at : at + 128] for at in COL_OUT], axis=1)
    feed_in = packed[:, :, COL_FEED:COL_DOWN]
    feed_out = jnp.stack([packed[:, :, COL_DOWN + 128 * a : COL_DOWN + 128 * a + 128] for a in range(4)], axis=1)
    return attn_in, attn_out, feed_in, feed_out.reshape(layers, 4 * rows, 128)


def flip(array, axis, bit, size):
    return lax.ppermute(array, axis, [(i, i ^ (1 << bit)) for i in range(size)])


def swap(array, mask):
    return lax.ppermute(array, "fsdp", [(i, i ^ mask) for i in range(SHARDS)])


def gather_rows(attn_in, attn_out, feed_in, feed_out):
    vmem = pl.BlockSpec(memory_space=pltpu.VMEM)
    row = pl.pallas_call(
        pack_kernel, out_shape=jax.ShapeDtypeStruct((1, 8, COLS), BF), in_specs=[vmem] * 4, out_specs=vmem, name="pack",
    )(attn_in, attn_out, feed_in, feed_out)
    column = jnp.concatenate([row] + [swap(row, 4 * z) for z in range(1, 4)], axis=0)
    mine = [column] + [swap(column, xy) for xy in range(1, 4)]
    return mine + [flip(part, "dp", 0, 2) for part in mine]


def reduce_big(big):
    held = big[0].astype(F32) + flip(big[1], "dp", 0, 2).astype(F32)
    parts = lax.all_to_all(held.astype(BF), "fsdp", 0, 0, tiled=True)
    return jnp.sum(parts.astype(F32), axis=0)


def reduce_small(small):
    held = small[0] + flip(small[1].astype(BF), "dp", 0, 2).astype(F32)
    for bit in STEP_BITS[::-1]:
        mine = held.astype(BF)
        held = mine.astype(F32) + flip(mine, "fsdp", bit, SHARDS).astype(F32)
    return held


def both_cores(mine, dp):
    other = flip(mine, "dp", 0, 2)
    return jnp.where(dp == 0, mine, other), jnp.where(dp == 0, other, mine)


def per_device(shard_count, patches, prompts, cls_token, attn_in, attn_out, feed_in, feed_out, token_operator,
               norm_gains, branch_scales, var_counts, dataset_ids, cotangent, adjust_cotangent):
    dp = lax.axis_index("dp")
    fast = shard_count == SHARDS
    if fast:
        gathered = gather_rows(attn_in, attn_out, feed_in, feed_out)
    else:
        whole_down = lax.all_gather(feed_out, "fsdp", axis=1, tiled=True)
        whole_down = whole_down.reshape(2, SHARDS, 4, 8, 128).transpose(0, 2, 1, 3, 4).reshape(2, 512, 128)
        rows = pack_rows(
            lax.all_gather(attn_in, "fsdp", axis=2, tiled=True),
            lax.all_gather(attn_out, "fsdp", axis=2, tiled=True),
            lax.all_gather(feed_in, "fsdp", axis=1, tiled=True),
            whole_down,
        )
        rows = rows.reshape(2, SHARDS, 8, COLS).transpose(1, 0, 2, 3)
        gathered = [rows[:, l].reshape(4, 4, 8, COLS)[:, xy] for l in range(2) for xy in range(4)]
    output, patch_grad, big, small = run_tower(
        fast, dataset_ids, var_counts, *gathered, token_operator, norm_gains, branch_scales, patches, prompts,
        cls_token.reshape(1, -1), cotangent, adjust_cotangent,
    )
    if fast:
        layer_grads = both_cores(reduce_big(big), dp)
        grads = unpack_rows(jnp.stack(layer_grads))
        tokens, rest = both_cores(reduce_small(small), dp)
    else:
        rows = big.astype(F32).reshape(2, 128, COLS)
        attn_in_g, attn_out_g, feed_in_g, feed_out_g = unpack_rows(rows)
        feed_out_g = feed_out_g.reshape(2, 4, SHARDS, 8, 128).transpose(0, 2, 1, 3, 4).reshape(2, 512, 128)
        grads = (
            lax.psum_scatter(lax.psum(attn_in_g, "dp"), "fsdp", scatter_dimension=2, tiled=True),
            lax.psum_scatter(lax.psum(attn_out_g, "dp"), "fsdp", scatter_dimension=2, tiled=True),
            lax.psum_scatter(lax.psum(feed_in_g, "dp"), "fsdp", scatter_dimension=1, tiled=True),
            lax.psum_scatter(lax.psum(feed_out_g, "dp"), "fsdp", scatter_dimension=1, tiled=True),
        )
        tokens, rest = lax.psum(small, ("dp", "fsdp"))
    token_grad = tokens.reshape(2, 128, 128)
    gains_grad = rest[:8, 10].reshape(2, 4, 128)
    scales_grad = rest[:8, 11].reshape(2, 4, 128)
    return (
        output, patch_grad, rest[:8, :10], rest[0, 12], *grads, token_grad, gains_grad, scales_grad,
        rest[8:, :10], rest[8, 12],
    )


def solution(mesh):
    batch = P(("dp", "fsdp"), None, None, None)
    wide = P(None, None, "fsdp", None)
    tall = P(None, "fsdp", None)
    return jax.shard_map(
        functools.partial(per_device, mesh.shape["fsdp"]),
        mesh=mesh,
        in_specs=(batch, P(), P(), wide, wide, tall, tall, P(), P(), P(), P(), P(("dp", "fsdp")), batch, batch),
        out_specs=(batch, batch, P(), P(), wide, wide, tall, tall, P(), P(), P(), P(), P()),
        check_vma=False,
    )
```

```python
import functools

import jax
import jax.numpy as jnp
from jax import lax
from jax.experimental import pallas as pl
from jax.experimental.pallas import tpu as pltpu
from jax.sharding import PartitionSpec as P

HEADS = 8
EPSILON = 1e-05
NEG_FILL = -1000000000.0
BF = jnp.bfloat16
F32 = jnp.float32

COL_IN = (0, 384)
COL_OUT = (768, 896)
COL_FEED = 1024
COL_DOWN = 2048
COLS = 2560
SHARDS = 16
STEP_BITS = (2, 3, 0, 1)


def dot_nn(a, b):
    return lax.dot_general(a, b, (((1,), (0,)), ((), ())), preferred_element_type=F32)


def dot_nt(a, b):
    return lax.dot_general(a, b, (((1,), (1,)), ((), ())), preferred_element_type=F32)


def norm_cols(x):
    centered = x - jnp.mean(x, axis=0, keepdims=True)
    inv = lax.rsqrt(jnp.mean(centered * centered, axis=0, keepdims=True) + EPSILON)
    return centered * inv, inv


def norm_cols_back(dn, gain, xhat, inv):
    e = dn * gain
    m1 = jnp.mean(e, axis=0, keepdims=True)
    m2 = jnp.mean(e * xhat, axis=0, keepdims=True)
    return inv * (e - m1 - xhat * m2)


def fold(part):
    return part[:, :128] + part[:, 128:]


def pack_kernel(attn_in_ref, attn_out_ref, feed_in_ref, feed_out_ref, out_ref):
    l = lax.axis_index("dp")
    down = feed_out_ref[l].astype(F32)
    parts = [attn_in_ref[l, 0], attn_in_ref[l, 1], attn_out_ref[l, 0], attn_out_ref[l, 1], feed_in_ref[l]]
    parts = [part.astype(F32) for part in parts] + [down[8 * a : 8 * a + 8] for a in range(4)]
    out_ref[0] = jnp.concatenate(parts, axis=1).astype(BF)


def tower_kernel(
    split,
    ids_ref, counts_ref, wmine0_ref, wmine1_ref, wmine2_ref, wmine3_ref, wother0_ref, wother1_ref, wother2_ref, wother3_ref,
    tok_ref, gains_ref, scales_ref, patches_ref, prompts_ref,
    cls_ref, cot_ref, adj_ref,
    out_ref, pgrad_ref, gbig_ref, gsmall_ref,
    stage_ref, w_ref, wd_ref, wt_ref, wdt_ref, colb_ref, tokscr_ref, h_ref, g_ref, xh_ref, inv_ref,
    qkvt_ref, pb_ref, ot_ref, qkvv_ref, pv_ref, ov_ref, pw_ref, qbd_ref, dob_ref, hid_ref, du_ref, dqkv_ref,
    dov_ref, ga_ref, gd_ref, gt_ref, gacc_ref,
):
    dp = lax.axis_index("dp") if split else 0
    me = lax.axis_index("fsdp") if split else 0
    layers = 2
    chunks = 4
    items = 2

    for rel in range(SHARDS):
        rows = pl.ds(pl.multiple_of(8 * (me ^ rel), 8), 8)
        mine_ref = (wmine0_ref, wmine1_ref, wmine2_ref, wmine3_ref)[rel % 4]
        other_ref = (wother0_ref, wother1_ref, wother2_ref, wother3_ref)[rel % 4]
        stage_ref[dp, rows, :] = mine_ref[rel // 4].astype(F32)
        stage_ref[1 - dp, rows, :] = other_ref[rel // 4].astype(F32)
    for l in range(layers):
        for pair in range(SHARDS // 2):
            lo = stage_ref[l, 16 * pair : 16 * pair + 8, :]
            hi = stage_ref[l, 16 * pair + 8 : 16 * pair + 16, :]
            w_ref[l, 16 * pair : 16 * pair + 16, :] = jnp.concatenate([lo[:, :COL_DOWN], hi[:, :COL_DOWN]], axis=0).astype(BF)
            for half, part in enumerate((lo, hi)):
                base = 64 * pair + 32 * half
                wd_ref[l, base : base + 32, :] = jnp.concatenate(
                    [part[:, COL_DOWN + 128 * a : COL_DOWN + 128 * a + 128] for a in range(4)], axis=0
                ).astype(BF)
        for block in range(COL_DOWN // 128):
            wt_ref[l, 128 * block : 128 * block + 128, :] = w_ref[l, :, 128 * block : 128 * block + 128].T
        for block in range(4):
            wdt_ref[l, :, 128 * block : 128 * block + 128] = wd_ref[l, 128 * block : 128 * block + 128, :].T
        for k in range(4):
            for offset, rows in ((0, gains_ref), (4, scales_ref)):
                col = jnp.broadcast_to(rows[l, k : k + 1, :], (128, 128)).T
                colb_ref[l * 8 + offset + k, :, 0:128] = col
                colb_ref[l * 8 + offset + k, :, 128:256] = col

    for b in range(items):
        ident = ids_ref[b]
        for v in range(4):
            bv = 4 * b + v
            tokscr_ref[bv, 0:10, :] = prompts_ref[ident].astype(F32)
            tokscr_ref[bv, 10:127, :] = patches_ref[b, v].astype(F32)
            tokscr_ref[bv, 127:128, :] = cls_ref[...].astype(F32)
            lanes = slice(128 * (v % 2), 128 * (v % 2) + 128)
            h_ref[2 * b + v // 2, :, lanes] = tokscr_ref[bv].T
            g_ref[0, 2 * b + v // 2, :, lanes] = cot_ref[b, v].astype(F32).T
            g_ref[1, 2 * b + v // 2, :, lanes] = adj_ref[b, v].astype(F32).T

    head_row = lax.broadcasted_iota(jnp.int32, (8, 128), 0)
    head_col = lax.broadcasted_iota(jnp.int32, (8, 128), 1) // 16
    gather_heads = jnp.where(head_row == head_col, 1.0, 0.0).astype(BF)
    spread_row = lax.broadcasted_iota(jnp.int32, (128, 8), 0) // 16
    spread_col = lax.broadcasted_iota(jnp.int32, (128, 8), 1)
    spread_heads = jnp.where(spread_row == spread_col, 1.0, 0.0).astype(BF)

    def head_sums(left, rights):
        return dot_nn(gather_heads, jnp.concatenate([(left * right).astype(BF) for right in rights], axis=1))

    def diag_heads(target_ref, at, rows):
        for head in range(HEADS):
            target_ref[at, 16 * head : 16 * head + 16, 128 * head : 128 * head + 128] = rows[16 * head : 16 * head + 16]

    qbd_ref[...] = jnp.zeros_like(qbd_ref)
    dob_ref[...] = jnp.zeros_like(dob_ref)

    def gain(l, k):
        return colb_ref[l * 8 + k]

    def scale(l, k):
        return colb_ref[l * 8 + 4 + k]

    def keep_norm(l, k, c, x):
        xhat, inv = norm_cols(x)
        xh_ref[l * 4 + k, c] = xhat
        inv_ref[l * 4 + k, c] = inv
        return (xhat * gain(l, k)).astype(BF)

    def time_forward(l, c):
        x = h_ref[c]
        n = keep_norm(l, 0, c, x)
        qkv = dot_nn(wt_ref[l, 0:384, :], n)
        queries = (qkv[:128] * 0.25).astype(BF)
        keys = qkv[128:256].astype(BF)
        values = qkv[256:].astype(BF)
        qkvt_ref[l, c, 0:128, :] = queries
        qkvt_ref[l, c, 128:256, :] = keys
        qkvt_ref[l, c, 256:384, :] = values
        for s in range(2):
            lanes = slice(128 * s, 128 * s + 128)
            at = 2 * (c % 2) + s
            diag_heads(qbd_ref, at, queries[:, lanes])
            key_rows = keys[:, lanes].T
            for hp in range(4):
                span = slice(256 * hp, 256 * hp + 256)
                rows = slice(32 * hp, 32 * hp + 32)
                scores = dot_nn(key_rows, qbd_ref[at, :, span])
                shifted = jnp.exp(scores - jnp.max(scores, axis=0, keepdims=True))
                prob = (shifted * (1.0 / jnp.sum(shifted, axis=0, keepdims=True))).astype(BF)
                pb_ref[l, 2 * c + s, :, span] = prob
                mixed = dot_nn(values[rows, lanes], prob)
                ot_ref[l, c, 32 * hp : 32 * hp + 16, lanes] = mixed[:16, :128].astype(BF)
                ot_ref[l, c, 32 * hp + 16 : 32 * hp + 32, lanes] = mixed[16:, 128:].astype(BF)
        branch = dot_nn(wt_ref[l, COL_OUT[0] : COL_OUT[0] + 128, :], ot_ref[l, c])
        h_ref[c] = x + scale(l, 0) * branch

    def var_forward(l, b):
        for cc in range(2):
            c = 2 * b + cc
            n = keep_norm(l, 1, c, h_ref[c])
            qkv = dot_nn(wt_ref[l, COL_IN[1] : COL_IN[1] + 384, :], n)
            qkvv_ref[l, c, 0:128, :] = (qkv[:128] * 0.25).astype(BF)
            qkvv_ref[l, c, 128:384, :] = qkv[128:].astype(BF)
        count = counts_ref[ids_ref[b]]

        def slot(first, i):
            lanes = slice(128 * (i % 2), 128 * (i % 2) + 128)
            return qkvv_ref[l, 2 * b + i // 2, first : first + 128, lanes].astype(F32)

        key_slots = [slot(128, j) for j in range(4)]
        value_slots = [slot(256, j) for j in range(4)]
        for i in range(4):
            scores = head_sums(slot(0, i), key_slots)
            parts = [scores[:, 128 * j : 128 * j + 128] for j in range(4)]
            parts = [jnp.where(jnp.full((8, 128), count, jnp.int32) > j, parts[j], NEG_FILL) for j in range(4)]
            top = jnp.maximum(jnp.maximum(parts[0], parts[1]), jnp.maximum(parts[2], parts[3]))
            shifted = [jnp.exp(part - top) for part in parts]
            total = 1.0 / ((shifted[0] + shifted[1]) + (shifted[2] + shifted[3]))
            prob = jnp.concatenate([part * total for part in shifted], axis=1)
            pv_ref[l, b, i] = prob
            spread = dot_nn(spread_heads, prob.astype(BF))
            pw_ref[l, b, i] = spread.astype(BF)
            mixed = spread[:, :128] * value_slots[0]
            for j in range(1, 4):
                mixed = mixed + spread[:, 128 * j : 128 * j + 128] * value_slots[j]
            lanes = slice(128 * (i % 2), 128 * (i % 2) + 128)
            ov_ref[l, 2 * b + i // 2, :, lanes] = mixed.astype(BF)
        for cc in range(2):
            c = 2 * b + cc
            branch = dot_nn(wt_ref[l, COL_OUT[1] : COL_OUT[1] + 128, :], ov_ref[l, c])
            h_ref[c] = h_ref[c] + scale(l, 1) * branch

    def tail_forward(l, c):
        x = h_ref[c]
        n = keep_norm(l, 2, c, x)
        mix = [dot_nt(n[:, 128 * s : 128 * s + 128], tok_ref[l]) for s in range(2)]
        x = x + scale(l, 2) * jnp.concatenate(mix, axis=1)
        n = keep_norm(l, 3, c, x)
        for z in range(4):
            gate = dot_nn(wt_ref[l, COL_FEED + 128 * z : COL_FEED + 128 * z + 128, :], n)
            up = dot_nn(wt_ref[l, COL_FEED + 512 + 128 * z : COL_FEED + 640 + 128 * z, :], n)
            sig = 0.5 * jnp.tanh(0.5 * gate) + 0.5
            hid_ref[c % 2, 128 * z : 128 * z + 128, :] = (gate * sig * up).astype(BF)
        h_ref[c] = x + scale(l, 3) * dot_nn(wdt_ref[l], hid_ref[c % 2])

    def norm_of(l, k, c):
        xhat = xh_ref[l * 4 + k, c]
        return xhat, inv_ref[l * 4 + k, c], (xhat * gain(l, k)).astype(BF)

    def pass_on(l, k, c, x, dn, xhat, inv):
        if x == 0:
            gacc_ref[l * 4 + k] += fold(dn * xhat)
        g_ref[x, c] += norm_cols_back(dn, gain(l, k), xhat, inv)

    def feed_backward(l, c):
        xhat, inv, n = norm_of(l, 3, c)
        dz = [(scale(l, 3) * g_ref[x, c]).astype(BF) for x in range(2)]
        for z in range(4):
            rows = slice(128 * z, 128 * z + 128)
            gate = dot_nn(wt_ref[l, COL_FEED + 128 * z : COL_FEED + 128 * z + 128, :], n)
            up = dot_nn(wt_ref[l, COL_FEED + 512 + 128 * z : COL_FEED + 640 + 128 * z, :], n)
            sig = 0.5 * jnp.tanh(0.5 * gate) + 0.5
            act = gate * sig
            hid_ref[c % 2, rows, :] = (act * up).astype(BF)
            slope = up * (sig * (1.0 + gate * (1.0 - sig)))
            for x in range(2):
                dhid = dot_nn(wd_ref[l, rows, :], dz[x])
                du_ref[2 * (c % 2) + x, 128 * z : 128 * z + 128, :] = (dhid * slope).astype(BF)
                du_ref[2 * (c % 2) + x, 512 + 128 * z : 640 + 128 * z, :] = (dhid * act).astype(BF)
        ga_ref[:, COL_FEED:COL_DOWN] += dot_nt(n, du_ref[2 * (c % 2)])
        gd_ref[...] += dot_nt(hid_ref[c % 2], dz[0])
        for x in range(2):
            dn = dot_nn(w_ref[l, :, COL_FEED:COL_DOWN], du_ref[2 * (c % 2) + x])
            pass_on(l, 3, c, x, dn, xhat, inv)

    def token_backward(l, c):
        xhat, inv, n = norm_of(l, 2, c)
        for x in range(2):
            dy = (scale(l, 2) * g_ref[x, c]).astype(BF)
            dn = []
            for s in range(2):
                part = dy[:, 128 * s : 128 * s + 128]
                dn.append(dot_nn(part, tok_ref[l]))
                if x == 0:
                    gt_ref[l] += dot_nn(part.T, n[:, 128 * s : 128 * s + 128])
            pass_on(l, 2, c, x, jnp.concatenate(dn, axis=1), xhat, inv)

    def var_backward(l, b):
        def slot(first, i):
            lanes = slice(128 * (i % 2), 128 * (i % 2) + 128)
            return qkvv_ref[l, 2 * b + i // 2, first : first + 128, lanes].astype(F32)

        for x in range(2):
            for cc in range(2):
                c = 2 * b + cc
                dt = (scale(l, 1) * g_ref[x, c]).astype(BF)
                dov_ref[4 * b + 2 * x + cc] = dot_nn(w_ref[l, :, COL_OUT[1] : COL_OUT[1] + 128], dt).astype(BF)
                if x == 0:
                    ga_ref[:, COL_OUT[1] : COL_OUT[1] + 128] += dot_nt(ov_ref[l, c], dt)
            value_slots = [slot(256, j) for j in range(4)]
            dkeys = [0.0] * 4
            dvalues = [0.0] * 4
            for i in range(4):
                lanes = slice(128 * (i % 2), 128 * (i % 2) + 128)
                grad = dov_ref[4 * b + 2 * x + i // 2, :, lanes].astype(F32)
                query = slot(0, i)
                prob = pv_ref[l, b, i]
                weighted = prob * head_sums(grad, value_slots)
                total = (weighted[:, :128] + weighted[:, 128:256]) + (weighted[:, 256:384] + weighted[:, 384:])
                ds = weighted - prob * jnp.concatenate([total] * 4, axis=1)
                ds_wide = dot_nn(spread_heads, ds.astype(BF))
                ds_slots = [ds_wide[:, 128 * j : 128 * j + 128] for j in range(4)]
                terms = [ds_slots[j] * slot(128, j) for j in range(4)]
                dquery = (terms[0] + terms[1]) + (terms[2] + terms[3])
                for j in range(4):
                    dkeys[j] = dkeys[j] + ds_slots[j] * query
                    dvalues[j] = dvalues[j] + pw_ref[l, b, i, :, 128 * j : 128 * j + 128].astype(F32) * grad
                dqkv_ref[4 * b + 2 * x + i // 2, 0:128, lanes] = (dquery * 0.25).astype(BF)
            for j in range(4):
                lanes = slice(128 * (j % 2), 128 * (j % 2) + 128)
                dqkv_ref[4 * b + 2 * x + j // 2, 128:256, lanes] = dkeys[j].astype(BF)
                dqkv_ref[4 * b + 2 * x + j // 2, 256:384, lanes] = dvalues[j].astype(BF)
            for cc in range(2):
                c = 2 * b + cc
                xhat, inv, n = norm_of(l, 1, c)
                dqkv = dqkv_ref[4 * b + 2 * x + cc]
                if x == 0:
                    ga_ref[:, COL_IN[1] : COL_IN[1] + 384] += dot_nt(n, dqkv)
                pass_on(l, 1, c, x, dot_nn(w_ref[l, :, COL_IN[1] : COL_IN[1] + 384], dqkv), xhat, inv)

    def time_backward(l, c):
        xhat, inv, n = norm_of(l, 0, c)
        queries = qkvt_ref[l, c, 0:128, :]
        keys = qkvt_ref[l, c, 128:256, :]
        values = qkvt_ref[l, c, 256:384, :]
        grads = []
        for x in range(2):
            dt = (scale(l, 0) * g_ref[x, c]).astype(BF)
            grads.append(dot_nn(w_ref[l, :, COL_OUT[0] : COL_OUT[0] + 128], dt).astype(BF))
            if x == 0:
                ga_ref[:, COL_OUT[0] : COL_OUT[0] + 128] += dot_nt(ot_ref[l, c], dt)
        for s in range(2):
            lanes = slice(128 * s, 128 * s + 128)
            at = 2 * (c % 2) + s
            diag_heads(qbd_ref, at, queries[:, lanes])
            value_rows = values[:, lanes].T
            for x in range(2):
                diag_heads(dob_ref, 2 * at + x, grads[x][:, lanes])
            for hp in range(4):
                span = slice(256 * hp, 256 * hp + 256)
                rows = slice(32 * hp, 32 * hp + 32)
                prob_bf = pb_ref[l, 2 * c + s, :, span]
                prob = prob_bf.astype(F32)
                for x in range(2):
                    weighted = prob * dot_nn(value_rows, dob_ref[2 * at + x, :, span])
                    ds = (weighted - prob * jnp.sum(weighted, axis=0, keepdims=True)).astype(BF)
                    dvalue = dot_nt(dob_ref[2 * at + x, rows, span], prob_bf)
                    dquery = dot_nn(keys[rows, lanes], ds) * 0.25
                    dkey = dot_nt(qbd_ref[at, rows, span], ds)
                    dqkv_ref[2 * c + x, 32 * hp : 32 * hp + 16, lanes] = dquery[:16, :128].astype(BF)
                    dqkv_ref[2 * c + x, 32 * hp + 16 : 32 * hp + 32, lanes] = dquery[16:, 128:].astype(BF)
                    dqkv_ref[2 * c + x, 128 + 32 * hp : 160 + 32 * hp, lanes] = dkey.astype(BF)
                    dqkv_ref[2 * c + x, 256 + 32 * hp : 288 + 32 * hp, lanes] = dvalue.astype(BF)
        ga_ref[:, COL_IN[0] : COL_IN[0] + 384] += dot_nt(n, dqkv_ref[2 * c])
        for x in range(2):
            pass_on(l, 0, c, x, dot_nn(w_ref[l, :, COL_IN[0] : COL_IN[0] + 384], dqkv_ref[2 * c + x]), xhat, inv)

    def each(count, stage, l):
        for i in range(count):
            stage(l, i)

    def forward_layer(l, carry):
        each(chunks, time_forward, l)
        each(items, var_forward, l)
        each(chunks, tail_forward, l)
        return carry

    lax.fori_loop(0, layers, forward_layer, 0)
    for b in range(items):
        for v in range(4):
            lanes = slice(128 * (v % 2), 128 * (v % 2) + 128)
            out_ref[b, v] = h_ref[2 * b + v // 2, :, lanes].T.astype(BF)

    gacc_ref[...] = jnp.zeros_like(gacc_ref)
    gt_ref[...] = jnp.zeros_like(gt_ref)
    gsmall_ref[...] = jnp.zeros_like(gsmall_ref)
    rest = 1 ^ dp
    def backward_layer(step, carry):
        l = layers - 1 - step
        ga_ref[...] = jnp.zeros_like(ga_ref)
        gd_ref[...] = jnp.zeros_like(gd_ref)
        each(chunks, feed_backward, l)
        each(chunks, token_backward, l)
        each(items, var_backward, l)
        each(chunks, time_backward, l)
        l_at = l ^ dp
        for f in range(SHARDS):
            down = jnp.concatenate([gd_ref[32 * f + 8 * a : 32 * f + 8 * a + 8, :] for a in range(4)], axis=1)
            block = jnp.concatenate([ga_ref[8 * f : 8 * f + 8, :], down], axis=1)
            gbig_ref[l_at, f] = block.astype(BF)
        gains_rows = [jnp.sum(gacc_ref[l * 4 + k].T, axis=0, keepdims=True) for k in range(4)]
        sums = [
            jnp.sum(w_ref[l, :, COL_OUT[k] : COL_OUT[k] + 128].astype(F32) * ga_ref[:, COL_OUT[k] : COL_OUT[k] + 128], axis=0, keepdims=True)
            for k in range(2)
        ]
        sums.append(gains_ref[l, 2:3, :] * gains_rows[2])
        sums.append(jnp.sum(wd_ref[l].astype(F32) * gd_ref[...], axis=0, keepdims=True))
        for k in range(4):
            gsmall_ref[rest, l * 4 + k, 10:11, :] = gains_rows[k]
            gsmall_ref[rest, l * 4 + k, 11:12, :] = sums[k] / scales_ref[l, k : k + 1, :]
        for block in range(8):
            gsmall_ref[dp, 8 * l + block] = gt_ref[l, 16 * block : 16 * block + 16, :]
        return carry

    lax.fori_loop(0, layers, backward_layer, 0)

    for x in range(2):
        cls_sum = None
        for b in range(items):
            prompt_sum = None
            for v in range(4):
                lanes = slice(128 * (v % 2), 128 * (v % 2) + 128)
                tokscr_ref[4 * b + v] = g_ref[x, 2 * b + v // 2, :, lanes].T
                head = tokscr_ref[4 * b + v, 0:10, :]
                last = tokscr_ref[4 * b + v, 127:128, :]
                prompt_sum = head if prompt_sum is None else prompt_sum + head
                cls_sum = last if cls_sum is None else cls_sum + last
                if x == 0:
                    pgrad_ref[b, v] = tokscr_ref[4 * b + v, 10:127, :]
            gsmall_ref[rest, 8 * x + ids_ref[b], 0:10, :] += prompt_sum
        gsmall_ref[rest, 8 * x, 12:13, :] = cls_sum


def run_tower(split, *operands):
    vmem = pl.BlockSpec(memory_space=pltpu.VMEM)
    smem = pl.BlockSpec(memory_space=pltpu.SMEM)
    return pl.pallas_call(
        functools.partial(tower_kernel, split),
        out_shape=(
            jax.ShapeDtypeStruct((2, 4, 128, 128), BF),
            jax.ShapeDtypeStruct((2, 4, 117, 128), F32),
            jax.ShapeDtypeStruct((2, SHARDS, 8, COLS), BF),
            jax.ShapeDtypeStruct((2, 16, 16, 128), F32),
        ),
        in_specs=[smem, smem] + [vmem] * 16,
        out_specs=[vmem] * 4,
        scratch_shapes=[
            pltpu.VMEM((2, 128, COLS), F32),
            pltpu.VMEM((2, 128, COL_DOWN), BF),
            pltpu.VMEM((2, 512, 128), BF),
            pltpu.VMEM((2, COL_DOWN, 128), BF),
            pltpu.VMEM((2, 128, 512), BF),
            pltpu.VMEM((16, 128, 256), F32),
            pltpu.VMEM((8, 128, 128), F32),
            pltpu.VMEM((4, 128, 256), F32),
            pltpu.VMEM((2, 4, 128, 256), F32),
            pltpu.VMEM((8, 4, 128, 256), F32),
            pltpu.VMEM((8, 4, 1, 256), F32),
            pltpu.VMEM((2, 4, 384, 256), BF),
            pltpu.VMEM((2, 8, 128, 1024), BF),
            pltpu.VMEM((2, 4, 128, 256), BF),
            pltpu.VMEM((2, 4, 384, 256), BF),
            pltpu.VMEM((2, 2, 4, 8, 512), F32),
            pltpu.VMEM((2, 4, 128, 256), BF),
            pltpu.VMEM((2, 2, 4, 128, 512), BF),
            pltpu.VMEM((4, 128, 1024), BF),
            pltpu.VMEM((8, 128, 1024), BF),
            pltpu.VMEM((2, 512, 256), BF),
            pltpu.VMEM((4, 1024, 256), BF),
            pltpu.VMEM((8, 384, 256), BF),
            pltpu.VMEM((8, 128, 256), BF),
            pltpu.VMEM((128, COL_DOWN), F32),
            pltpu.VMEM((512, 128), F32),
            pltpu.VMEM((2, 128, 128), F32),
            pltpu.VMEM((8, 128, 128), F32),
        ],
        compiler_params=pltpu.CompilerParams(vmem_limit_bytes=56 * 1024 * 1024),
        name="tower",
    )(*operands)


def pack_rows(attn_in, attn_out, feed_in, feed_out):
    layers, _, rows, _ = attn_in.shape
    down = feed_out.reshape(layers, 4, rows, 128)
    return jnp.concatenate(
        [attn_in[:, 0], attn_in[:, 1], attn_out[:, 0], attn_out[:, 1], feed_in] + [down[:, a] for a in range(4)], axis=2
    )


def unpack_rows(packed):
    layers, rows, _ = packed.shape
    attn_in = jnp.stack([packed[:, :, at : at + 384] for at in COL_IN], axis=1)
    attn_out = jnp.stack([packed[:, :, at : at + 128] for at in COL_OUT], axis=1)
    feed_in = packed[:, :, COL_FEED:COL_DOWN]
    feed_out = jnp.stack([packed[:, :, COL_DOWN + 128 * a : COL_DOWN + 128 * a + 128] for a in range(4)], axis=1)
    return attn_in, attn_out, feed_in, feed_out.reshape(layers, 4 * rows, 128)


def flip(array, axis, bit, size):
    return lax.ppermute(array, axis, [(i, i ^ (1 << bit)) for i in range(size)])


def swap(array, mask):
    return lax.ppermute(array, "fsdp", [(i, i ^ mask) for i in range(SHARDS)])


def gather_rows(attn_in, attn_out, feed_in, feed_out):
    vmem = pl.BlockSpec(memory_space=pltpu.VMEM)
    row = pl.pallas_call(
        pack_kernel, out_shape=jax.ShapeDtypeStruct((1, 8, COLS), BF), in_specs=[vmem] * 4, out_specs=vmem, name="pack",
    )(attn_in, attn_out, feed_in, feed_out)
    column = jnp.concatenate([row] + [swap(row, 4 * z) for z in range(1, 4)], axis=0)
    mine = [column] + [swap(column, xy) for xy in range(1, 4)]
    return mine + [flip(part, "dp", 0, 2) for part in mine]


def reduce_big(big):
    held = big[0].astype(F32) + flip(big[1], "dp", 0, 2).astype(F32)
    parts = lax.all_to_all(held.astype(BF), "fsdp", 0, 0, tiled=True)
    return jnp.sum(parts.astype(F32), axis=0)


def reduce_small(small):
    held = small[0] + flip(small[1].astype(BF), "dp", 0, 2).astype(F32)
    for bit in STEP_BITS[::-1]:
        mine = held.astype(BF)
        held = mine.astype(F32) + flip(mine, "fsdp", bit, SHARDS).astype(F32)
    return held


def both_cores(mine, dp):
    other = flip(mine, "dp", 0, 2)
    return jnp.where(dp == 0, mine, other), jnp.where(dp == 0, other, mine)


def per_device(shard_count, patches, prompts, cls_token, attn_in, attn_out, feed_in, feed_out, token_operator,
               norm_gains, branch_scales, var_counts, dataset_ids, cotangent, adjust_cotangent):
    dp = lax.axis_index("dp")
    fast = shard_count == SHARDS
    if fast:
        gathered = gather_rows(attn_in, attn_out, feed_in, feed_out)
    else:
        whole_down = lax.all_gather(feed_out, "fsdp", axis=1, tiled=True)
        whole_down = whole_down.reshape(2, SHARDS, 4, 8, 128).transpose(0, 2, 1, 3, 4).reshape(2, 512, 128)
        rows = pack_rows(
            lax.all_gather(attn_in, "fsdp", axis=2, tiled=True),
            lax.all_gather(attn_out, "fsdp", axis=2, tiled=True),
            lax.all_gather(feed_in, "fsdp", axis=1, tiled=True),
            whole_down,
        )
        rows = rows.reshape(2, SHARDS, 8, COLS).transpose(1, 0, 2, 3)
        gathered = [rows[:, l].reshape(4, 4, 8, COLS)[:, xy] for l in range(2) for xy in range(4)]
    output, patch_grad, big, small = run_tower(
        fast, dataset_ids, var_counts, *gathered, token_operator, norm_gains, branch_scales, patches, prompts,
        cls_token.reshape(1, -1), cotangent, adjust_cotangent,
    )
    if fast:
        layer_grads = both_cores(reduce_big(big), dp)
        grads = unpack_rows(jnp.stack(layer_grads))
        tokens, rest = both_cores(reduce_small(small), dp)
    else:
        rows = big.astype(F32).reshape(2, 128, COLS)
        attn_in_g, attn_out_g, feed_in_g, feed_out_g = unpack_rows(rows)
        feed_out_g = feed_out_g.reshape(2, 4, SHARDS, 8, 128).transpose(0, 2, 1, 3, 4).reshape(2, 512, 128)
        grads = (
            lax.psum_scatter(lax.psum(attn_in_g, "dp"), "fsdp", scatter_dimension=2, tiled=True),
            lax.psum_scatter(lax.psum(attn_out_g, "dp"), "fsdp", scatter_dimension=2, tiled=True),
            lax.psum_scatter(lax.psum(feed_in_g, "dp"), "fsdp", scatter_dimension=1, tiled=True),
            lax.psum_scatter(lax.psum(feed_out_g, "dp"), "fsdp", scatter_dimension=1, tiled=True),
        )
        tokens, rest = lax.psum(small, ("dp", "fsdp"))
    token_grad = tokens.reshape(2, 128, 128)
    gains_grad = rest[:8, 10].reshape(2, 4, 128)
    scales_grad = rest[:8, 11].reshape(2, 4, 128)
    return (
        output, patch_grad, rest[:8, :10], rest[0, 12], *grads, token_grad, gains_grad, scales_grad,
        rest[8:, :10], rest[8, 12],
    )


def solution(mesh):
    batch = P(("dp", "fsdp"), None, None, None)
    wide = P(None, None, "fsdp", None)
    tall = P(None, "fsdp", None)
    return jax.shard_map(
        functools.partial(per_device, mesh.shape["fsdp"]),
        mesh=mesh,
        in_specs=(batch, P(), P(), wide, wide, tall, tall, P(), P(), P(), P(), P(("dp", "fsdp")), batch, batch),
        out_specs=(batch, batch, P(), P(), wide, wide, tall, tall, P(), P(), P(), P(), P()),
        check_vma=False,
    )
```

```python
import functools

import jax
import jax.numpy as jnp
from jax import lax
from jax.experimental import pallas as pl
from jax.experimental.pallas import tpu as pltpu
from jax.sharding import PartitionSpec as P

HEADS = 8
EPSILON = 1e-05
NEG_FILL = -1000000000.0
BF = jnp.bfloat16
F32 = jnp.float32

COL_IN = (0, 384)
COL_OUT = (768, 896)
COL_FEED = 1024
COL_DOWN = 2048
COLS = 2560
SHARDS = 16
STEP_BITS = (2, 3, 0, 1)


def dot_nn(a, b):
    return lax.dot_general(a, b, (((1,), (0,)), ((), ())), preferred_element_type=F32)


def dot_nt(a, b):
    return lax.dot_general(a, b, (((1,), (1,)), ((), ())), preferred_element_type=F32)


def norm_cols(x):
    centered = x - jnp.mean(x, axis=0, keepdims=True)
    inv = lax.rsqrt(jnp.mean(centered * centered, axis=0, keepdims=True) + EPSILON)
    return centered * inv, inv


def norm_cols_back(dn, gain, xhat, inv):
    e = dn * gain
    m1 = jnp.mean(e, axis=0, keepdims=True)
    m2 = jnp.mean(e * xhat, axis=0, keepdims=True)
    return inv * (e - m1 - xhat * m2)


def fold(part):
    return part[:, :128] + part[:, 128:]


def pack_kernel(attn_in_ref, attn_out_ref, feed_in_ref, feed_out_ref, out_ref):
    l = lax.axis_index("dp")
    down = feed_out_ref[l].astype(F32)
    parts = [attn_in_ref[l, 0], attn_in_ref[l, 1], attn_out_ref[l, 0], attn_out_ref[l, 1], feed_in_ref[l]]
    parts = [part.astype(F32) for part in parts] + [down[8 * a : 8 * a + 8] for a in range(4)]
    out_ref[0] = jnp.concatenate(parts, axis=1).astype(BF)


def tower_kernel(
    split,
    ids_ref, counts_ref, wmine0_ref, wmine1_ref, wmine2_ref, wmine3_ref, wother0_ref, wother1_ref, wother2_ref, wother3_ref,
    tok_ref, gains_ref, scales_ref, patches_ref, prompts_ref, cls_ref, cot_ref, adj_ref,
    out_ref, pgrad_ref, bigmine_ref, bigother_ref, smallmine_ref, smallother_ref,
    stage_ref, w_ref, wd_ref, wt_ref, wdt_ref, colb_ref, tokscr_ref, h_ref, g_ref, xh_ref, inv_ref,
    qkvt_ref, pb_ref, ot_ref, qkvv_ref, pv_ref, ov_ref, pw_ref, qbd_ref, dob_ref, hid_ref, du_ref, dqkv_ref,
    dov_ref, ga_ref, gf_ref, gd_ref, gt_ref, gacc_ref, gbig_ref, pacc_ref,
):
    dp = lax.axis_index("dp") if split else 0
    me = lax.axis_index("fsdp") if split else 0
    layers = 2
    chunks = 4
    items = 2

    for rel in range(SHARDS):
        rows = pl.ds(pl.multiple_of(8 * (me ^ rel), 8), 8)
        mine_ref = (wmine0_ref, wmine1_ref, wmine2_ref, wmine3_ref)[rel % 4]
        other_ref = (wother0_ref, wother1_ref, wother2_ref, wother3_ref)[rel % 4]
        stage_ref[dp, rows, :] = mine_ref[rel // 4].astype(F32)
        stage_ref[1 - dp, rows, :] = other_ref[rel // 4].astype(F32)
    for l in range(layers):
        for pair in range(SHARDS // 2):
            lo = stage_ref[l, 16 * pair : 16 * pair + 8, :]
            hi = stage_ref[l, 16 * pair + 8 : 16 * pair + 16, :]
            w_ref[l, 16 * pair : 16 * pair + 16, :] = jnp.concatenate([lo[:, :COL_DOWN], hi[:, :COL_DOWN]], axis=0).astype(BF)
            for half, part in enumerate((lo, hi)):
                base = 64 * pair + 32 * half
                wd_ref[l, base : base + 32, :] = jnp.concatenate(
                    [part[:, COL_DOWN + 128 * a : COL_DOWN + 128 * a + 128] for a in range(4)], axis=0
                ).astype(BF)
        for block in range(COL_DOWN // 128):
            wt_ref[l, 128 * block : 128 * block + 128, :] = w_ref[l, :, 128 * block : 128 * block + 128].T
        for block in range(4):
            wdt_ref[l, :, 128 * block : 128 * block + 128] = wd_ref[l, 128 * block : 128 * block + 128, :].T
        for k in range(4):
            for offset, rows in ((0, gains_ref), (4, scales_ref)):
                col = jnp.broadcast_to(rows[l, k : k + 1, :], (128, 128)).T
                colb_ref[l * 8 + offset + k, :, 0:128] = col
                colb_ref[l * 8 + offset + k, :, 128:256] = col

    for b in range(items):
        ident = ids_ref[b]
        for v in range(4):
            bv = 4 * b + v
            tokscr_ref[bv, 0:10, :] = prompts_ref[ident].astype(F32)
            tokscr_ref[bv, 10:127, :] = patches_ref[b, v].astype(F32)
            tokscr_ref[bv, 127:128, :] = cls_ref[...].astype(F32)
            lanes = slice(128 * (v % 2), 128 * (v % 2) + 128)
            h_ref[2 * b + v // 2, :, lanes] = tokscr_ref[bv].T
            g_ref[0, 2 * b + v // 2, :, lanes] = cot_ref[b, v].astype(F32).T
            g_ref[1, 2 * b + v // 2, :, lanes] = adj_ref[b, v].astype(F32).T

    head_row = lax.broadcasted_iota(jnp.int32, (8, 128), 0)
    head_col = lax.broadcasted_iota(jnp.int32, (8, 128), 1) // 16
    gather_heads = jnp.where(head_row == head_col, 1.0, 0.0).astype(BF)
    spread_row = lax.broadcasted_iota(jnp.int32, (128, 8), 0) // 16
    spread_col = lax.broadcasted_iota(jnp.int32, (128, 8), 1)
    spread_heads = jnp.where(spread_row == spread_col, 1.0, 0.0).astype(BF)

    def head_sums(left, rights):
        return dot_nn(gather_heads, jnp.concatenate([(left * right).astype(BF) for right in rights], axis=1))

    def diag_heads(target_ref, at, rows):
        for head in range(HEADS):
            target_ref[at, 16 * head : 16 * head + 16, 128 * head : 128 * head + 128] = rows[16 * head : 16 * head + 16]

    qbd_ref[...] = jnp.zeros_like(qbd_ref)
    dob_ref[...] = jnp.zeros_like(dob_ref)

    def gain(l, k):
        return colb_ref[l * 8 + k]

    def scale(l, k):
        return colb_ref[l * 8 + 4 + k]

    def keep_norm(l, k, c, x):
        xhat, inv = norm_cols(x)
        xh_ref[l * 4 + k, c] = xhat
        inv_ref[l * 4 + k, c] = inv
        return (xhat * gain(l, k)).astype(BF)

    def time_forward(l, c):
        x = h_ref[c]
        n = keep_norm(l, 0, c, x)
        qkv = dot_nn(wt_ref[l, 0:384, :], n)
        queries = (qkv[:128] * 0.25).astype(BF)
        keys = qkv[128:256].astype(BF)
        values = qkv[256:].astype(BF)
        qkvt_ref[l, c, 0:128, :] = queries
        qkvt_ref[l, c, 128:256, :] = keys
        qkvt_ref[l, c, 256:384, :] = values
        for s in range(2):
            lanes = slice(128 * s, 128 * s + 128)
            at = 2 * (c % 2) + s
            diag_heads(qbd_ref, at, queries[:, lanes])
            key_rows = keys[:, lanes].T
            for hp in range(4):
                span = slice(256 * hp, 256 * hp + 256)
                rows = slice(32 * hp, 32 * hp + 32)
                scores = dot_nn(key_rows, qbd_ref[at, :, span])
                shifted = jnp.exp(scores - jnp.max(scores, axis=0, keepdims=True))
                prob = (shifted * (1.0 / jnp.sum(shifted, axis=0, keepdims=True))).astype(BF)
                pb_ref[l, 2 * c + s, :, span] = prob
                mixed = dot_nn(values[rows, lanes], prob)
                ot_ref[l, c, 32 * hp : 32 * hp + 16, lanes] = mixed[:16, :128].astype(BF)
                ot_ref[l, c, 32 * hp + 16 : 32 * hp + 32, lanes] = mixed[16:, 128:].astype(BF)
        branch = dot_nn(wt_ref[l, COL_OUT[0] : COL_OUT[0] + 128, :], ot_ref[l, c])
        h_ref[c] = x + scale(l, 0) * branch

    def var_forward(l, b):
        for cc in range(2):
            c = 2 * b + cc
            n = keep_norm(l, 1, c, h_ref[c])
            qkv = dot_nn(wt_ref[l, COL_IN[1] : COL_IN[1] + 384, :], n)
            qkvv_ref[l, c, 0:128, :] = (qkv[:128] * 0.25).astype(BF)
            qkvv_ref[l, c, 128:384, :] = qkv[128:].astype(BF)
        count = counts_ref[ids_ref[b]]

        def slot(first, i):
            lanes = slice(128 * (i % 2), 128 * (i % 2) + 128)
            return qkvv_ref[l, 2 * b + i // 2, first : first + 128, lanes].astype(F32)

        key_slots = [slot(128, j) for j in range(4)]
        value_slots = [slot(256, j) for j in range(4)]
        for i in range(4):
            scores = head_sums(slot(0, i), key_slots)
            parts = [scores[:, 128 * j : 128 * j + 128] for j in range(4)]
            parts = [jnp.where(jnp.full((8, 128), count, jnp.int32) > j, parts[j], NEG_FILL) for j in range(4)]
            top = jnp.maximum(jnp.maximum(parts[0], parts[1]), jnp.maximum(parts[2], parts[3]))
            shifted = [jnp.exp(part - top) for part in parts]
            total = 1.0 / ((shifted[0] + shifted[1]) + (shifted[2] + shifted[3]))
            prob = jnp.concatenate([part * total for part in shifted], axis=1)
            pv_ref[l, b, i] = prob
            spread = dot_nn(spread_heads, prob.astype(BF))
            pw_ref[l, b, i] = spread.astype(BF)
            mixed = spread[:, :128] * value_slots[0]
            for j in range(1, 4):
                mixed = mixed + spread[:, 128 * j : 128 * j + 128] * value_slots[j]
            lanes = slice(128 * (i % 2), 128 * (i % 2) + 128)
            ov_ref[l, 2 * b + i // 2, :, lanes] = mixed.astype(BF)
        for cc in range(2):
            c = 2 * b + cc
            branch = dot_nn(wt_ref[l, COL_OUT[1] : COL_OUT[1] + 128, :], ov_ref[l, c])
            h_ref[c] = h_ref[c] + scale(l, 1) * branch

    def tail_forward(l, c):
        x = h_ref[c]
        n = keep_norm(l, 2, c, x)
        mix = [dot_nt(n[:, 128 * s : 128 * s + 128], tok_ref[l]) for s in range(2)]
        x = x + scale(l, 2) * jnp.concatenate(mix, axis=1)
        n = keep_norm(l, 3, c, x)
        for z in range(4):
            gate = dot_nn(wt_ref[l, COL_FEED + 128 * z : COL_FEED + 128 * z + 128, :], n)
            up = dot_nn(wt_ref[l, COL_FEED + 512 + 128 * z : COL_FEED + 640 + 128 * z, :], n)
            sig = 0.5 * jnp.tanh(0.5 * gate) + 0.5
            hid_ref[c % 2, 128 * z : 128 * z + 128, :] = (gate * sig * up).astype(BF)
        h_ref[c] = x + scale(l, 3) * dot_nn(wdt_ref[l], hid_ref[c % 2])

    def norm_of(l, k, c):
        xhat = xh_ref[l * 4 + k, c]
        return xhat, inv_ref[l * 4 + k, c], (xhat * gain(l, k)).astype(BF)

    def pass_on(l, k, c, x, dn, xhat, inv):
        if x == 0:
            gacc_ref[l * 4 + k] += fold(dn * xhat)
        g_ref[x, c] += norm_cols_back(dn, gain(l, k), xhat, inv)

    def feed_backward(l, c):
        xhat, inv, n = norm_of(l, 3, c)
        dz = [(scale(l, 3) * g_ref[x, c]).astype(BF) for x in range(2)]
        for z in range(4):
            rows = slice(128 * z, 128 * z + 128)
            gate = dot_nn(wt_ref[l, COL_FEED + 128 * z : COL_FEED + 128 * z + 128, :], n)
            up = dot_nn(wt_ref[l, COL_FEED + 512 + 128 * z : COL_FEED + 640 + 128 * z, :], n)
            sig = 0.5 * jnp.tanh(0.5 * gate) + 0.5
            act = gate * sig
            hid_ref[c % 2, rows, :] = (act * up).astype(BF)
            slope = up * (sig * (1.0 + gate * (1.0 - sig)))
            for x in range(2):
                dhid = dot_nn(wd_ref[l, rows, :], dz[x])
                du_ref[2 * (c % 2) + x, 128 * z : 128 * z + 128, :] = (dhid * slope).astype(BF)
                du_ref[2 * (c % 2) + x, 512 + 128 * z : 640 + 128 * z, :] = (dhid * act).astype(BF)
        gf_ref[...] += dot_nt(du_ref[2 * (c % 2)], n)
        gd_ref[...] += dot_nt(hid_ref[c % 2], dz[0])
        for x in range(2):
            dn = dot_nn(w_ref[l, :, COL_FEED:COL_DOWN], du_ref[2 * (c % 2) + x])
            pass_on(l, 3, c, x, dn, xhat, inv)

    def token_backward(l, c):
        xhat, inv, n = norm_of(l, 2, c)
        for x in range(2):
            dy = (scale(l, 2) * g_ref[x, c]).astype(BF)
            dn = []
            for s in range(2):
                part = dy[:, 128 * s : 128 * s + 128]
                dn.append(dot_nn(part, tok_ref[l]))
                if x == 0:
                    gt_ref[l] += dot_nn(part.T, n[:, 128 * s : 128 * s + 128])
            pass_on(l, 2, c, x, jnp.concatenate(dn, axis=1), xhat, inv)

    def var_backward(l, b):
        def slot(first, i):
            lanes = slice(128 * (i % 2), 128 * (i % 2) + 128)
            return qkvv_ref[l, 2 * b + i // 2, first : first + 128, lanes].astype(F32)

        for x in range(2):
            for cc in range(2):
                c = 2 * b + cc
                dt = (scale(l, 1) * g_ref[x, c]).astype(BF)
                dov_ref[4 * b + 2 * x + cc] = dot_nn(w_ref[l, :, COL_OUT[1] : COL_OUT[1] + 128], dt).astype(BF)
                if x == 0:
                    ga_ref[:, COL_OUT[1] : COL_OUT[1] + 128] += dot_nt(ov_ref[l, c], dt)
            value_slots = [slot(256, j) for j in range(4)]
            dkeys = [0.0] * 4
            dvalues = [0.0] * 4
            for i in range(4):
                lanes = slice(128 * (i % 2), 128 * (i % 2) + 128)
                grad = dov_ref[4 * b + 2 * x + i // 2, :, lanes].astype(F32)
                query = slot(0, i)
                prob = pv_ref[l, b, i]
                weighted = prob * head_sums(grad, value_slots)
                total = (weighted[:, :128] + weighted[:, 128:256]) + (weighted[:, 256:384] + weighted[:, 384:])
                ds = weighted - prob * jnp.concatenate([total] * 4, axis=1)
                ds_wide = dot_nn(spread_heads, ds.astype(BF))
                ds_slots = [ds_wide[:, 128 * j : 128 * j + 128] for j in range(4)]
                terms = [ds_slots[j] * slot(128, j) for j in range(4)]
                dquery = (terms[0] + terms[1]) + (terms[2] + terms[3])
                for j in range(4):
                    dkeys[j] = dkeys[j] + ds_slots[j] * query
                    dvalues[j] = dvalues[j] + pw_ref[l, b, i, :, 128 * j : 128 * j + 128].astype(F32) * grad
                dqkv_ref[4 * b + 2 * x + i // 2, 0:128, lanes] = (dquery * 0.25).astype(BF)
            for j in range(4):
                lanes = slice(128 * (j % 2), 128 * (j % 2) + 128)
                dqkv_ref[4 * b + 2 * x + j // 2, 128:256, lanes] = dkeys[j].astype(BF)
                dqkv_ref[4 * b + 2 * x + j // 2, 256:384, lanes] = dvalues[j].astype(BF)
            for cc in range(2):
                c = 2 * b + cc
                xhat, inv, n = norm_of(l, 1, c)
                dqkv = dqkv_ref[4 * b + 2 * x + cc]
                if x == 0:
                    ga_ref[:, COL_IN[1] : COL_IN[1] + 384] += dot_nt(n, dqkv)
                pass_on(l, 1, c, x, dot_nn(w_ref[l, :, COL_IN[1] : COL_IN[1] + 384], dqkv), xhat, inv)

    def time_backward(l, c):
        xhat, inv, n = norm_of(l, 0, c)
        queries = qkvt_ref[l, c, 0:128, :]
        keys = qkvt_ref[l, c, 128:256, :]
        values = qkvt_ref[l, c, 256:384, :]
        grads = []
        for x in range(2):
            dt = (scale(l, 0) * g_ref[x, c]).astype(BF)
            grads.append(dot_nn(w_ref[l, :, COL_OUT[0] : COL_OUT[0] + 128], dt).astype(BF))
            if x == 0:
                ga_ref[:, COL_OUT[0] : COL_OUT[0] + 128] += dot_nt(ot_ref[l, c], dt)
        for s in range(2):
            lanes = slice(128 * s, 128 * s + 128)
            at = 2 * (c % 2) + s
            diag_heads(qbd_ref, at, queries[:, lanes])
            value_rows = values[:, lanes].T
            for x in range(2):
                diag_heads(dob_ref, 2 * at + x, grads[x][:, lanes])
            for hp in range(4):
                span = slice(256 * hp, 256 * hp + 256)
                rows = slice(32 * hp, 32 * hp + 32)
                prob_bf = pb_ref[l, 2 * c + s, :, span]
                prob = prob_bf.astype(F32)
                for x in range(2):
                    weighted = prob * dot_nn(value_rows, dob_ref[2 * at + x, :, span])
                    ds = (weighted - prob * jnp.sum(weighted, axis=0, keepdims=True)).astype(BF)
                    dvalue = dot_nt(dob_ref[2 * at + x, rows, span], prob_bf)
                    dquery = dot_nn(keys[rows, lanes], ds) * 0.25
                    dkey = dot_nt(qbd_ref[at, rows, span], ds)
                    dqkv_ref[2 * c + x, 32 * hp : 32 * hp + 16, lanes] = dquery[:16, :128].astype(BF)
                    dqkv_ref[2 * c + x, 32 * hp + 16 : 32 * hp + 32, lanes] = dquery[16:, 128:].astype(BF)
                    dqkv_ref[2 * c + x, 128 + 32 * hp : 160 + 32 * hp, lanes] = dkey.astype(BF)
                    dqkv_ref[2 * c + x, 256 + 32 * hp : 288 + 32 * hp, lanes] = dvalue.astype(BF)
        ga_ref[:, COL_IN[0] : COL_IN[0] + 384] += dot_nt(n, dqkv_ref[2 * c])
        for x in range(2):
            pass_on(l, 0, c, x, dot_nn(w_ref[l, :, COL_IN[0] : COL_IN[0] + 384], dqkv_ref[2 * c + x]), xhat, inv)

    def each(count, stage, l):
        for i in range(count):
            stage(l, i)

    def forward_layer(l, carry):
        each(chunks, time_forward, l)
        each(items, var_forward, l)
        each(chunks, tail_forward, l)
        return carry

    lax.fori_loop(0, layers, forward_layer, 0)
    for b in range(items):
        for v in range(4):
            lanes = slice(128 * (v % 2), 128 * (v % 2) + 128)
            out_ref[b, v] = h_ref[2 * b + v // 2, :, lanes].T.astype(BF)

    gacc_ref[...] = jnp.zeros_like(gacc_ref)
    gt_ref[...] = jnp.zeros_like(gt_ref)
    pacc_ref[...] = jnp.zeros_like(pacc_ref)

    def backward_layer(step, carry):
        l = layers - 1 - step
        ga_ref[...] = jnp.zeros_like(ga_ref)
        gd_ref[...] = jnp.zeros_like(gd_ref)
        gf_ref[...] = jnp.zeros_like(gf_ref)
        each(chunks, feed_backward, l)
        each(chunks, token_backward, l)
        each(items, var_backward, l)
        each(chunks, time_backward, l)
        for k in range(8):
            turned = gf_ref[128 * k : 128 * k + 128, :].T
            for f in range(SHARDS):
                gbig_ref[l, f, :, COL_FEED + 128 * k : COL_FEED + 128 * k + 128] = turned[8 * f : 8 * f + 8].astype(BF)
        for f in range(SHARDS):
            gbig_ref[l, f, :, 0:COL_FEED] = ga_ref[8 * f : 8 * f + 8, :].astype(BF)
            down = jnp.concatenate([gd_ref[32 * f + 8 * a : 32 * f + 8 * a + 8, :] for a in range(4)], axis=1)
            gbig_ref[l, f, :, COL_DOWN:COLS] = down.astype(BF)
        gains_rows = [jnp.sum(gacc_ref[l * 4 + k].T, axis=0, keepdims=True) for k in range(4)]
        sums = [
            jnp.sum(w_ref[l, :, COL_OUT[k] : COL_OUT[k] + 128].astype(F32) * ga_ref[:, COL_OUT[k] : COL_OUT[k] + 128], axis=0, keepdims=True)
            for k in range(2)
        ]
        sums.append(gains_ref[l, 2:3, :] * gains_rows[2])
        sums.append(jnp.sum(wd_ref[l].astype(F32) * gd_ref[...], axis=0, keepdims=True))
        for k in range(4):
            pacc_ref[0, l * 4 + k, 10:11, :] = gains_rows[k]
            pacc_ref[0, l * 4 + k, 11:12, :] = sums[k] / scales_ref[l, k : k + 1, :]
        return carry

    lax.fori_loop(0, layers, backward_layer, 0)

    for x in range(2):
        cls_sum = None
        for b in range(items):
            prompt_sum = None
            for v in range(4):
                lanes = slice(128 * (v % 2), 128 * (v % 2) + 128)
                tokscr_ref[4 * b + v] = g_ref[x, 2 * b + v // 2, :, lanes].T
                head = tokscr_ref[4 * b + v, 0:10, :]
                last = tokscr_ref[4 * b + v, 127:128, :]
                prompt_sum = head if prompt_sum is None else prompt_sum + head
                cls_sum = last if cls_sum is None else cls_sum + last
                if x == 0:
                    pgrad_ref[b, v] = tokscr_ref[4 * b + v, 10:127, :]
            pacc_ref[x, ids_ref[b], 0:10, :] += prompt_sum
        pacc_ref[x, 0, 12:13, :] = cls_sum

    for big_ref, small_ref, c in ((bigmine_ref, smallmine_ref, dp), (bigother_ref, smallother_ref, 1 - dp)):
        for rel in range(SHARDS):
            big_ref[rel % 4, rel // 4] = gbig_ref[c, me ^ rel]
        for block in range(16):
            if block < 8:
                pair = gt_ref[c, 16 * block : 16 * block + 16, :]
            else:
                pair = pacc_ref[block // 4 - 2, 4 * c + block % 4]
            lanes = slice(256 * (block % 4), 256 * (block % 4) + 256)
            small_ref[block // 4, :, lanes] = jnp.concatenate([pair[:8], pair[8:]], axis=1)


def call(kernel, name, out_shape, in_spaces, scratch, *operands, cost=None):
    spaces = {"v": pltpu.VMEM, "s": pltpu.SMEM}
    return pl.pallas_call(
        kernel,
        out_shape=out_shape,
        in_specs=[pl.BlockSpec(memory_space=spaces[space]) for space in in_spaces],
        out_specs=[pl.BlockSpec(memory_space=pltpu.VMEM)] * len(out_shape),
        scratch_shapes=scratch,
        compiler_params=pltpu.CompilerParams(vmem_limit_bytes=58 * 1024 * 1024),
        cost_estimate=cost,
        name=name,
    )(*operands)


def shape_of(shape, kind=F32):
    return jax.ShapeDtypeStruct(shape, kind)


def run_tower(split, *operands):
    half = [shape_of((4, 4, 8, COLS), BF)] * 2 + [shape_of((4, 8, 1024))] * 2
    return call(
        functools.partial(tower_kernel, split),
        "tower",
        [shape_of((2, 4, 128, 128), BF), shape_of((2, 4, 117, 128))] + half,
        "ss" + "v" * 16,
        [
            pltpu.VMEM((2, 128, COLS), F32),
            pltpu.VMEM((2, 128, COL_DOWN), BF),
            pltpu.VMEM((2, 512, 128), BF),
            pltpu.VMEM((2, COL_DOWN, 128), BF),
            pltpu.VMEM((2, 128, 512), BF),
            pltpu.VMEM((16, 128, 256), F32),
            pltpu.VMEM((8, 128, 128), F32),
            pltpu.VMEM((4, 128, 256), F32),
            pltpu.VMEM((2, 4, 128, 256), F32),
            pltpu.VMEM((8, 4, 128, 256), F32),
            pltpu.VMEM((8, 4, 1, 256), F32),
            pltpu.VMEM((2, 4, 384, 256), BF),
            pltpu.VMEM((2, 8, 128, 1024), BF),
            pltpu.VMEM((2, 4, 128, 256), BF),
            pltpu.VMEM((2, 4, 384, 256), BF),
            pltpu.VMEM((2, 2, 4, 8, 512), F32),
            pltpu.VMEM((2, 4, 128, 256), BF),
            pltpu.VMEM((2, 2, 4, 128, 512), BF),
            pltpu.VMEM((4, 128, 1024), BF),
            pltpu.VMEM((8, 128, 1024), BF),
            pltpu.VMEM((2, 512, 256), BF),
            pltpu.VMEM((4, 1024, 256), BF),
            pltpu.VMEM((8, 384, 256), BF),
            pltpu.VMEM((8, 128, 256), BF),
            pltpu.VMEM((128, COL_FEED), F32),
            pltpu.VMEM((1024, 128), F32),
            pltpu.VMEM((512, 128), F32),
            pltpu.VMEM((2, 128, 128), F32),
            pltpu.VMEM((8, 128, 128), F32),
            pltpu.VMEM((2, SHARDS, 8, COLS), BF),
            pltpu.VMEM((2, 8, 16, 128), F32),
        ],
        *operands,
        cost=pl.CostEstimate(flops=10**10, bytes_accessed=20 * 10**6, transcendentals=0),
    )


def pack_rows(attn_in, attn_out, feed_in, feed_out):
    layers, _, rows, _ = attn_in.shape
    down = feed_out.reshape(layers, 4, rows, 128)
    return jnp.concatenate(
        [attn_in[:, 0], attn_in[:, 1], attn_out[:, 0], attn_out[:, 1], feed_in] + [down[:, a] for a in range(4)], axis=2
    )


def unpack_rows(packed):
    layers, rows, _ = packed.shape
    attn_in = jnp.stack([packed[:, :, at : at + 384] for at in COL_IN], axis=1)
    attn_out = jnp.stack([packed[:, :, at : at + 128] for at in COL_OUT], axis=1)
    feed_in = packed[:, :, COL_FEED:COL_DOWN]
    feed_out = jnp.stack([packed[:, :, COL_DOWN + 128 * a : COL_DOWN + 128 * a + 128] for a in range(4)], axis=1)
    return attn_in, attn_out, feed_in, feed_out.reshape(layers, 4 * rows, 128)


def flip(array, axis, bit, size):
    return lax.ppermute(array, axis, [(i, i ^ (1 << bit)) for i in range(size)])


def swap(array, mask):
    return lax.ppermute(array, "fsdp", [(i, i ^ mask) for i in range(SHARDS)])


def gather_rows(attn_in, attn_out, feed_in, feed_out):
    row = call(pack_kernel, "pack", [shape_of((1, 8, COLS), BF)], "vvvv", [], attn_in, attn_out, feed_in, feed_out)[0]
    column = jnp.concatenate([row] + [swap(row, 4 * z) for z in range(1, 4)], axis=0)
    mine = [column] + [swap(column, xy) for xy in range(1, 4)]
    return mine + [flip(part, "dp", 0, 2) for part in mine]


def final_kernel(big_mine, big_other, small_mine, small_other, attn_in, attn_out, feed_in, feed_out, tokens, gains, scales,
                 prompt, cls, adjust_prompt, adjust_cls):
    dp = lax.axis_index("dp")
    for part, l in ((big_mine, dp), (big_other, 1 - dp)):
        for k in range(2):
            attn_in[l, k] = part[:, COL_IN[k] : COL_IN[k] + 384]
            attn_out[l, k] = part[:, COL_OUT[k] : COL_OUT[k] + 128]
        feed_in[l] = part[:, COL_FEED:COL_DOWN]
        for a in range(4):
            feed_out[l, 8 * a : 8 * a + 8, :] = part[:, COL_DOWN + 128 * a : COL_DOWN + 128 * a + 128]
    for c in range(2):
        parts = [slice(256 * k, 256 * k + 256) for k in range(16)]
        tiles = [jnp.where(dp == c, small_mine[:, part], small_other[:, part]) for part in parts]
        blocks = [jnp.concatenate([tile[:, :128], tile[:, 128:]], axis=0) for tile in tiles]
        for k in range(8):
            tokens[c, 16 * k : 16 * k + 16, :] = blocks[k]
        for k in range(4):
            for row in range(10):
                prompt[row, 4 * c + k : 4 * c + k + 1, :] = blocks[8 + k][row : row + 1]
                adjust_prompt[row, 4 * c + k : 4 * c + k + 1, :] = blocks[12 + k][row : row + 1]
            gains[c, k : k + 1, :] = blocks[8 + k][10:11]
            scales[c, k : k + 1, :] = blocks[8 + k][11:12]
        if c == 0:
            cls[...] = blocks[8][12:13]
            adjust_cls[...] = blocks[12][12:13]


def four(first, rest):
    return (first.astype(F32) + rest[0].astype(F32)) + (rest[1].astype(F32) + rest[2].astype(F32))


def reduce_all(big_mine, big_other, small_mine, small_other):
    big = (big_mine.astype(F32) + flip(big_other, "dp", 0, 2).astype(F32)).astype(BF)
    small = (small_mine + flip(small_other, "dp", 0, 2)).astype(BF)
    got = [swap(jnp.concatenate([big[xy], small], axis=2), xy) for xy in range(1, 4)]
    big = four(big[0], [part[:, :, :COLS] for part in got]).astype(BF)
    small = four(small, [part[:, :, COLS:] for part in got]).astype(BF)
    small = jnp.concatenate([small[at] for at in range(4)], axis=1)
    got = [swap(jnp.concatenate([big[z], small], axis=1), 4 * z) for z in range(1, 4)]
    big = four(big[0], [part[:, :COLS] for part in got])
    small = four(small, [part[:, COLS:] for part in got])
    return call(
        final_kernel, "final",
        [shape_of((2, 2, 8, 384)), shape_of((2, 2, 8, 128)), shape_of((2, 8, 1024)), shape_of((2, 32, 128)), shape_of((2, 128, 128)),
         shape_of((2, 4, 128)), shape_of((2, 4, 128)), shape_of((10, 8, 128)), shape_of((1, 128)), shape_of((10, 8, 128)), shape_of((1, 128))],
        "vvvv", [], big, flip(big, "dp", 0, 2), small, flip(small, "dp", 0, 2),
    )


def per_device(shard_count, patches, prompts, cls_token, attn_in, attn_out, feed_in, feed_out, token_operator,
               norm_gains, branch_scales, var_counts, dataset_ids, cotangent, adjust_cotangent):
    fast = shard_count == SHARDS
    if fast:
        gathered = gather_rows(attn_in, attn_out, feed_in, feed_out)
    else:
        whole_down = lax.all_gather(feed_out, "fsdp", axis=1, tiled=True)
        whole_down = whole_down.reshape(2, SHARDS, 4, 8, 128).transpose(0, 2, 1, 3, 4).reshape(2, 512, 128)
        rows = pack_rows(
            lax.all_gather(attn_in, "fsdp", axis=2, tiled=True),
            lax.all_gather(attn_out, "fsdp", axis=2, tiled=True),
            lax.all_gather(feed_in, "fsdp", axis=1, tiled=True),
            whole_down,
        )
        rows = rows.reshape(2, SHARDS, 8, COLS).transpose(1, 0, 2, 3)
        gathered = [rows[:, l].reshape(4, 4, 8, COLS)[:, xy] for l in range(2) for xy in range(4)]
    output, patch_grad, *sums = run_tower(
        fast, dataset_ids, var_counts, *gathered, token_operator, norm_gains, branch_scales, patches, prompts,
        cls_token.reshape(1, -1), cotangent, adjust_cotangent,
    )
    if fast:
        (attn_in_g, attn_out_g, feed_in_g, feed_out_g, token_g, gains_g, scales_g, prompt_g, cls_g, adjust_prompt_g,
         adjust_cls_g) = reduce_all(*sums)
        return (output, patch_grad, prompt_g.transpose(1, 0, 2), cls_g[0], attn_in_g, attn_out_g, feed_in_g, feed_out_g, token_g, gains_g,
                scales_g, adjust_prompt_g.transpose(1, 0, 2), adjust_cls_g[0])
    rows = jnp.stack(sums[:2]).transpose(0, 2, 1, 3, 4).astype(F32).reshape(2, 128, COLS)
    attn_in_g, attn_out_g, feed_in_g, feed_out_g = unpack_rows(rows)
    feed_out_g = feed_out_g.reshape(2, 4, SHARDS, 8, 128).transpose(0, 2, 1, 3, 4).reshape(2, 512, 128)
    matrices = (
        lax.psum_scatter(lax.psum(attn_in_g, "dp"), "fsdp", scatter_dimension=2, tiled=True),
        lax.psum_scatter(lax.psum(attn_out_g, "dp"), "fsdp", scatter_dimension=2, tiled=True),
        lax.psum_scatter(lax.psum(feed_in_g, "dp"), "fsdp", scatter_dimension=1, tiled=True),
        lax.psum_scatter(lax.psum(feed_out_g, "dp"), "fsdp", scatter_dimension=1, tiled=True),
    )
    small = lax.psum(jnp.stack(sums[2:]), ("dp", "fsdp"))
    small = small.reshape(2, 4, 8, 4, 2, 128).transpose(0, 1, 3, 4, 2, 5).reshape(2, 16, 16, 128)
    main, adjust = small[:, 8:12].reshape(8, 16, 128), small[:, 12:].reshape(8, 16, 128)
    return (output, patch_grad, main[:, :10], main[0, 12], *matrices, small[:, :8].reshape(2, 128, 128),
            main[:, 10].reshape(2, 4, 128), main[:, 11].reshape(2, 4, 128), adjust[:, :10], adjust[0, 12])


def solution(mesh):
    batch = P(("dp", "fsdp"), None, None, None)
    wide = P(None, None, "fsdp", None)
    tall = P(None, "fsdp", None)
    return jax.shard_map(
        functools.partial(per_device, mesh.shape["fsdp"]),
        mesh=mesh,
        in_specs=(batch, P(), P(), wide, wide, tall, tall, P(), P(), P(), P(), P(("dp", "fsdp")), batch, batch),
        out_specs=(batch, batch, P(), P(), wide, wide, tall, tall, P(), P(), P(), P(), P()),
        check_vma=False,
    )
```

```python
import functools

import jax
import jax.numpy as jnp
from jax import lax
from jax.experimental import pallas as pl
from jax.experimental.pallas import tpu as pltpu
from jax.sharding import PartitionSpec as P

HEADS = 8
EPSILON = 1e-05
NEG_FILL = -1000000000.0
BF = jnp.bfloat16
F32 = jnp.float32

COL_IN = (0, 384)
COL_OUT = (768, 896)
COL_FEED = 1024
COL_DOWN = 2048
COLS = 2560
SHARDS = 16
STEP_BITS = (2, 3, 0, 1)


def dot_nn(a, b):
    return lax.dot_general(a, b, (((1,), (0,)), ((), ())), preferred_element_type=F32)


def dot_nt(a, b):
    return lax.dot_general(a, b, (((1,), (1,)), ((), ())), preferred_element_type=F32)


def turn(eye, x):
    return dot_nt(eye, x)


def norm_cols(x):
    centered = x - jnp.mean(x, axis=0, keepdims=True)
    inv = lax.rsqrt(jnp.mean(centered * centered, axis=0, keepdims=True) + EPSILON)
    return centered * inv, inv


def norm_cols_back(dn, gain, xhat, inv):
    e = dn * gain
    both = e * xhat
    m1 = jnp.mean(e, axis=0, keepdims=True)
    m2 = jnp.mean(both, axis=0, keepdims=True)
    return inv * (e - m1 - xhat * m2), both


def fold(part):
    return part[:, :128] + part[:, 128:]


def pack_kernel(attn_in_ref, attn_out_ref, feed_in_ref, feed_out_ref, out_ref):
    l = lax.axis_index("dp")
    down = feed_out_ref[l].astype(F32)
    parts = [attn_in_ref[l, 0], attn_in_ref[l, 1], attn_out_ref[l, 0], attn_out_ref[l, 1], feed_in_ref[l]]
    parts = [part.astype(F32) for part in parts] + [down[8 * a : 8 * a + 8] for a in range(4)]
    out_ref[0] = jnp.concatenate(parts, axis=1).astype(BF)


def tower_kernel(
    split,
    ids_ref, counts_ref, wmine0_ref, wmine1_ref, wmine2_ref, wmine3_ref, wother0_ref, wother1_ref, wother2_ref, wother3_ref,
    tok_ref, gains_ref, scales_ref, patches_ref, prompts_ref, cls_ref, cot_ref, adj_ref,
    out_ref, pgrad_ref, bigmine_ref, bigother_ref, smallmine_ref, smallother_ref,
    stage_ref, w_ref, wd_ref, wt_ref, wdt_ref, colb_ref, tokscr_ref, h_ref, g_ref, xh_ref, inv_ref,
    qkvt_ref, pb_ref, ot_ref, qkvv_ref, pv_ref, ov_ref, pw_ref, qbd_ref, dob_ref, hid_ref, du_ref, dqkv_ref,
    dov_ref, ga_ref, gf_ref, gd_ref, gt_ref, gacc_ref, gbig_ref, pacc_ref,
):
    dp = lax.axis_index("dp") if split else 0
    eye_row = lax.broadcasted_iota(jnp.int32, (128, 128), 0)
    eye = jnp.where(eye_row == lax.broadcasted_iota(jnp.int32, (128, 128), 1), 1.0, 0.0).astype(BF)
    me = lax.axis_index("fsdp") if split else 0
    layers = 2
    chunks = 4
    items = 2

    for rel in range(SHARDS):
        rows = pl.ds(pl.multiple_of(8 * (me ^ rel), 8), 8)
        mine_ref = (wmine0_ref, wmine1_ref, wmine2_ref, wmine3_ref)[rel % 4]
        other_ref = (wother0_ref, wother1_ref, wother2_ref, wother3_ref)[rel % 4]
        stage_ref[dp, rows, :] = mine_ref[rel // 4].astype(F32)
        stage_ref[1 - dp, rows, :] = other_ref[rel // 4].astype(F32)
    for l in range(layers):
        for pair in range(SHARDS // 2):
            lo = stage_ref[l, 16 * pair : 16 * pair + 8, :]
            hi = stage_ref[l, 16 * pair + 8 : 16 * pair + 16, :]
            w_ref[l, 16 * pair : 16 * pair + 16, :] = jnp.concatenate([lo[:, :COL_DOWN], hi[:, :COL_DOWN]], axis=0).astype(BF)
            for half, part in enumerate((lo, hi)):
                base = 64 * pair + 32 * half
                wd_ref[l, base : base + 32, :] = jnp.concatenate(
                    [part[:, COL_DOWN + 128 * a : COL_DOWN + 128 * a + 128] for a in range(4)], axis=0
                ).astype(BF)
        for block in range(COL_DOWN // 128):
            wt_ref[l, 128 * block : 128 * block + 128, :] = turn(eye, w_ref[l, :, 128 * block : 128 * block + 128]).astype(BF)
        for block in range(4):
            wdt_ref[l, :, 128 * block : 128 * block + 128] = turn(eye, wd_ref[l, 128 * block : 128 * block + 128, :]).astype(BF)
        for k in range(4):
            for offset, rows in ((0, gains_ref), (4, scales_ref)):
                col = jnp.broadcast_to(rows[l, k : k + 1, :], (128, 128)).T
                colb_ref[l * 8 + offset + k, :, 0:128] = col
                colb_ref[l * 8 + offset + k, :, 128:256] = col

    for b in range(items):
        ident = ids_ref[b]
        for v in range(4):
            bv = 4 * b + v
            tokscr_ref[bv, 0:10, :] = prompts_ref[ident].astype(F32)
            tokscr_ref[bv, 10:127, :] = patches_ref[b, v].astype(F32)
            tokscr_ref[bv, 127:128, :] = cls_ref[...].astype(F32)
            lanes = slice(128 * (v % 2), 128 * (v % 2) + 128)
            h_ref[2 * b + v // 2, :, lanes] = turn(eye, tokscr_ref[bv].astype(BF))
            g_ref[0, 2 * b + v // 2, :, lanes] = turn(eye, cot_ref[b, v])
            g_ref[1, 2 * b + v // 2, :, lanes] = turn(eye, adj_ref[b, v])

    head_row = lax.broadcasted_iota(jnp.int32, (8, 128), 0)
    head_col = lax.broadcasted_iota(jnp.int32, (8, 128), 1) // 16
    gather_heads = jnp.where(head_row == head_col, 1.0, 0.0).astype(BF)
    spread_row = lax.broadcasted_iota(jnp.int32, (128, 8), 0) // 16
    spread_col = lax.broadcasted_iota(jnp.int32, (128, 8), 1)
    spread_heads = jnp.where(spread_row == spread_col, 1.0, 0.0).astype(BF)

    def head_sums(left, rights):
        return dot_nn(gather_heads, jnp.concatenate([(left * right).astype(BF) for right in rights], axis=1))

    def diag_heads(target_ref, at, rows):
        for head in range(HEADS):
            target_ref[at, 16 * head : 16 * head + 16, 128 * head : 128 * head + 128] = rows[16 * head : 16 * head + 16]

    qbd_ref[...] = jnp.zeros_like(qbd_ref)
    dob_ref[...] = jnp.zeros_like(dob_ref)

    def gain(l, k):
        return colb_ref[l * 8 + k]

    def scale(l, k):
        return colb_ref[l * 8 + 4 + k]

    def keep_norm(l, k, c, x):
        xhat, inv = norm_cols(x)
        xh_ref[l * 4 + k, c] = xhat
        inv_ref[l * 4 + k, c] = inv
        return (xhat * gain(l, k)).astype(BF)

    def time_forward(l, c):
        x = h_ref[c]
        n = keep_norm(l, 0, c, x)
        qkv = dot_nn(wt_ref[l, 0:384, :], n)
        queries = (qkv[:128] * 0.25).astype(BF)
        keys = qkv[128:256].astype(BF)
        values = qkv[256:].astype(BF)
        qkvt_ref[l, c, 0:128, :] = queries
        qkvt_ref[l, c, 128:256, :] = keys
        qkvt_ref[l, c, 256:384, :] = values
        for s in range(2):
            lanes = slice(128 * s, 128 * s + 128)
            at = 2 * (c % 2) + s
            diag_heads(qbd_ref, at, queries[:, lanes])
            key_rows = turn(eye, keys[:, lanes]).astype(BF)
            for hp in range(4):
                span = slice(256 * hp, 256 * hp + 256)
                rows = slice(32 * hp, 32 * hp + 32)
                scores = dot_nn(key_rows, qbd_ref[at, :, span])
                shifted = jnp.exp(scores - jnp.max(scores, axis=0, keepdims=True))
                prob = (shifted * (1.0 / jnp.sum(shifted, axis=0, keepdims=True))).astype(BF)
                pb_ref[l, 2 * c + s, :, span] = prob
                mixed = dot_nn(values[rows, lanes], prob)
                ot_ref[l, c, 32 * hp : 32 * hp + 16, lanes] = mixed[:16, :128].astype(BF)
                ot_ref[l, c, 32 * hp + 16 : 32 * hp + 32, lanes] = mixed[16:, 128:].astype(BF)
        branch = dot_nn(wt_ref[l, COL_OUT[0] : COL_OUT[0] + 128, :], ot_ref[l, c])
        h_ref[c] = x + scale(l, 0) * branch

    def var_forward(l, b):
        for cc in range(2):
            c = 2 * b + cc
            n = keep_norm(l, 1, c, h_ref[c])
            qkv = dot_nn(wt_ref[l, COL_IN[1] : COL_IN[1] + 384, :], n)
            qkvv_ref[l, c, 0:128, :] = (qkv[:128] * 0.25).astype(BF)
            qkvv_ref[l, c, 128:384, :] = qkv[128:].astype(BF)
        count = counts_ref[ids_ref[b]]

        def slot(first, i):
            lanes = slice(128 * (i % 2), 128 * (i % 2) + 128)
            return qkvv_ref[l, 2 * b + i // 2, first : first + 128, lanes].astype(F32)

        key_slots = [slot(128, j) for j in range(4)]
        value_slots = [slot(256, j) for j in range(4)]
        for i in range(4):
            scores = head_sums(slot(0, i), key_slots)
            parts = [scores[:, 128 * j : 128 * j + 128] for j in range(4)]
            parts = [jnp.where(jnp.full((8, 128), count, jnp.int32) > j, parts[j], NEG_FILL) for j in range(4)]
            top = jnp.maximum(jnp.maximum(parts[0], parts[1]), jnp.maximum(parts[2], parts[3]))
            shifted = [jnp.exp(part - top) for part in parts]
            total = 1.0 / ((shifted[0] + shifted[1]) + (shifted[2] + shifted[3]))
            prob = jnp.concatenate([part * total for part in shifted], axis=1)
            pv_ref[l, b, i] = prob
            spread = dot_nn(spread_heads, prob.astype(BF))
            pw_ref[l, b, i] = spread.astype(BF)
            mixed = spread[:, :128] * value_slots[0]
            for j in range(1, 4):
                mixed = mixed + spread[:, 128 * j : 128 * j + 128] * value_slots[j]
            lanes = slice(128 * (i % 2), 128 * (i % 2) + 128)
            ov_ref[l, 2 * b + i // 2, :, lanes] = mixed.astype(BF)
        for cc in range(2):
            c = 2 * b + cc
            branch = dot_nn(wt_ref[l, COL_OUT[1] : COL_OUT[1] + 128, :], ov_ref[l, c])
            h_ref[c] = h_ref[c] + scale(l, 1) * branch

    def tail_forward(l, c):
        x = h_ref[c]
        n = keep_norm(l, 2, c, x)
        mix = [dot_nt(n[:, 128 * s : 128 * s + 128], tok_ref[l]) for s in range(2)]
        x = x + scale(l, 2) * jnp.concatenate(mix, axis=1)
        n = keep_norm(l, 3, c, x)
        for z in range(4):
            gate = dot_nn(wt_ref[l, COL_FEED + 128 * z : COL_FEED + 128 * z + 128, :], n)
            up = dot_nn(wt_ref[l, COL_FEED + 512 + 128 * z : COL_FEED + 640 + 128 * z, :], n)
            sig = 0.5 * jnp.tanh(0.5 * gate) + 0.5
            hid_ref[c % 2, 128 * z : 128 * z + 128, :] = (gate * sig * up).astype(BF)
        h_ref[c] = x + scale(l, 3) * dot_nn(wdt_ref[l], hid_ref[c % 2])

    def norm_of(l, k, c):
        xhat = xh_ref[l * 4 + k, c]
        return xhat, inv_ref[l * 4 + k, c], (xhat * gain(l, k)).astype(BF)

    def pass_on(l, k, c, x, dn, xhat, inv):
        back, both = norm_cols_back(dn, gain(l, k), xhat, inv)
        if x == 0:
            gacc_ref[l * 4 + k] += fold(both)
        g_ref[x, c] += back

    def feed_backward(l, c):
        xhat, inv, n = norm_of(l, 3, c)
        dz = [(scale(l, 3) * g_ref[x, c]).astype(BF) for x in range(2)]
        for z in range(4):
            rows = slice(128 * z, 128 * z + 128)
            gate = dot_nn(wt_ref[l, COL_FEED + 128 * z : COL_FEED + 128 * z + 128, :], n)
            up = dot_nn(wt_ref[l, COL_FEED + 512 + 128 * z : COL_FEED + 640 + 128 * z, :], n)
            sig = 0.5 * jnp.tanh(0.5 * gate) + 0.5
            act = gate * sig
            hid_ref[c % 2, rows, :] = (act * up).astype(BF)
            slope = up * (sig * (1.0 + gate * (1.0 - sig)))
            for x in range(2):
                dhid = dot_nn(wd_ref[l, rows, :], dz[x])
                du_ref[2 * (c % 2) + x, 128 * z : 128 * z + 128, :] = (dhid * slope).astype(BF)
                du_ref[2 * (c % 2) + x, 512 + 128 * z : 640 + 128 * z, :] = (dhid * act).astype(BF)
        gf_ref[...] += dot_nt(du_ref[2 * (c % 2)], n)
        gd_ref[...] += dot_nt(hid_ref[c % 2], dz[0])
        for x in range(2):
            dn = dot_nn(w_ref[l, :, COL_FEED:COL_DOWN], du_ref[2 * (c % 2) + x])
            pass_on(l, 3, c, x, dn, xhat, inv)

    def token_backward(l, c):
        xhat, inv, n = norm_of(l, 2, c)
        for x in range(2):
            dy = (scale(l, 2) * g_ref[x, c]).astype(BF)
            dn = []
            for s in range(2):
                part = dy[:, 128 * s : 128 * s + 128]
                dn.append(dot_nn(part, tok_ref[l]))
                if x == 0:
                    gt_ref[l] += dot_nn(turn(eye, part).astype(BF), n[:, 128 * s : 128 * s + 128])
            pass_on(l, 2, c, x, jnp.concatenate(dn, axis=1), xhat, inv)

    def var_backward(l, b):
        def slot(first, i):
            lanes = slice(128 * (i % 2), 128 * (i % 2) + 128)
            return qkvv_ref[l, 2 * b + i // 2, first : first + 128, lanes].astype(F32)

        for x in range(2):
            for cc in range(2):
                c = 2 * b + cc
                dt = (scale(l, 1) * g_ref[x, c]).astype(BF)
                dov_ref[4 * b + 2 * x + cc] = dot_nn(w_ref[l, :, COL_OUT[1] : COL_OUT[1] + 128], dt).astype(BF)
                if x == 0:
                    ga_ref[:, COL_OUT[1] : COL_OUT[1] + 128] += dot_nt(ov_ref[l, c], dt)
            value_slots = [slot(256, j) for j in range(4)]
            dkeys = [0.0] * 4
            dvalues = [0.0] * 4
            for i in range(4):
                lanes = slice(128 * (i % 2), 128 * (i % 2) + 128)
                grad = dov_ref[4 * b + 2 * x + i // 2, :, lanes].astype(F32)
                query = slot(0, i)
                prob = pv_ref[l, b, i]
                weighted = prob * head_sums(grad, value_slots)
                total = (weighted[:, :128] + weighted[:, 128:256]) + (weighted[:, 256:384] + weighted[:, 384:])
                ds = weighted - prob * jnp.concatenate([total] * 4, axis=1)
                ds_wide = dot_nn(spread_heads, ds.astype(BF))
                ds_slots = [ds_wide[:, 128 * j : 128 * j + 128] for j in range(4)]
                terms = [ds_slots[j] * slot(128, j) for j in range(4)]
                dquery = (terms[0] + terms[1]) + (terms[2] + terms[3])
                for j in range(4):
                    dkeys[j] = dkeys[j] + ds_slots[j] * query
                    dvalues[j] = dvalues[j] + pw_ref[l, b, i, :, 128 * j : 128 * j + 128].astype(F32) * grad
                dqkv_ref[4 * b + 2 * x + i // 2, 0:128, lanes] = (dquery * 0.25).astype(BF)
            for j in range(4):
                lanes = slice(128 * (j % 2), 128 * (j % 2) + 128)
                dqkv_ref[4 * b + 2 * x + j // 2, 128:256, lanes] = dkeys[j].astype(BF)
                dqkv_ref[4 * b + 2 * x + j // 2, 256:384, lanes] = dvalues[j].astype(BF)
            for cc in range(2):
                c = 2 * b + cc
                xhat, inv, n = norm_of(l, 1, c)
                dqkv = dqkv_ref[4 * b + 2 * x + cc]
                if x == 0:
                    ga_ref[:, COL_IN[1] : COL_IN[1] + 384] += dot_nt(n, dqkv)
                pass_on(l, 1, c, x, dot_nn(w_ref[l, :, COL_IN[1] : COL_IN[1] + 384], dqkv), xhat, inv)

    def time_backward(l, c):
        xhat, inv, n = norm_of(l, 0, c)
        queries = qkvt_ref[l, c, 0:128, :]
        keys = qkvt_ref[l, c, 128:256, :]
        values = qkvt_ref[l, c, 256:384, :]
        grads = []
        for x in range(2):
            dt = (scale(l, 0) * g_ref[x, c]).astype(BF)
            grads.append(dot_nn(w_ref[l, :, COL_OUT[0] : COL_OUT[0] + 128], dt).astype(BF))
            if x == 0:
                ga_ref[:, COL_OUT[0] : COL_OUT[0] + 128] += dot_nt(ot_ref[l, c], dt)
        for s in range(2):
            lanes = slice(128 * s, 128 * s + 128)
            at = 2 * (c % 2) + s
            diag_heads(qbd_ref, at, queries[:, lanes])
            value_rows = turn(eye, values[:, lanes]).astype(BF)
            for x in range(2):
                diag_heads(dob_ref, 2 * at + x, grads[x][:, lanes])
            for hp in range(4):
                span = slice(256 * hp, 256 * hp + 256)
                rows = slice(32 * hp, 32 * hp + 32)
                prob_bf = pb_ref[l, 2 * c + s, :, span]
                prob = prob_bf.astype(F32)
                for x in range(2):
                    weighted = prob * dot_nn(value_rows, dob_ref[2 * at + x, :, span])
                    ds = (weighted - prob * jnp.sum(weighted, axis=0, keepdims=True)).astype(BF)
                    dvalue = dot_nt(dob_ref[2 * at + x, rows, span], prob_bf)
                    dquery = dot_nn(keys[rows, lanes], ds) * 0.25
                    dkey = dot_nt(qbd_ref[at, rows, span], ds)
                    dqkv_ref[2 * c + x, 32 * hp : 32 * hp + 16, lanes] = dquery[:16, :128].astype(BF)
                    dqkv_ref[2 * c + x, 32 * hp + 16 : 32 * hp + 32, lanes] = dquery[16:, 128:].astype(BF)
                    dqkv_ref[2 * c + x, 128 + 32 * hp : 160 + 32 * hp, lanes] = dkey.astype(BF)
                    dqkv_ref[2 * c + x, 256 + 32 * hp : 288 + 32 * hp, lanes] = dvalue.astype(BF)
        ga_ref[:, COL_IN[0] : COL_IN[0] + 384] += dot_nt(n, dqkv_ref[2 * c])
        for x in range(2):
            pass_on(l, 0, c, x, dot_nn(w_ref[l, :, COL_IN[0] : COL_IN[0] + 384], dqkv_ref[2 * c + x]), xhat, inv)

    def each(count, stage, l):
        for i in range(count):
            stage(l, i)

    def forward_layer(l, carry):
        each(chunks, time_forward, l)
        each(items, var_forward, l)
        each(chunks, tail_forward, l)
        return carry

    lax.fori_loop(0, layers, forward_layer, 0)
    for b in range(items):
        for v in range(4):
            lanes = slice(128 * (v % 2), 128 * (v % 2) + 128)
            out_ref[b, v] = turn(eye, h_ref[2 * b + v // 2, :, lanes].astype(BF)).astype(BF)

    gacc_ref[...] = jnp.zeros_like(gacc_ref)
    gt_ref[...] = jnp.zeros_like(gt_ref)
    pacc_ref[...] = jnp.zeros_like(pacc_ref)

    def backward_layer(step, carry):
        l = layers - 1 - step
        ga_ref[...] = jnp.zeros_like(ga_ref)
        gd_ref[...] = jnp.zeros_like(gd_ref)
        gf_ref[...] = jnp.zeros_like(gf_ref)
        each(chunks, feed_backward, l)
        each(chunks, token_backward, l)
        each(items, var_backward, l)
        each(chunks, time_backward, l)
        for k in range(8):
            turned = gf_ref[128 * k : 128 * k + 128, :].T
            for f in range(SHARDS):
                gbig_ref[l, f, :, COL_FEED + 128 * k : COL_FEED + 128 * k + 128] = turned[8 * f : 8 * f + 8].astype(BF)
        for f in range(SHARDS):
            gbig_ref[l, f, :, 0:COL_FEED] = ga_ref[8 * f : 8 * f + 8, :].astype(BF)
            down = jnp.concatenate([gd_ref[32 * f + 8 * a : 32 * f + 8 * a + 8, :] for a in range(4)], axis=1)
            gbig_ref[l, f, :, COL_DOWN:COLS] = down.astype(BF)
        gains_rows = [jnp.sum(gacc_ref[l * 4 + k].T, axis=0, keepdims=True) for k in range(4)]
        sums = [
            jnp.sum(w_ref[l, :, COL_OUT[k] : COL_OUT[k] + 128].astype(F32) * ga_ref[:, COL_OUT[k] : COL_OUT[k] + 128], axis=0, keepdims=True)
            for k in range(2)
        ]
        sums.append(gains_rows[2])
        sums.append(jnp.sum(wd_ref[l].astype(F32) * gd_ref[...], axis=0, keepdims=True))
        for k in range(4):
            pacc_ref[0, l * 4 + k, 10:11, :] = gains_rows[k] / gains_ref[l, k : k + 1, :]
            pacc_ref[0, l * 4 + k, 11:12, :] = sums[k] / scales_ref[l, k : k + 1, :]
        return carry

    lax.fori_loop(0, layers, backward_layer, 0)

    for x in range(2):
        cls_sum = None
        for b in range(items):
            prompt_sum = None
            for v in range(4):
                lanes = slice(128 * (v % 2), 128 * (v % 2) + 128)
                tokscr_ref[4 * b + v] = g_ref[x, 2 * b + v // 2, :, lanes].T
                head = tokscr_ref[4 * b + v, 0:10, :]
                last = tokscr_ref[4 * b + v, 127:128, :]
                prompt_sum = head if prompt_sum is None else prompt_sum + head
                cls_sum = last if cls_sum is None else cls_sum + last
                if x == 0:
                    pgrad_ref[b, v] = tokscr_ref[4 * b + v, 10:127, :]
            pacc_ref[x, ids_ref[b], 0:10, :] += prompt_sum
        pacc_ref[x, 0, 12:13, :] = cls_sum

    for big_ref, small_ref, c in ((bigmine_ref, smallmine_ref, dp), (bigother_ref, smallother_ref, 1 - dp)):
        for rel in range(SHARDS):
            big_ref[rel % 4, rel // 4] = gbig_ref[c, me ^ rel]
        for block in range(16):
            if block < 8:
                pair = gt_ref[c, 16 * block : 16 * block + 16, :]
            else:
                pair = pacc_ref[block // 4 - 2, 4 * c + block % 4]
            lanes = slice(256 * (block % 4), 256 * (block % 4) + 256)
            small_ref[block // 4, :, lanes] = jnp.concatenate([pair[:8], pair[8:]], axis=1)


def call(kernel, name, out_shape, in_spaces, scratch, *operands, cost=None):
    spaces = {"v": pltpu.VMEM, "s": pltpu.SMEM}
    return pl.pallas_call(
        kernel,
        out_shape=out_shape,
        in_specs=[pl.BlockSpec(memory_space=spaces[space]) for space in in_spaces],
        out_specs=[pl.BlockSpec(memory_space=pltpu.VMEM)] * len(out_shape),
        scratch_shapes=scratch,
        compiler_params=pltpu.CompilerParams(vmem_limit_bytes=58 * 1024 * 1024),
        cost_estimate=cost,
        name=name,
    )(*operands)


def shape_of(shape, kind=F32):
    return jax.ShapeDtypeStruct(shape, kind)


def run_tower(split, *operands):
    half = [shape_of((4, 4, 8, COLS), BF)] * 2 + [shape_of((4, 8, 1024))] * 2
    return call(
        functools.partial(tower_kernel, split),
        "tower",
        [shape_of((2, 4, 128, 128), BF), shape_of((2, 4, 117, 128))] + half,
        "ss" + "v" * 16,
        [
            pltpu.VMEM((2, 128, COLS), F32),
            pltpu.VMEM((2, 128, COL_DOWN), BF),
            pltpu.VMEM((2, 512, 128), BF),
            pltpu.VMEM((2, COL_DOWN, 128), BF),
            pltpu.VMEM((2, 128, 512), BF),
            pltpu.VMEM((16, 128, 256), F32),
            pltpu.VMEM((8, 128, 128), F32),
            pltpu.VMEM((4, 128, 256), F32),
            pltpu.VMEM((2, 4, 128, 256), F32),
            pltpu.VMEM((8, 4, 128, 256), F32),
            pltpu.VMEM((8, 4, 1, 256), F32),
            pltpu.VMEM((2, 4, 384, 256), BF),
            pltpu.VMEM((2, 8, 128, 1024), BF),
            pltpu.VMEM((2, 4, 128, 256), BF),
            pltpu.VMEM((2, 4, 384, 256), BF),
            pltpu.VMEM((2, 2, 4, 8, 512), F32),
            pltpu.VMEM((2, 4, 128, 256), BF),
            pltpu.VMEM((2, 2, 4, 128, 512), BF),
            pltpu.VMEM((4, 128, 1024), BF),
            pltpu.VMEM((8, 128, 1024), BF),
            pltpu.VMEM((2, 512, 256), BF),
            pltpu.VMEM((4, 1024, 256), BF),
            pltpu.VMEM((8, 384, 256), BF),
            pltpu.VMEM((8, 128, 256), BF),
            pltpu.VMEM((128, COL_FEED), F32),
            pltpu.VMEM((1024, 128), F32),
            pltpu.VMEM((512, 128), F32),
            pltpu.VMEM((2, 128, 128), F32),
            pltpu.VMEM((8, 128, 128), F32),
            pltpu.VMEM((2, SHARDS, 8, COLS), BF),
            pltpu.VMEM((2, 8, 16, 128), F32),
        ],
        *operands,
        cost=pl.CostEstimate(flops=10**10, bytes_accessed=20 * 10**6, transcendentals=0),
    )


def pack_rows(attn_in, attn_out, feed_in, feed_out):
    layers, _, rows, _ = attn_in.shape
    down = feed_out.reshape(layers, 4, rows, 128)
    return jnp.concatenate(
        [attn_in[:, 0], attn_in[:, 1], attn_out[:, 0], attn_out[:, 1], feed_in] + [down[:, a] for a in range(4)], axis=2
    )


def unpack_rows(packed):
    layers, rows, _ = packed.shape
    attn_in = jnp.stack([packed[:, :, at : at + 384] for at in COL_IN], axis=1)
    attn_out = jnp.stack([packed[:, :, at : at + 128] for at in COL_OUT], axis=1)
    feed_in = packed[:, :, COL_FEED:COL_DOWN]
    feed_out = jnp.stack([packed[:, :, COL_DOWN + 128 * a : COL_DOWN + 128 * a + 128] for a in range(4)], axis=1)
    return attn_in, attn_out, feed_in, feed_out.reshape(layers, 4 * rows, 128)


def flip(array, axis, bit, size):
    return lax.ppermute(array, axis, [(i, i ^ (1 << bit)) for i in range(size)])


def swap(array, mask):
    return lax.ppermute(array, "fsdp", [(i, i ^ mask) for i in range(SHARDS)])


def gather_rows(attn_in, attn_out, feed_in, feed_out):
    row = call(pack_kernel, "pack", [shape_of((1, 8, COLS), BF)], "vvvv", [], attn_in, attn_out, feed_in, feed_out)[0]
    column = jnp.concatenate([row] + [swap(row, 4 * z) for z in range(1, 4)], axis=0)
    mine = [column] + [swap(column, xy) for xy in range(1, 4)]
    return mine + [flip(part, "dp", 0, 2) for part in mine]


def final_kernel(big_mine, big_other, small_mine, small_other, attn_in, attn_out, feed_in, feed_out, tokens, gains, scales,
                 prompt, cls, adjust_prompt, adjust_cls):
    dp = lax.axis_index("dp")
    for part, l in ((big_mine, dp), (big_other, 1 - dp)):
        for k in range(2):
            attn_in[l, k] = part[:, COL_IN[k] : COL_IN[k] + 384]
            attn_out[l, k] = part[:, COL_OUT[k] : COL_OUT[k] + 128]
        feed_in[l] = part[:, COL_FEED:COL_DOWN]
        for a in range(4):
            feed_out[l, 8 * a : 8 * a + 8, :] = part[:, COL_DOWN + 128 * a : COL_DOWN + 128 * a + 128]
    for c in range(2):
        parts = [slice(256 * k, 256 * k + 256) for k in range(16)]
        tiles = [jnp.where(dp == c, small_mine[:, part], small_other[:, part]) for part in parts]
        blocks = [jnp.concatenate([tile[:, :128], tile[:, 128:]], axis=0) for tile in tiles]
        for k in range(8):
            tokens[c, 16 * k : 16 * k + 16, :] = blocks[k]
        for k in range(4):
            for row in range(10):
                prompt[row, 4 * c + k : 4 * c + k + 1, :] = blocks[8 + k][row : row + 1]
                adjust_prompt[row, 4 * c + k : 4 * c + k + 1, :] = blocks[12 + k][row : row + 1]
            gains[c, k : k + 1, :] = blocks[8 + k][10:11]
            scales[c, k : k + 1, :] = blocks[8 + k][11:12]
        if c == 0:
            cls[...] = blocks[8][12:13]
            adjust_cls[...] = blocks[12][12:13]


def four(first, rest):
    return (first.astype(F32) + rest[0].astype(F32)) + (rest[1].astype(F32) + rest[2].astype(F32))


def reduce_all(big_mine, big_other, small_mine, small_other):
    big = (big_mine.astype(F32) + flip(big_other, "dp", 0, 2).astype(F32)).astype(BF)
    small = (small_mine + flip(small_other, "dp", 0, 2)).astype(BF)
    got = [swap(jnp.concatenate([big[xy], small], axis=2), xy) for xy in range(1, 4)]
    big = four(big[0], [part[:, :, :COLS] for part in got]).astype(BF)
    small = four(small, [part[:, :, COLS:] for part in got]).astype(BF)
    small = jnp.concatenate([small[at] for at in range(4)], axis=1)
    got = [swap(jnp.concatenate([big[z], small], axis=1), 4 * z) for z in range(1, 4)]
    big = four(big[0], [part[:, :COLS] for part in got])
    small = four(small, [part[:, COLS:] for part in got])
    return call(
        final_kernel, "final",
        [shape_of((2, 2, 8, 384)), shape_of((2, 2, 8, 128)), shape_of((2, 8, 1024)), shape_of((2, 32, 128)), shape_of((2, 128, 128)),
         shape_of((2, 4, 128)), shape_of((2, 4, 128)), shape_of((10, 8, 128)), shape_of((1, 128)), shape_of((10, 8, 128)), shape_of((1, 128))],
        "vvvv", [], big, flip(big, "dp", 0, 2), small, flip(small, "dp", 0, 2),
    )


def per_device(shard_count, patches, prompts, cls_token, attn_in, attn_out, feed_in, feed_out, token_operator,
               norm_gains, branch_scales, var_counts, dataset_ids, cotangent, adjust_cotangent):
    fast = shard_count == SHARDS
    if fast:
        gathered = gather_rows(attn_in, attn_out, feed_in, feed_out)
    else:
        whole_down = lax.all_gather(feed_out, "fsdp", axis=1, tiled=True)
        whole_down = whole_down.reshape(2, SHARDS, 4, 8, 128).transpose(0, 2, 1, 3, 4).reshape(2, 512, 128)
        rows = pack_rows(
            lax.all_gather(attn_in, "fsdp", axis=2, tiled=True),
            lax.all_gather(attn_out, "fsdp", axis=2, tiled=True),
            lax.all_gather(feed_in, "fsdp", axis=1, tiled=True),
            whole_down,
        )
        rows = rows.reshape(2, SHARDS, 8, COLS).transpose(1, 0, 2, 3)
        gathered = [rows[:, l].reshape(4, 4, 8, COLS)[:, xy] for l in range(2) for xy in range(4)]
    output, patch_grad, *sums = run_tower(
        fast, dataset_ids, var_counts, *gathered, token_operator, norm_gains, branch_scales, patches, prompts,
        cls_token.reshape(1, -1), cotangent, adjust_cotangent,
    )
    if fast:
        (attn_in_g, attn_out_g, feed_in_g, feed_out_g, token_g, gains_g, scales_g, prompt_g, cls_g, adjust_prompt_g,
         adjust_cls_g) = reduce_all(*sums)
        return (output, patch_grad, prompt_g.transpose(1, 0, 2), cls_g[0], attn_in_g, attn_out_g, feed_in_g, feed_out_g, token_g, gains_g,
                scales_g, adjust_prompt_g.transpose(1, 0, 2), adjust_cls_g[0])
    rows = jnp.stack(sums[:2]).transpose(0, 2, 1, 3, 4).astype(F32).reshape(2, 128, COLS)
    attn_in_g, attn_out_g, feed_in_g, feed_out_g = unpack_rows(rows)
    feed_out_g = feed_out_g.reshape(2, 4, SHARDS, 8, 128).transpose(0, 2, 1, 3, 4).reshape(2, 512, 128)
    matrices = (
        lax.psum_scatter(lax.psum(attn_in_g, "dp"), "fsdp", scatter_dimension=2, tiled=True),
        lax.psum_scatter(lax.psum(attn_out_g, "dp"), "fsdp", scatter_dimension=2, tiled=True),
        lax.psum_scatter(lax.psum(feed_in_g, "dp"), "fsdp", scatter_dimension=1, tiled=True),
        lax.psum_scatter(lax.psum(feed_out_g, "dp"), "fsdp", scatter_dimension=1, tiled=True),
    )
    small = lax.psum(jnp.stack(sums[2:]), ("dp", "fsdp"))
    small = small.reshape(2, 4, 8, 4, 2, 128).transpose(0, 1, 3, 4, 2, 5).reshape(2, 16, 16, 128)
    main, adjust = small[:, 8:12].reshape(8, 16, 128), small[:, 12:].reshape(8, 16, 128)
    return (output, patch_grad, main[:, :10], main[0, 12], *matrices, small[:, :8].reshape(2, 128, 128),
            main[:, 10].reshape(2, 4, 128), main[:, 11].reshape(2, 4, 128), adjust[:, :10], adjust[0, 12])


def solution(mesh):
    batch = P(("dp", "fsdp"), None, None, None)
    wide = P(None, None, "fsdp", None)
    tall = P(None, "fsdp", None)
    return jax.shard_map(
        functools.partial(per_device, mesh.shape["fsdp"]),
        mesh=mesh,
        in_specs=(batch, P(), P(), wide, wide, tall, tall, P(), P(), P(), P(), P(("dp", "fsdp")), batch, batch),
        out_specs=(batch, batch, P(), P(), wide, wide, tall, tall, P(), P(), P(), P(), P()),
        check_vma=False,
    )
```

```python
import functools

import jax
import jax.numpy as jnp
from jax import lax
from jax.experimental import pallas as pl
from jax.experimental.pallas import tpu as pltpu
from jax.sharding import PartitionSpec as P

HEADS = 8
EPSILON = 1e-05
NEG_FILL = -1000000000.0
BF = jnp.bfloat16
F32 = jnp.float32

COL_IN = (0, 384)
COL_OUT = (768, 896)
COL_FEED = 1024
COL_DOWN = 2048
COLS = 2560
SHARDS = 16
STEP_BITS = (2, 3, 0, 1)


def dot_nn(a, b):
    return lax.dot_general(a, b, (((1,), (0,)), ((), ())), preferred_element_type=F32)


def dot_nt(a, b):
    return lax.dot_general(a, b, (((1,), (1,)), ((), ())), preferred_element_type=F32)


def norm_cols(x):
    centered = x - jnp.mean(x, axis=0, keepdims=True)
    inv = lax.rsqrt(jnp.mean(centered * centered, axis=0, keepdims=True) + EPSILON)
    return centered * inv, inv


def norm_cols_back(dn, gain, xhat, inv):
    e = dn * gain
    both = e * xhat
    m1 = jnp.mean(e, axis=0, keepdims=True)
    m2 = jnp.mean(both, axis=0, keepdims=True)
    return inv * (e - m1 - xhat * m2), both


def fold(part):
    return part[:, :128] + part[:, 128:]


def pack_kernel(attn_in_ref, attn_out_ref, feed_in_ref, feed_out_ref, out_ref):
    l = lax.axis_index("dp")
    down = feed_out_ref[l].astype(F32)
    parts = [attn_in_ref[l, 0], attn_in_ref[l, 1], attn_out_ref[l, 0], attn_out_ref[l, 1], feed_in_ref[l]]
    parts = [part.astype(F32) for part in parts] + [down[8 * a : 8 * a + 8] for a in range(4)]
    out_ref[0] = jnp.concatenate(parts, axis=1).astype(BF)


def tower_kernel(
    split,
    ids_ref, counts_ref, wmine0_ref, wmine1_ref, wmine2_ref, wmine3_ref, wother0_ref, wother1_ref, wother2_ref, wother3_ref,
    tok_ref, gains_ref, scales_ref, patches_ref, prompts_ref, cls_ref, cot_ref, adj_ref,
    out_ref, pgrad_ref, bigmine_ref, bigother_ref, smallmine_ref, smallother_ref,
    stage_ref, w_ref, wd_ref, wt_ref, wdt_ref, colb_ref, tokscr_ref, h_ref, g_ref, xh_ref, inv_ref,
    qkvt_ref, pb_ref, ot_ref, qkvv_ref, pv_ref, ov_ref, pw_ref, qbd_ref, dob_ref, hid_ref, du_ref, dqkv_ref,
    dov_ref, ga_ref, gd_ref, gt_ref, gacc_ref, gbig_ref, pacc_ref, spread_ref, act_ref, slope_ref, gdt_ref,
):
    dp = lax.axis_index("dp") if split else 0
    me = lax.axis_index("fsdp") if split else 0
    layers = 2
    chunks = 4
    items = 2

    for rel in range(SHARDS):
        rows = pl.ds(pl.multiple_of(8 * (me ^ rel), 8), 8)
        mine_ref = (wmine0_ref, wmine1_ref, wmine2_ref, wmine3_ref)[rel % 4]
        other_ref = (wother0_ref, wother1_ref, wother2_ref, wother3_ref)[rel % 4]
        stage_ref[dp, rows, :] = mine_ref[rel // 4].astype(F32)
        stage_ref[1 - dp, rows, :] = other_ref[rel // 4].astype(F32)
    for l in range(layers):
        for pair in range(SHARDS // 2):
            lo = stage_ref[l, 16 * pair : 16 * pair + 8, :]
            hi = stage_ref[l, 16 * pair + 8 : 16 * pair + 16, :]
            w_ref[l, 16 * pair : 16 * pair + 16, :] = jnp.concatenate([lo[:, :COL_DOWN], hi[:, :COL_DOWN]], axis=0).astype(BF)
            for half, part in enumerate((lo, hi)):
                base = 64 * pair + 32 * half
                wd_ref[l, base : base + 32, :] = jnp.concatenate(
                    [part[:, COL_DOWN + 128 * a : COL_DOWN + 128 * a + 128] for a in range(4)], axis=0
                ).astype(BF)
        for block in range(COL_DOWN // 128):
            wt_ref[l, 128 * block : 128 * block + 128, :] = w_ref[l, :, 128 * block : 128 * block + 128].T
        for block in range(4):
            wdt_ref[l, :, 128 * block : 128 * block + 128] = wd_ref[l, 128 * block : 128 * block + 128, :].T
        for k in range(4):
            for offset, rows in ((0, gains_ref), (4, scales_ref)):
                col = jnp.broadcast_to(rows[l, k : k + 1, :], (128, 128)).T
                colb_ref[l * 8 + offset + k, :, 0:128] = col
                colb_ref[l * 8 + offset + k, :, 128:256] = col

    for b in range(items):
        ident = ids_ref[b]
        for v in range(4):
            bv = 4 * b + v
            tokscr_ref[bv, 0:10, :] = prompts_ref[ident].astype(F32)
            tokscr_ref[bv, 10:127, :] = patches_ref[b, v].astype(F32)
            tokscr_ref[bv, 127:128, :] = cls_ref[...].astype(F32)
            lanes = slice(128 * (v % 2), 128 * (v % 2) + 128)
            h_ref[2 * b + v // 2, :, lanes] = tokscr_ref[bv].T
            g_ref[0, 2 * b + v // 2, :, lanes] = cot_ref[b, v].astype(F32).T
            g_ref[1, 2 * b + v // 2, :, lanes] = adj_ref[b, v].astype(F32).T

    head_row = lax.broadcasted_iota(jnp.int32, (8, 128), 0)
    head_col = lax.broadcasted_iota(jnp.int32, (8, 128), 1) // 16
    gather_heads = jnp.where(head_row == head_col, 1.0, 0.0).astype(BF)
    def spread_of(at, j):
        lanes = slice(128 * j, 128 * j + 128)
        return jnp.concatenate([jnp.broadcast_to(spread_ref[at, h : h + 1, lanes], (16, 128)) for h in range(HEADS)], axis=0)

    def head_sums(left, rights):
        return dot_nn(gather_heads, jnp.concatenate([(left * right).astype(BF) for right in rights], axis=1))

    def diag_heads(target_ref, at, rows):
        for head in range(HEADS):
            target_ref[at, 16 * head : 16 * head + 16, 128 * head : 128 * head + 128] = rows[16 * head : 16 * head + 16]

    qbd_ref[...] = jnp.zeros_like(qbd_ref)
    dob_ref[...] = jnp.zeros_like(dob_ref)

    def gain(l, k):
        return colb_ref[l * 8 + k]

    def scale(l, k):
        return colb_ref[l * 8 + 4 + k]

    def keep_norm(l, k, c, x):
        xhat, inv = norm_cols(x)
        xh_ref[l * 4 + k, c] = xhat
        inv_ref[l * 4 + k, c] = inv
        return (xhat * gain(l, k)).astype(BF)

    def time_forward(l, c):
        x = h_ref[c]
        n = keep_norm(l, 0, c, x)
        qkv = dot_nn(wt_ref[l, 0:384, :], n)
        queries = (qkv[:128] * 0.25).astype(BF)
        keys = qkv[128:256].astype(BF)
        values = qkv[256:].astype(BF)
        qkvt_ref[l, c, 0:128, :] = queries
        qkvt_ref[l, c, 128:256, :] = keys
        qkvt_ref[l, c, 256:384, :] = values
        for s in range(2):
            lanes = slice(128 * s, 128 * s + 128)
            at = 2 * (c % 2) + s
            diag_heads(qbd_ref, at, queries[:, lanes])
            key_rows = keys[:, lanes].T
            for hp in range(4):
                span = slice(256 * hp, 256 * hp + 256)
                rows = slice(32 * hp, 32 * hp + 32)
                scores = dot_nn(key_rows, qbd_ref[at, :, span])
                shifted = jnp.exp(scores - jnp.max(scores, axis=0, keepdims=True))
                prob = (shifted * (1.0 / jnp.sum(shifted, axis=0, keepdims=True))).astype(BF)
                pb_ref[l, 2 * c + s, :, span] = prob
                mixed = dot_nn(values[rows, lanes], prob)
                ot_ref[l, c, 32 * hp : 32 * hp + 16, lanes] = mixed[:16, :128].astype(BF)
                ot_ref[l, c, 32 * hp + 16 : 32 * hp + 32, lanes] = mixed[16:, 128:].astype(BF)
        branch = dot_nn(wt_ref[l, COL_OUT[0] : COL_OUT[0] + 128, :], ot_ref[l, c])
        h_ref[c] = x + scale(l, 0) * branch

    def var_forward(l, b):
        for cc in range(2):
            c = 2 * b + cc
            n = keep_norm(l, 1, c, h_ref[c])
            qkv = dot_nn(wt_ref[l, COL_IN[1] : COL_IN[1] + 384, :], n)
            qkvv_ref[l, c, 0:128, :] = (qkv[:128] * 0.25).astype(BF)
            qkvv_ref[l, c, 128:384, :] = qkv[128:].astype(BF)
        count = counts_ref[ids_ref[b]]

        def slot(first, i):
            lanes = slice(128 * (i % 2), 128 * (i % 2) + 128)
            return qkvv_ref[l, 2 * b + i // 2, first : first + 128, lanes].astype(F32)

        key_slots = [slot(128, j) for j in range(4)]
        value_slots = [slot(256, j) for j in range(4)]
        for i in range(4):
            scores = head_sums(slot(0, i), key_slots)
            parts = [scores[:, 128 * j : 128 * j + 128] for j in range(4)]
            parts = [jnp.where(jnp.full((8, 128), count, jnp.int32) > j, parts[j], NEG_FILL) for j in range(4)]
            top = jnp.maximum(jnp.maximum(parts[0], parts[1]), jnp.maximum(parts[2], parts[3]))
            shifted = [jnp.exp(part - top) for part in parts]
            total = 1.0 / ((shifted[0] + shifted[1]) + (shifted[2] + shifted[3]))
            prob = jnp.concatenate([part * total for part in shifted], axis=1)
            pv_ref[l, b, i] = prob
            spread_ref[4 * b + i] = prob.astype(BF).astype(F32)
            mixed = None
            for j in range(4):
                spread = spread_of(4 * b + i, j)
                pw_ref[l, b, i, :, 128 * j : 128 * j + 128] = spread.astype(BF)
                mixed = spread * value_slots[j] if mixed is None else mixed + spread * value_slots[j]
            lanes = slice(128 * (i % 2), 128 * (i % 2) + 128)
            ov_ref[l, 2 * b + i // 2, :, lanes] = mixed.astype(BF)
        for cc in range(2):
            c = 2 * b + cc
            branch = dot_nn(wt_ref[l, COL_OUT[1] : COL_OUT[1] + 128, :], ov_ref[l, c])
            h_ref[c] = h_ref[c] + scale(l, 1) * branch

    def tail_forward(l, c):
        x = h_ref[c]
        n = keep_norm(l, 2, c, x)
        mix = [dot_nt(n[:, 128 * s : 128 * s + 128], tok_ref[l]) for s in range(2)]
        x = x + scale(l, 2) * jnp.concatenate(mix, axis=1)
        n = keep_norm(l, 3, c, x)
        for z in range(4):
            rows = slice(128 * z, 128 * z + 128)
            gate = dot_nn(wt_ref[l, COL_FEED + 128 * z : COL_FEED + 128 * z + 128, :], n)
            up = dot_nn(wt_ref[l, COL_FEED + 512 + 128 * z : COL_FEED + 640 + 128 * z, :], n)
            sig = 0.5 * jnp.tanh(0.5 * gate) + 0.5
            act = gate * sig
            hid_ref[l, c, rows, :] = (act * up).astype(BF)
            act_ref[l, c, rows, :] = act.astype(BF)
            slope_ref[l, c, rows, :] = (up * (sig * (1.0 + gate * (1.0 - sig)))).astype(BF)
        h_ref[c] = x + scale(l, 3) * dot_nn(wdt_ref[l], hid_ref[l, c])

    def norm_of(l, k, c):
        xhat = xh_ref[l * 4 + k, c]
        return xhat, inv_ref[l * 4 + k, c], (xhat * gain(l, k)).astype(BF)

    def pass_on(l, k, c, x, dn, xhat, inv):
        back, both = norm_cols_back(dn, gain(l, k), xhat, inv)
        if x == 0:
            gacc_ref[l * 4 + k] += fold(both)
        g_ref[x, c] += back

    def feed_backward(l, c):
        xhat, inv, n = norm_of(l, 3, c)
        dz = [(scale(l, 3) * g_ref[x, c]).astype(BF) for x in range(2)]
        for z in range(4):
            rows = slice(128 * z, 128 * z + 128)
            act = act_ref[l, c, rows, :].astype(F32)
            slope = slope_ref[l, c, rows, :].astype(F32)
            for x in range(2):
                dhid = dot_nn(wd_ref[l, rows, :], dz[x])
                du_ref[2 * (c % 2) + x, 128 * z : 128 * z + 128, :] = (dhid * slope).astype(BF)
                du_ref[2 * (c % 2) + x, 512 + 128 * z : 640 + 128 * z, :] = (dhid * act).astype(BF)
        ga_ref[:, COL_FEED:COL_DOWN] += dot_nt(n, du_ref[2 * (c % 2)])
        gdt_ref[...] += dot_nt(dz[0], hid_ref[l, c])
        for x in range(2):
            dn = dot_nn(w_ref[l, :, COL_FEED:COL_DOWN], du_ref[2 * (c % 2) + x])
            pass_on(l, 3, c, x, dn, xhat, inv)

    def token_backward(l, c):
        xhat, inv, n = norm_of(l, 2, c)
        for x in range(2):
            dy = (scale(l, 2) * g_ref[x, c]).astype(BF)
            if x == 0:
                turned = jnp.concatenate([dy[:, :128].T, dy[:, 128:].T], axis=1)
                gt_ref[l] += dot_nn(turned, jnp.concatenate([n[:, :128], n[:, 128:]], axis=0))
            dn = [dot_nn(dy[:, 128 * s : 128 * s + 128], tok_ref[l]) for s in range(2)]
            pass_on(l, 2, c, x, jnp.concatenate(dn, axis=1), xhat, inv)

    def var_backward(l, b):
        def slot(first, i):
            lanes = slice(128 * (i % 2), 128 * (i % 2) + 128)
            return qkvv_ref[l, 2 * b + i // 2, first : first + 128, lanes].astype(F32)

        for x in range(2):
            for cc in range(2):
                c = 2 * b + cc
                dt = (scale(l, 1) * g_ref[x, c]).astype(BF)
                dov_ref[4 * b + 2 * x + cc] = dot_nn(w_ref[l, :, COL_OUT[1] : COL_OUT[1] + 128], dt).astype(BF)
                if x == 0:
                    ga_ref[:, COL_OUT[1] : COL_OUT[1] + 128] += dot_nt(ov_ref[l, c], dt)
            value_slots = [slot(256, j) for j in range(4)]
            dkeys = [0.0] * 4
            dvalues = [0.0] * 4
            for i in range(4):
                lanes = slice(128 * (i % 2), 128 * (i % 2) + 128)
                grad = dov_ref[4 * b + 2 * x + i // 2, :, lanes].astype(F32)
                query = slot(0, i)
                prob = pv_ref[l, b, i]
                weighted = prob * head_sums(grad, value_slots)
                total = (weighted[:, :128] + weighted[:, 128:256]) + (weighted[:, 256:384] + weighted[:, 384:])
                ds = weighted - prob * jnp.concatenate([total] * 4, axis=1)
                spread_ref[8 * b + 4 * x + i] = ds.astype(BF).astype(F32)
                ds_slots = [spread_of(8 * b + 4 * x + i, j) for j in range(4)]
                terms = [ds_slots[j] * slot(128, j) for j in range(4)]
                dquery = (terms[0] + terms[1]) + (terms[2] + terms[3])
                for j in range(4):
                    dkeys[j] = dkeys[j] + ds_slots[j] * query
                    dvalues[j] = dvalues[j] + pw_ref[l, b, i, :, 128 * j : 128 * j + 128].astype(F32) * grad
                dqkv_ref[4 * b + 2 * x + i // 2, 0:128, lanes] = (dquery * 0.25).astype(BF)
            for j in range(4):
                lanes = slice(128 * (j % 2), 128 * (j % 2) + 128)
                dqkv_ref[4 * b + 2 * x + j // 2, 128:256, lanes] = dkeys[j].astype(BF)
                dqkv_ref[4 * b + 2 * x + j // 2, 256:384, lanes] = dvalues[j].astype(BF)
            for cc in range(2):
                c = 2 * b + cc
                xhat, inv, n = norm_of(l, 1, c)
                dqkv = dqkv_ref[4 * b + 2 * x + cc]
                if x == 0:
                    ga_ref[:, COL_IN[1] : COL_IN[1] + 384] += dot_nt(n, dqkv)
                pass_on(l, 1, c, x, dot_nn(w_ref[l, :, COL_IN[1] : COL_IN[1] + 384], dqkv), xhat, inv)

    def time_backward(l, c):
        xhat, inv, n = norm_of(l, 0, c)
        queries = qkvt_ref[l, c, 0:128, :]
        keys = qkvt_ref[l, c, 128:256, :]
        values = qkvt_ref[l, c, 256:384, :]
        grads = []
        for x in range(2):
            dt = (scale(l, 0) * g_ref[x, c]).astype(BF)
            grads.append(dot_nn(w_ref[l, :, COL_OUT[0] : COL_OUT[0] + 128], dt).astype(BF))
            if x == 0:
                ga_ref[:, COL_OUT[0] : COL_OUT[0] + 128] += dot_nt(ot_ref[l, c], dt)
        for s in range(2):
            lanes = slice(128 * s, 128 * s + 128)
            at = 2 * (c % 2) + s
            diag_heads(qbd_ref, at, queries[:, lanes])
            value_rows = values[:, lanes].T
            for x in range(2):
                diag_heads(dob_ref, 2 * at + x, grads[x][:, lanes])
            for hp in range(4):
                span = slice(256 * hp, 256 * hp + 256)
                rows = slice(32 * hp, 32 * hp + 32)
                prob_bf = pb_ref[l, 2 * c + s, :, span]
                prob = prob_bf.astype(F32)
                for x in range(2):
                    weighted = prob * dot_nn(value_rows, dob_ref[2 * at + x, :, span])
                    ds = (weighted - prob * jnp.sum(weighted, axis=0, keepdims=True)).astype(BF)
                    dvalue = dot_nt(dob_ref[2 * at + x, rows, span], prob_bf)
                    dquery = dot_nn(keys[rows, lanes], ds) * 0.25
                    dkey = dot_nt(qbd_ref[at, rows, span], ds)
                    dqkv_ref[2 * c + x, 32 * hp : 32 * hp + 16, lanes] = dquery[:16, :128].astype(BF)
                    dqkv_ref[2 * c + x, 32 * hp + 16 : 32 * hp + 32, lanes] = dquery[16:, 128:].astype(BF)
                    dqkv_ref[2 * c + x, 128 + 32 * hp : 160 + 32 * hp, lanes] = dkey.astype(BF)
                    dqkv_ref[2 * c + x, 256 + 32 * hp : 288 + 32 * hp, lanes] = dvalue.astype(BF)
        ga_ref[:, COL_IN[0] : COL_IN[0] + 384] += dot_nt(n, dqkv_ref[2 * c])
        for x in range(2):
            pass_on(l, 0, c, x, dot_nn(w_ref[l, :, COL_IN[0] : COL_IN[0] + 384], dqkv_ref[2 * c + x]), xhat, inv)

    def each(count, stage, l):
        for i in range(count):
            stage(l, i)

    def forward_layer(l, carry):
        each(chunks, time_forward, l)
        each(items, var_forward, l)
        each(chunks, tail_forward, l)
        return carry

    lax.fori_loop(0, layers, forward_layer, 0)
    for b in range(items):
        for v in range(4):
            lanes = slice(128 * (v % 2), 128 * (v % 2) + 128)
            out_ref[b, v] = h_ref[2 * b + v // 2, :, lanes].T.astype(BF)

    gacc_ref[...] = jnp.zeros_like(gacc_ref)
    gt_ref[...] = jnp.zeros_like(gt_ref)
    pacc_ref[...] = jnp.zeros_like(pacc_ref)

    def backward_layer(step, carry):
        l = layers - 1 - step
        ga_ref[...] = jnp.zeros_like(ga_ref)
        gdt_ref[...] = jnp.zeros_like(gdt_ref)
        each(chunks, feed_backward, l)
        each(chunks, token_backward, l)
        each(items, var_backward, l)
        each(chunks, time_backward, l)
        for k in range(4):
            gd_ref[128 * k : 128 * k + 128, :] = gdt_ref[:, 128 * k : 128 * k + 128].T
        for f in range(SHARDS):
            down = jnp.concatenate([gd_ref[32 * f + 8 * a : 32 * f + 8 * a + 8, :] for a in range(4)], axis=1)
            block = jnp.concatenate([ga_ref[8 * f : 8 * f + 8, :], down], axis=1)
            gbig_ref[l, f] = block.astype(BF)
        gains_rows = [jnp.sum(gacc_ref[l * 4 + k].T, axis=0, keepdims=True) for k in range(4)]
        sums = [
            jnp.sum(w_ref[l, :, COL_OUT[k] : COL_OUT[k] + 128].astype(F32) * ga_ref[:, COL_OUT[k] : COL_OUT[k] + 128], axis=0, keepdims=True)
            for k in range(2)
        ]
        sums.append(gains_rows[2])
        sums.append(jnp.sum(wd_ref[l].astype(F32) * gd_ref[...], axis=0, keepdims=True))
        for k in range(4):
            pacc_ref[0, l * 4 + k, 10:11, :] = gains_rows[k] / gains_ref[l, k : k + 1, :]
            pacc_ref[0, l * 4 + k, 11:12, :] = sums[k] / scales_ref[l, k : k + 1, :]
        return carry

    lax.fori_loop(0, layers, backward_layer, 0)

    for x in range(2):
        cls_sum = None
        for b in range(items):
            prompt_sum = None
            for v in range(4):
                lanes = slice(128 * (v % 2), 128 * (v % 2) + 128)
                tokscr_ref[4 * b + v] = g_ref[x, 2 * b + v // 2, :, lanes].T
                head = tokscr_ref[4 * b + v, 0:10, :]
                last = tokscr_ref[4 * b + v, 127:128, :]
                prompt_sum = head if prompt_sum is None else prompt_sum + head
                cls_sum = last if cls_sum is None else cls_sum + last
                if x == 0:
                    pgrad_ref[b, v] = tokscr_ref[4 * b + v, 10:127, :]
            pacc_ref[x, ids_ref[b], 0:10, :] += prompt_sum
        pacc_ref[x, 0, 12:13, :] = cls_sum

    for big_ref, small_ref, c in ((bigmine_ref, smallmine_ref, dp), (bigother_ref, smallother_ref, 1 - dp)):
        for rel in range(SHARDS):
            big_ref[rel % 4, rel // 4] = gbig_ref[c, me ^ rel]
        for block in range(16):
            if block < 8:
                pair = gt_ref[c, 16 * block : 16 * block + 16, :]
            else:
                pair = pacc_ref[block // 4 - 2, 4 * c + block % 4]
            lanes = slice(256 * (block % 4), 256 * (block % 4) + 256)
            small_ref[block // 4, :, lanes] = jnp.concatenate([pair[:8], pair[8:]], axis=1)


def call(kernel, name, out_shape, in_spaces, scratch, *operands, cost=None):
    spaces = {"v": pltpu.VMEM, "s": pltpu.SMEM}
    return pl.pallas_call(
        kernel,
        out_shape=out_shape,
        in_specs=[pl.BlockSpec(memory_space=spaces[space]) for space in in_spaces],
        out_specs=[pl.BlockSpec(memory_space=pltpu.VMEM)] * len(out_shape),
        scratch_shapes=scratch,
        compiler_params=pltpu.CompilerParams(vmem_limit_bytes=58 * 1024 * 1024),
        cost_estimate=cost,
        name=name,
    )(*operands)


def shape_of(shape, kind=F32):
    return jax.ShapeDtypeStruct(shape, kind)


def run_tower(split, *operands):
    half = [shape_of((4, 4, 8, COLS), BF)] * 2 + [shape_of((4, 8, 1024))] * 2
    return call(
        functools.partial(tower_kernel, split),
        "tower",
        [shape_of((2, 4, 128, 128), BF), shape_of((2, 4, 117, 128))] + half,
        "ss" + "v" * 16,
        [
            pltpu.VMEM((2, 128, COLS), F32),
            pltpu.VMEM((2, 128, COL_DOWN), BF),
            pltpu.VMEM((2, 512, 128), BF),
            pltpu.VMEM((2, COL_DOWN, 128), BF),
            pltpu.VMEM((2, 128, 512), BF),
            pltpu.VMEM((16, 128, 256), F32),
            pltpu.VMEM((8, 128, 128), F32),
            pltpu.VMEM((4, 128, 256), F32),
            pltpu.VMEM((2, 4, 128, 256), F32),
            pltpu.VMEM((8, 4, 128, 256), F32),
            pltpu.VMEM((8, 4, 1, 256), F32),
            pltpu.VMEM((2, 4, 384, 256), BF),
            pltpu.VMEM((2, 8, 128, 1024), BF),
            pltpu.VMEM((2, 4, 128, 256), BF),
            pltpu.VMEM((2, 4, 384, 256), BF),
            pltpu.VMEM((2, 2, 4, 8, 512), F32),
            pltpu.VMEM((2, 4, 128, 256), BF),
            pltpu.VMEM((2, 2, 4, 128, 512), BF),
            pltpu.VMEM((4, 128, 1024), BF),
            pltpu.VMEM((8, 128, 1024), BF),
            pltpu.VMEM((2, 4, 512, 256), BF),
            pltpu.VMEM((4, 1024, 256), BF),
            pltpu.VMEM((8, 384, 256), BF),
            pltpu.VMEM((8, 128, 256), BF),
            pltpu.VMEM((128, COL_DOWN), F32),
            pltpu.VMEM((512, 128), F32),
            pltpu.VMEM((2, 128, 128), F32),
            pltpu.VMEM((8, 128, 128), F32),
            pltpu.VMEM((2, SHARDS, 8, COLS), BF),
            pltpu.VMEM((2, 8, 16, 128), F32),
            pltpu.VMEM((16, 8, 512), F32),
            pltpu.VMEM((2, 4, 512, 256), BF),
            pltpu.VMEM((2, 4, 512, 256), BF),
            pltpu.VMEM((128, 512), F32),
        ],
        *operands,
        cost=pl.CostEstimate(flops=10**10, bytes_accessed=20 * 10**6, transcendentals=0),
    )


def pack_rows(attn_in, attn_out, feed_in, feed_out):
    layers, _, rows, _ = attn_in.shape
    down = feed_out.reshape(layers, 4, rows, 128)
    return jnp.concatenate(
        [attn_in[:, 0], attn_in[:, 1], attn_out[:, 0], attn_out[:, 1], feed_in] + [down[:, a] for a in range(4)], axis=2
    )


def unpack_rows(packed):
    layers, rows, _ = packed.shape
    attn_in = jnp.stack([packed[:, :, at : at + 384] for at in COL_IN], axis=1)
    attn_out = jnp.stack([packed[:, :, at : at + 128] for at in COL_OUT], axis=1)
    feed_in = packed[:, :, COL_FEED:COL_DOWN]
    feed_out = jnp.stack([packed[:, :, COL_DOWN + 128 * a : COL_DOWN + 128 * a + 128] for a in range(4)], axis=1)
    return attn_in, attn_out, feed_in, feed_out.reshape(layers, 4 * rows, 128)


def flip(array, axis, bit, size):
    return lax.ppermute(array, axis, [(i, i ^ (1 << bit)) for i in range(size)])


def swap(array, mask):
    return lax.ppermute(array, "fsdp", [(i, i ^ mask) for i in range(SHARDS)])


def gather_rows(attn_in, attn_out, feed_in, feed_out):
    row = call(pack_kernel, "pack", [shape_of((1, 8, COLS), BF)], "vvvv", [], attn_in, attn_out, feed_in, feed_out)[0]
    column = jnp.concatenate([row] + [swap(row, 4 * z) for z in range(1, 4)], axis=0)
    mine = [column] + [swap(column, xy) for xy in range(1, 4)]
    return mine + [flip(part, "dp", 0, 2) for part in mine]


def final_kernel(big_mine, big_other, small_mine, small_other, attn_in, attn_out, feed_in, feed_out, tokens, gains, scales,
                 prompt, cls, adjust_prompt, adjust_cls):
    dp = lax.axis_index("dp")
    for part, l in ((big_mine, dp), (big_other, 1 - dp)):
        for k in range(2):
            attn_in[l, k] = part[:, COL_IN[k] : COL_IN[k] + 384]
            attn_out[l, k] = part[:, COL_OUT[k] : COL_OUT[k] + 128]
        feed_in[l] = part[:, COL_FEED:COL_DOWN]
        for a in range(4):
            feed_out[l, 8 * a : 8 * a + 8, :] = part[:, COL_DOWN + 128 * a : COL_DOWN + 128 * a + 128]
    for c in range(2):
        parts = [slice(256 * k, 256 * k + 256) for k in range(16)]
        tiles = [jnp.where(dp == c, small_mine[:, part], small_other[:, part]) for part in parts]
        blocks = [jnp.concatenate([tile[:, :128], tile[:, 128:]], axis=0) for tile in tiles]
        for k in range(8):
            tokens[c, 16 * k : 16 * k + 16, :] = blocks[k]
        for k in range(4):
            for row in range(10):
                prompt[row, 4 * c + k : 4 * c + k + 1, :] = blocks[8 + k][row : row + 1]
                adjust_prompt[row, 4 * c + k : 4 * c + k + 1, :] = blocks[12 + k][row : row + 1]
            gains[c, k : k + 1, :] = blocks[8 + k][10:11]
            scales[c, k : k + 1, :] = blocks[8 + k][11:12]
        if c == 0:
            cls[...] = blocks[8][12:13]
            adjust_cls[...] = blocks[12][12:13]


def four(first, rest):
    return (first.astype(F32) + rest[0].astype(F32)) + (rest[1].astype(F32) + rest[2].astype(F32))


def reduce_all(big_mine, big_other, small_mine, small_other):
    big = (big_mine.astype(F32) + flip(big_other, "dp", 0, 2).astype(F32)).astype(BF)
    small = (small_mine + flip(small_other, "dp", 0, 2)).astype(BF)
    got = [swap(jnp.concatenate([big[xy], small], axis=2), xy) for xy in range(1, 4)]
    big = four(big[0], [part[:, :, :COLS] for part in got]).astype(BF)
    small = four(small, [part[:, :, COLS:] for part in got]).astype(BF)
    small = jnp.concatenate([small[at] for at in range(4)], axis=1)
    got = [swap(jnp.concatenate([big[z], small], axis=1), 4 * z) for z in range(1, 4)]
    big = four(big[0], [part[:, :COLS] for part in got])
    small = four(small, [part[:, COLS:] for part in got])
    return call(
        final_kernel, "final",
        [shape_of((2, 2, 8, 384)), shape_of((2, 2, 8, 128)), shape_of((2, 8, 1024)), shape_of((2, 32, 128)), shape_of((2, 128, 128)),
         shape_of((2, 4, 128)), shape_of((2, 4, 128)), shape_of((10, 8, 128)), shape_of((1, 128)), shape_of((10, 8, 128)), shape_of((1, 128))],
        "vvvv", [], big, flip(big, "dp", 0, 2), small, flip(small, "dp", 0, 2),
    )


def per_device(shard_count, patches, prompts, cls_token, attn_in, attn_out, feed_in, feed_out, token_operator,
               norm_gains, branch_scales, var_counts, dataset_ids, cotangent, adjust_cotangent):
    fast = shard_count == SHARDS
    if fast:
        gathered = gather_rows(attn_in, attn_out, feed_in, feed_out)
    else:
        whole_down = lax.all_gather(feed_out, "fsdp", axis=1, tiled=True)
        whole_down = whole_down.reshape(2, SHARDS, 4, 8, 128).transpose(0, 2, 1, 3, 4).reshape(2, 512, 128)
        rows = pack_rows(
            lax.all_gather(attn_in, "fsdp", axis=2, tiled=True),
            lax.all_gather(attn_out, "fsdp", axis=2, tiled=True),
            lax.all_gather(feed_in, "fsdp", axis=1, tiled=True),
            whole_down,
        )
        rows = rows.reshape(2, SHARDS, 8, COLS).transpose(1, 0, 2, 3)
        gathered = [rows[:, l].reshape(4, 4, 8, COLS)[:, xy] for l in range(2) for xy in range(4)]
    output, patch_grad, *sums = run_tower(
        fast, dataset_ids, var_counts, *gathered, token_operator, norm_gains, branch_scales, patches, prompts,
        cls_token.reshape(1, -1), cotangent, adjust_cotangent,
    )
    if fast:
        (attn_in_g, attn_out_g, feed_in_g, feed_out_g, token_g, gains_g, scales_g, prompt_g, cls_g, adjust_prompt_g,
         adjust_cls_g) = reduce_all(*sums)
        return (output, patch_grad, prompt_g.transpose(1, 0, 2), cls_g[0], attn_in_g, attn_out_g, feed_in_g, feed_out_g, token_g, gains_g,
                scales_g, adjust_prompt_g.transpose(1, 0, 2), adjust_cls_g[0])
    rows = jnp.stack(sums[:2]).transpose(0, 2, 1, 3, 4).astype(F32).reshape(2, 128, COLS)
    attn_in_g, attn_out_g, feed_in_g, feed_out_g = unpack_rows(rows)
    feed_out_g = feed_out_g.reshape(2, 4, SHARDS, 8, 128).transpose(0, 2, 1, 3, 4).reshape(2, 512, 128)
    matrices = (
        lax.psum_scatter(lax.psum(attn_in_g, "dp"), "fsdp", scatter_dimension=2, tiled=True),
        lax.psum_scatter(lax.psum(attn_out_g, "dp"), "fsdp", scatter_dimension=2, tiled=True),
        lax.psum_scatter(lax.psum(feed_in_g, "dp"), "fsdp", scatter_dimension=1, tiled=True),
        lax.psum_scatter(lax.psum(feed_out_g, "dp"), "fsdp", scatter_dimension=1, tiled=True),
    )
    small = lax.psum(jnp.stack(sums[2:]), ("dp", "fsdp"))
    small = small.reshape(2, 4, 8, 4, 2, 128).transpose(0, 1, 3, 4, 2, 5).reshape(2, 16, 16, 128)
    main, adjust = small[:, 8:12].reshape(8, 16, 128), small[:, 12:].reshape(8, 16, 128)
    return (output, patch_grad, main[:, :10], main[0, 12], *matrices, small[:, :8].reshape(2, 128, 128),
            main[:, 10].reshape(2, 4, 128), main[:, 11].reshape(2, 4, 128), adjust[:, :10], adjust[0, 12])


def solution(mesh):
    batch = P(("dp", "fsdp"), None, None, None)
    wide = P(None, None, "fsdp", None)
    tall = P(None, "fsdp", None)
    return jax.shard_map(
        functools.partial(per_device, mesh.shape["fsdp"]),
        mesh=mesh,
        in_specs=(batch, P(), P(), wide, wide, tall, tall, P(), P(), P(), P(), P(("dp", "fsdp")), batch, batch),
        out_specs=(batch, batch, P(), P(), wide, wide, tall, tall, P(), P(), P(), P(), P()),
        check_vma=False,
    )
```

```python
import functools

import jax
import jax.numpy as jnp
from jax import lax
from jax.experimental import pallas as pl
from jax.experimental.pallas import tpu as pltpu
from jax.sharding import PartitionSpec as P

HEADS = 8
EPSILON = 1e-05
NEG_FILL = -1000000000.0
BF = jnp.bfloat16
F32 = jnp.float32

COL_IN = (0, 384)
COL_OUT = (768, 896)
COL_FEED = 1024
COL_DOWN = 2048
COLS = 2560
SHARDS = 16
STEP_BITS = (2, 3, 0, 1)


def dot_nn(a, b):
    return lax.dot_general(a, b, (((1,), (0,)), ((), ())), preferred_element_type=F32)


def dot_nt(a, b):
    return lax.dot_general(a, b, (((1,), (1,)), ((), ())), preferred_element_type=F32)


def norm_cols(x):
    centered = x - jnp.mean(x, axis=0, keepdims=True)
    inv = lax.rsqrt(jnp.mean(centered * centered, axis=0, keepdims=True) + EPSILON)
    return centered * inv, inv


def norm_cols_back(dn, gain, xhat, inv):
    e = dn * gain
    both = e * xhat
    m1 = jnp.mean(e, axis=0, keepdims=True)
    m2 = jnp.mean(both, axis=0, keepdims=True)
    return inv * (e - m1 - xhat * m2), both


def fold(part):
    return part[:, :128] + part[:, 128:]


def pack_kernel(attn_in_ref, attn_out_ref, feed_in_ref, feed_out_ref, out_ref):
    l = lax.axis_index("dp")
    down = feed_out_ref[l].astype(F32)
    parts = [attn_in_ref[l, 0], attn_in_ref[l, 1], attn_out_ref[l, 0], attn_out_ref[l, 1], feed_in_ref[l]]
    parts = [part.astype(F32) for part in parts] + [down[8 * a : 8 * a + 8] for a in range(4)]
    out_ref[0] = jnp.concatenate(parts, axis=1).astype(BF)


def prepare_kernel(ids_ref, patches_ref, prompts_ref, cls_ref, cot_ref, adj_ref, turned_ref, tok_ref):
    for b in range(2):
        ident = ids_ref[b]
        for v in range(4):
            at = 4 * b + v
            lanes = slice(128 * (v % 2), 128 * (v % 2) + 128)
            tok_ref[at, 0:10, :] = prompts_ref[ident].astype(F32)
            tok_ref[at, 10:127, :] = patches_ref[b, v].astype(F32)
            tok_ref[at, 127:128, :] = cls_ref[...].astype(F32)
            turned_ref[0, 2 * b + v // 2, :, lanes] = tok_ref[at].T.astype(BF)
            turned_ref[1, 2 * b + v // 2, :, lanes] = cot_ref[b, v].T
            turned_ref[2, 2 * b + v // 2, :, lanes] = adj_ref[b, v].T


def tower_kernel(
    split,
    ids_ref, counts_ref, wmine0_ref, wmine1_ref, wmine2_ref, wmine3_ref, wother0_ref, wother1_ref, wother2_ref, wother3_ref,
    tok_ref, gains_ref, scales_ref, turned_ref,
    out_ref, pgrad_ref, bigmine_ref, bigother_ref, smallmine_ref, smallother_ref,
    stage_ref, w_ref, wd_ref, wt_ref, wdt_ref, colb_ref, tokscr_ref, h_ref, g_ref, xh_ref, inv_ref,
    qkvt_ref, pb_ref, ot_ref, qkvv_ref, pv_ref, ov_ref, pw_ref, qbd_ref, dob_ref, hid_ref, du_ref, dqkv_ref,
    dov_ref, ga_ref, gd_ref, gt_ref, gacc_ref, gbig_ref, pacc_ref, spread_ref, act_ref, slope_ref, gdt_ref, both_ref,
):
    dp = lax.axis_index("dp") if split else 0
    me = lax.axis_index("fsdp") if split else 0
    layers = 2
    chunks = 4
    items = 2

    for rel in range(SHARDS):
        rows = pl.ds(pl.multiple_of(8 * (me ^ rel), 8), 8)
        mine_ref = (wmine0_ref, wmine1_ref, wmine2_ref, wmine3_ref)[rel % 4]
        other_ref = (wother0_ref, wother1_ref, wother2_ref, wother3_ref)[rel % 4]
        stage_ref[dp, rows, :] = mine_ref[rel // 4].astype(F32)
        stage_ref[1 - dp, rows, :] = other_ref[rel // 4].astype(F32)
    for l in range(layers):
        for pair in range(SHARDS // 2):
            lo = stage_ref[l, 16 * pair : 16 * pair + 8, :]
            hi = stage_ref[l, 16 * pair + 8 : 16 * pair + 16, :]
            w_ref[l, 16 * pair : 16 * pair + 16, :] = jnp.concatenate([lo[:, :COL_DOWN], hi[:, :COL_DOWN]], axis=0).astype(BF)
            for half, part in enumerate((lo, hi)):
                base = 64 * pair + 32 * half
                wd_ref[l, base : base + 32, :] = jnp.concatenate(
                    [part[:, COL_DOWN + 128 * a : COL_DOWN + 128 * a + 128] for a in range(4)], axis=0
                ).astype(BF)
        for block in range(COL_DOWN // 128):
            wt_ref[l, 128 * block : 128 * block + 128, :] = w_ref[l, :, 128 * block : 128 * block + 128].T
        for block in range(4):
            wdt_ref[l, :, 128 * block : 128 * block + 128] = wd_ref[l, 128 * block : 128 * block + 128, :].T
        for k in range(4):
            for offset, rows in ((0, gains_ref), (4, scales_ref)):
                col = jnp.broadcast_to(rows[l, k : k + 1, :], (128, 128)).T
                colb_ref[l * 8 + offset + k, :, 0:128] = col
                colb_ref[l * 8 + offset + k, :, 128:256] = col

    h_ref[...] = turned_ref[0].astype(F32)
    g_ref[...] = turned_ref[1:3].astype(F32)

    head_row = lax.broadcasted_iota(jnp.int32, (8, 128), 0)
    head_col = lax.broadcasted_iota(jnp.int32, (8, 128), 1) // 16
    gather_heads = jnp.where(head_row == head_col, 1.0, 0.0).astype(BF)
    def spread_of(at, j):
        lanes = slice(128 * j, 128 * j + 128)
        return jnp.concatenate([jnp.broadcast_to(spread_ref[at, h : h + 1, lanes], (16, 128)) for h in range(HEADS)], axis=0)

    def head_sums(left, rights):
        return dot_nn(gather_heads, jnp.concatenate([(left * right).astype(BF) for right in rights], axis=1))

    def diag_heads(target_ref, at, rows):
        for head in range(HEADS):
            target_ref[at, 16 * head : 16 * head + 16, 128 * head : 128 * head + 128] = rows[16 * head : 16 * head + 16]

    both_ref[...] = jnp.zeros_like(both_ref)
    for half in range(2):
        both_ref[:, 128 * half : 128 * half + 128, 128 * half : 128 * half + 128] = tok_ref[...]
    qbd_ref[...] = jnp.zeros_like(qbd_ref)
    dob_ref[...] = jnp.zeros_like(dob_ref)

    def gain(l, k):
        return colb_ref[l * 8 + k]

    def scale(l, k):
        return colb_ref[l * 8 + 4 + k]

    def keep_norm(l, k, c, x):
        xhat, inv = norm_cols(x)
        xh_ref[l * 4 + k, c] = xhat
        inv_ref[l * 4 + k, c] = inv
        return (xhat * gain(l, k)).astype(BF)

    def time_forward(l, c):
        x = h_ref[c]
        n = keep_norm(l, 0, c, x)
        qkv = dot_nn(wt_ref[l, 0:384, :], n)
        queries = (qkv[:128] * 0.25).astype(BF)
        keys = qkv[128:256].astype(BF)
        values = qkv[256:].astype(BF)
        qkvt_ref[l, c, 0:128, :] = queries
        qkvt_ref[l, c, 128:256, :] = keys
        qkvt_ref[l, c, 256:384, :] = values
        for s in range(2):
            lanes = slice(128 * s, 128 * s + 128)
            at = 2 * (c % 2) + s
            diag_heads(qbd_ref, at, queries[:, lanes])
            key_rows = keys[:, lanes].T
            for hp in range(4):
                span = slice(256 * hp, 256 * hp + 256)
                rows = slice(32 * hp, 32 * hp + 32)
                scores = dot_nn(key_rows, qbd_ref[at, :, span])
                shifted = jnp.exp(scores - jnp.max(scores, axis=0, keepdims=True))
                prob = (shifted * (1.0 / jnp.sum(shifted, axis=0, keepdims=True))).astype(BF)
                pb_ref[l, 2 * c + s, :, span] = prob
                mixed = dot_nn(values[rows, lanes], prob)
                ot_ref[l, c, 32 * hp : 32 * hp + 16, lanes] = mixed[:16, :128].astype(BF)
                ot_ref[l, c, 32 * hp + 16 : 32 * hp + 32, lanes] = mixed[16:, 128:].astype(BF)
        branch = dot_nn(wt_ref[l, COL_OUT[0] : COL_OUT[0] + 128, :], ot_ref[l, c])
        h_ref[c] = x + scale(l, 0) * branch

    def var_forward(l, b):
        for cc in range(2):
            c = 2 * b + cc
            n = keep_norm(l, 1, c, h_ref[c])
            qkv = dot_nn(wt_ref[l, COL_IN[1] : COL_IN[1] + 384, :], n)
            qkvv_ref[l, c, 0:128, :] = (qkv[:128] * 0.25).astype(BF)
            qkvv_ref[l, c, 128:384, :] = qkv[128:].astype(BF)
        count = counts_ref[ids_ref[b]]

        def slot(first, i):
            lanes = slice(128 * (i % 2), 128 * (i % 2) + 128)
            return qkvv_ref[l, 2 * b + i // 2, first : first + 128, lanes].astype(F32)

        key_slots = [slot(128, j) for j in range(4)]
        value_slots = [slot(256, j) for j in range(4)]
        for i in range(4):
            scores = head_sums(slot(0, i), key_slots)
            parts = [scores[:, 128 * j : 128 * j + 128] for j in range(4)]
            parts = [jnp.where(jnp.full((8, 128), count, jnp.int32) > j, parts[j], NEG_FILL) for j in range(4)]
            top = jnp.maximum(jnp.maximum(parts[0], parts[1]), jnp.maximum(parts[2], parts[3]))
            shifted = [jnp.exp(part - top) for part in parts]
            total = 1.0 / ((shifted[0] + shifted[1]) + (shifted[2] + shifted[3]))
            prob = jnp.concatenate([part * total for part in shifted], axis=1)
            pv_ref[l, b, i] = prob
            spread_ref[4 * b + i] = prob.astype(BF).astype(F32)
            mixed = None
            for j in range(4):
                spread = spread_of(4 * b + i, j)
                pw_ref[l, b, i, :, 128 * j : 128 * j + 128] = spread.astype(BF)
                mixed = spread * value_slots[j] if mixed is None else mixed + spread * value_slots[j]
            lanes = slice(128 * (i % 2), 128 * (i % 2) + 128)
            ov_ref[l, 2 * b + i // 2, :, lanes] = mixed.astype(BF)
        for cc in range(2):
            c = 2 * b + cc
            branch = dot_nn(wt_ref[l, COL_OUT[1] : COL_OUT[1] + 128, :], ov_ref[l, c])
            h_ref[c] = h_ref[c] + scale(l, 1) * branch

    def tail_forward(l, c):
        x = h_ref[c]
        n = keep_norm(l, 2, c, x)
        x = x + scale(l, 2) * dot_nt(n, both_ref[l])
        n = keep_norm(l, 3, c, x)
        for z in range(4):
            rows = slice(128 * z, 128 * z + 128)
            gate = dot_nn(wt_ref[l, COL_FEED + 128 * z : COL_FEED + 128 * z + 128, :], n)
            up = dot_nn(wt_ref[l, COL_FEED + 512 + 128 * z : COL_FEED + 640 + 128 * z, :], n)
            sig = 0.5 * jnp.tanh(0.5 * gate) + 0.5
            act = gate * sig
            hid_ref[l, c, rows, :] = (act * up).astype(BF)
            act_ref[l, c, rows, :] = act.astype(BF)
            slope_ref[l, c, rows, :] = (up * (sig * (1.0 + gate * (1.0 - sig)))).astype(BF)
        h_ref[c] = x + scale(l, 3) * dot_nn(wdt_ref[l], hid_ref[l, c])

    def norm_of(l, k, c):
        xhat = xh_ref[l * 4 + k, c]
        return xhat, inv_ref[l * 4 + k, c], (xhat * gain(l, k)).astype(BF)

    def pass_on(l, k, c, x, dn, xhat, inv):
        back, both = norm_cols_back(dn, gain(l, k), xhat, inv)
        if x == 0:
            gacc_ref[l * 4 + k] += fold(both)
        g_ref[x, c] += back

    def feed_backward(l, c):
        xhat, inv, n = norm_of(l, 3, c)
        dz = [(scale(l, 3) * g_ref[x, c]).astype(BF) for x in range(2)]
        for z in range(4):
            rows = slice(128 * z, 128 * z + 128)
            act = act_ref[l, c, rows, :].astype(F32)
            slope = slope_ref[l, c, rows, :].astype(F32)
            for x in range(2):
                dhid = dot_nn(wd_ref[l, rows, :], dz[x])
                du_ref[2 * (c % 2) + x, 128 * z : 128 * z + 128, :] = (dhid * slope).astype(BF)
                du_ref[2 * (c % 2) + x, 512 + 128 * z : 640 + 128 * z, :] = (dhid * act).astype(BF)
        ga_ref[:, COL_FEED:COL_DOWN] += dot_nt(n, du_ref[2 * (c % 2)])
        gdt_ref[...] += dot_nt(dz[0], hid_ref[l, c])
        for x in range(2):
            dn = dot_nn(w_ref[l, :, COL_FEED:COL_DOWN], du_ref[2 * (c % 2) + x])
            pass_on(l, 3, c, x, dn, xhat, inv)

    def token_backward(l, c):
        xhat, inv, n = norm_of(l, 2, c)
        for x in range(2):
            dy = (scale(l, 2) * g_ref[x, c]).astype(BF)
            if x == 0:
                turned = jnp.concatenate([dy[:, :128].T, dy[:, 128:].T], axis=1)
                gt_ref[l] += dot_nn(turned, jnp.concatenate([n[:, :128], n[:, 128:]], axis=0))
            pass_on(l, 2, c, x, dot_nn(dy, both_ref[l]), xhat, inv)

    def var_backward(l, b):
        def slot(first, i):
            lanes = slice(128 * (i % 2), 128 * (i % 2) + 128)
            return qkvv_ref[l, 2 * b + i // 2, first : first + 128, lanes].astype(F32)

        for x in range(2):
            for cc in range(2):
                c = 2 * b + cc
                dt = (scale(l, 1) * g_ref[x, c]).astype(BF)
                dov_ref[4 * b + 2 * x + cc] = dot_nn(w_ref[l, :, COL_OUT[1] : COL_OUT[1] + 128], dt).astype(BF)
                if x == 0:
                    ga_ref[:, COL_OUT[1] : COL_OUT[1] + 128] += dot_nt(ov_ref[l, c], dt)
            value_slots = [slot(256, j) for j in range(4)]
            dkeys = [0.0] * 4
            dvalues = [0.0] * 4
            for i in range(4):
                lanes = slice(128 * (i % 2), 128 * (i % 2) + 128)
                grad = dov_ref[4 * b + 2 * x + i // 2, :, lanes].astype(F32)
                query = slot(0, i)
                prob = pv_ref[l, b, i]
                weighted = prob * head_sums(grad, value_slots)
                total = (weighted[:, :128] + weighted[:, 128:256]) + (weighted[:, 256:384] + weighted[:, 384:])
                ds = weighted - prob * jnp.concatenate([total] * 4, axis=1)
                spread_ref[8 * b + 4 * x + i] = ds.astype(BF).astype(F32)
                ds_slots = [spread_of(8 * b + 4 * x + i, j) for j in range(4)]
                terms = [ds_slots[j] * slot(128, j) for j in range(4)]
                dquery = (terms[0] + terms[1]) + (terms[2] + terms[3])
                for j in range(4):
                    dkeys[j] = dkeys[j] + ds_slots[j] * query
                    dvalues[j] = dvalues[j] + pw_ref[l, b, i, :, 128 * j : 128 * j + 128].astype(F32) * grad
                dqkv_ref[4 * b + 2 * x + i // 2, 0:128, lanes] = (dquery * 0.25).astype(BF)
            for j in range(4):
                lanes = slice(128 * (j % 2), 128 * (j % 2) + 128)
                dqkv_ref[4 * b + 2 * x + j // 2, 128:256, lanes] = dkeys[j].astype(BF)
                dqkv_ref[4 * b + 2 * x + j // 2, 256:384, lanes] = dvalues[j].astype(BF)
            for cc in range(2):
                c = 2 * b + cc
                xhat, inv, n = norm_of(l, 1, c)
                dqkv = dqkv_ref[4 * b + 2 * x + cc]
                if x == 0:
                    ga_ref[:, COL_IN[1] : COL_IN[1] + 384] += dot_nt(n, dqkv)
                pass_on(l, 1, c, x, dot_nn(w_ref[l, :, COL_IN[1] : COL_IN[1] + 384], dqkv), xhat, inv)

    def time_backward(l, c):
        xhat, inv, n = norm_of(l, 0, c)
        queries = qkvt_ref[l, c, 0:128, :]
        keys = qkvt_ref[l, c, 128:256, :]
        values = qkvt_ref[l, c, 256:384, :]
        grads = []
        for x in range(2):
            dt = (scale(l, 0) * g_ref[x, c]).astype(BF)
            grads.append(dot_nn(w_ref[l, :, COL_OUT[0] : COL_OUT[0] + 128], dt).astype(BF))
            if x == 0:
                ga_ref[:, COL_OUT[0] : COL_OUT[0] + 128] += dot_nt(ot_ref[l, c], dt)
        for s in range(2):
            lanes = slice(128 * s, 128 * s + 128)
            at = 2 * (c % 2) + s
            diag_heads(qbd_ref, at, queries[:, lanes])
            value_rows = values[:, lanes].T
            for x in range(2):
                diag_heads(dob_ref, 2 * at + x, grads[x][:, lanes])
            for hp in range(4):
                span = slice(256 * hp, 256 * hp + 256)
                rows = slice(32 * hp, 32 * hp + 32)
                prob_bf = pb_ref[l, 2 * c + s, :, span]
                prob = prob_bf.astype(F32)
                for x in range(2):
                    weighted = prob * dot_nn(value_rows, dob_ref[2 * at + x, :, span])
                    ds = (weighted - prob * jnp.sum(weighted, axis=0, keepdims=True)).astype(BF)
                    dvalue = dot_nt(dob_ref[2 * at + x, rows, span], prob_bf)
                    dquery = dot_nn(keys[rows, lanes], ds) * 0.25
                    dkey = dot_nt(qbd_ref[at, rows, span], ds)
                    dqkv_ref[2 * c + x, 32 * hp : 32 * hp + 16, lanes] = dquery[:16, :128].astype(BF)
                    dqkv_ref[2 * c + x, 32 * hp + 16 : 32 * hp + 32, lanes] = dquery[16:, 128:].astype(BF)
                    dqkv_ref[2 * c + x, 128 + 32 * hp : 160 + 32 * hp, lanes] = dkey.astype(BF)
                    dqkv_ref[2 * c + x, 256 + 32 * hp : 288 + 32 * hp, lanes] = dvalue.astype(BF)
        ga_ref[:, COL_IN[0] : COL_IN[0] + 384] += dot_nt(n, dqkv_ref[2 * c])
        for x in range(2):
            pass_on(l, 0, c, x, dot_nn(w_ref[l, :, COL_IN[0] : COL_IN[0] + 384], dqkv_ref[2 * c + x]), xhat, inv)

    def each(count, stage, l):
        for i in range(count):
            stage(l, i)

    def forward_layer(l, carry):
        each(chunks, time_forward, l)
        each(items, var_forward, l)
        each(chunks, tail_forward, l)
        return carry

    lax.fori_loop(0, layers, forward_layer, 0)
    for b in range(items):
        for v in range(4):
            lanes = slice(128 * (v % 2), 128 * (v % 2) + 128)
            out_ref[b, v] = h_ref[2 * b + v // 2, :, lanes].T.astype(BF)

    gacc_ref[...] = jnp.zeros_like(gacc_ref)
    gt_ref[...] = jnp.zeros_like(gt_ref)
    pacc_ref[...] = jnp.zeros_like(pacc_ref)

    def backward_layer(step, carry):
        l = layers - 1 - step
        ga_ref[...] = jnp.zeros_like(ga_ref)
        gdt_ref[...] = jnp.zeros_like(gdt_ref)
        each(chunks, feed_backward, l)
        each(chunks, token_backward, l)
        each(items, var_backward, l)
        each(chunks, time_backward, l)
        for k in range(4):
            gd_ref[128 * k : 128 * k + 128, :] = gdt_ref[:, 128 * k : 128 * k + 128].T
        for f in range(SHARDS):
            down = jnp.concatenate([gd_ref[32 * f + 8 * a : 32 * f + 8 * a + 8, :] for a in range(4)], axis=1)
            block = jnp.concatenate([ga_ref[8 * f : 8 * f + 8, :], down], axis=1)
            gbig_ref[l, f] = block.astype(BF)
        gains_rows = [jnp.sum(gacc_ref[l * 4 + k].T, axis=0, keepdims=True) for k in range(4)]
        sums = [
            jnp.sum(w_ref[l, :, COL_OUT[k] : COL_OUT[k] + 128].astype(F32) * ga_ref[:, COL_OUT[k] : COL_OUT[k] + 128], axis=0, keepdims=True)
            for k in range(2)
        ]
        sums.append(gains_rows[2])
        sums.append(jnp.sum(wd_ref[l].astype(F32) * gd_ref[...], axis=0, keepdims=True))
        for k in range(4):
            pacc_ref[0, l * 4 + k, 10:11, :] = gains_rows[k] / gains_ref[l, k : k + 1, :]
            pacc_ref[0, l * 4 + k, 11:12, :] = sums[k] / scales_ref[l, k : k + 1, :]
        return carry

    lax.fori_loop(0, layers, backward_layer, 0)

    for x in range(2):
        cls_sum = None
        for b in range(items):
            prompt_sum = None
            for v in range(4):
                lanes = slice(128 * (v % 2), 128 * (v % 2) + 128)
                tokscr_ref[4 * b + v] = g_ref[x, 2 * b + v // 2, :, lanes].T
                head = tokscr_ref[4 * b + v, 0:10, :]
                last = tokscr_ref[4 * b + v, 127:128, :]
                prompt_sum = head if prompt_sum is None else prompt_sum + head
                cls_sum = last if cls_sum is None else cls_sum + last
                if x == 0:
                    pgrad_ref[b, v] = tokscr_ref[4 * b + v, 10:127, :]
            pacc_ref[x, ids_ref[b], 0:10, :] += prompt_sum
        pacc_ref[x, 0, 12:13, :] = cls_sum

    for big_ref, small_ref, c in ((bigmine_ref, smallmine_ref, dp), (bigother_ref, smallother_ref, 1 - dp)):
        for rel in range(SHARDS):
            big_ref[rel % 4, rel // 4] = gbig_ref[c, me ^ rel]
        for block in range(16):
            if block < 8:
                pair = gt_ref[c, 16 * block : 16 * block + 16, :]
            else:
                pair = pacc_ref[block // 4 - 2, 4 * c + block % 4]
            lanes = slice(256 * (block % 4), 256 * (block % 4) + 256)
            small_ref[block // 4, :, lanes] = jnp.concatenate([pair[:8], pair[8:]], axis=1)


def call(kernel, name, out_shape, in_spaces, scratch, *operands, cost=None):
    spaces = {"v": pltpu.VMEM, "s": pltpu.SMEM}
    return pl.pallas_call(
        kernel,
        out_shape=out_shape,
        in_specs=[pl.BlockSpec(memory_space=spaces[space]) for space in in_spaces],
        out_specs=[pl.BlockSpec(memory_space=pltpu.VMEM)] * len(out_shape),
        scratch_shapes=scratch,
        compiler_params=pltpu.CompilerParams(vmem_limit_bytes=58 * 1024 * 1024),
        cost_estimate=cost,
        name=name,
    )(*operands)


def shape_of(shape, kind=F32):
    return jax.ShapeDtypeStruct(shape, kind)


def run_tower(split, *operands):
    half = [shape_of((4, 4, 8, COLS), BF)] * 2 + [shape_of((4, 8, 1024))] * 2
    return call(
        functools.partial(tower_kernel, split),
        "tower",
        [shape_of((2, 4, 128, 128), BF), shape_of((2, 4, 117, 128))] + half,
        "ss" + "v" * 12,
        [
            pltpu.VMEM((2, 128, COLS), F32),
            pltpu.VMEM((2, 128, COL_DOWN), BF),
            pltpu.VMEM((2, 512, 128), BF),
            pltpu.VMEM((2, COL_DOWN, 128), BF),
            pltpu.VMEM((2, 128, 512), BF),
            pltpu.VMEM((16, 128, 256), F32),
            pltpu.VMEM((8, 128, 128), F32),
            pltpu.VMEM((4, 128, 256), F32),
            pltpu.VMEM((2, 4, 128, 256), F32),
            pltpu.VMEM((8, 4, 128, 256), F32),
            pltpu.VMEM((8, 4, 1, 256), F32),
            pltpu.VMEM((2, 4, 384, 256), BF),
            pltpu.VMEM((2, 8, 128, 1024), BF),
            pltpu.VMEM((2, 4, 128, 256), BF),
            pltpu.VMEM((2, 4, 384, 256), BF),
            pltpu.VMEM((2, 2, 4, 8, 512), F32),
            pltpu.VMEM((2, 4, 128, 256), BF),
            pltpu.VMEM((2, 2, 4, 128, 512), BF),
            pltpu.VMEM((4, 128, 1024), BF),
            pltpu.VMEM((8, 128, 1024), BF),
            pltpu.VMEM((2, 4, 512, 256), BF),
            pltpu.VMEM((4, 1024, 256), BF),
            pltpu.VMEM((8, 384, 256), BF),
            pltpu.VMEM((8, 128, 256), BF),
            pltpu.VMEM((128, COL_DOWN), F32),
            pltpu.VMEM((512, 128), F32),
            pltpu.VMEM((2, 128, 128), F32),
            pltpu.VMEM((8, 128, 128), F32),
            pltpu.VMEM((2, SHARDS, 8, COLS), BF),
            pltpu.VMEM((2, 8, 16, 128), F32),
            pltpu.VMEM((16, 8, 512), F32),
            pltpu.VMEM((2, 4, 512, 256), BF),
            pltpu.VMEM((2, 4, 512, 256), BF),
            pltpu.VMEM((128, 512), F32),
            pltpu.VMEM((2, 256, 256), BF),
        ],
        *operands,
        cost=pl.CostEstimate(flops=10**10, bytes_accessed=20 * 10**6, transcendentals=0),
    )


def pack_rows(attn_in, attn_out, feed_in, feed_out):
    layers, _, rows, _ = attn_in.shape
    down = feed_out.reshape(layers, 4, rows, 128)
    return jnp.concatenate(
        [attn_in[:, 0], attn_in[:, 1], attn_out[:, 0], attn_out[:, 1], feed_in] + [down[:, a] for a in range(4)], axis=2
    )


def unpack_rows(packed):
    layers, rows, _ = packed.shape
    attn_in = jnp.stack([packed[:, :, at : at + 384] for at in COL_IN], axis=1)
    attn_out = jnp.stack([packed[:, :, at : at + 128] for at in COL_OUT], axis=1)
    feed_in = packed[:, :, COL_FEED:COL_DOWN]
    feed_out = jnp.stack([packed[:, :, COL_DOWN + 128 * a : COL_DOWN + 128 * a + 128] for a in range(4)], axis=1)
    return attn_in, attn_out, feed_in, feed_out.reshape(layers, 4 * rows, 128)


def flip(array, axis, bit, size):
    return lax.ppermute(array, axis, [(i, i ^ (1 << bit)) for i in range(size)])


def swap(array, mask):
    return lax.ppermute(array, "fsdp", [(i, i ^ mask) for i in range(SHARDS)])


def gather_rows(attn_in, attn_out, feed_in, feed_out, turned):
    row = call(pack_kernel, "pack", [shape_of((1, 8, COLS), BF)], "vvvv", [], attn_in, attn_out, feed_in, feed_out)[0]
    column = jnp.concatenate([row] + [swap(row, 4 * z) for z in range(1, 4)], axis=0)
    mine = [column] + [swap(column, xy) for xy in range(1, 4)]
    mine, turned = lax.optimization_barrier((mine, turned))
    return mine + [flip(part, "dp", 0, 2) for part in mine], turned


def final_kernel(big_mine, big_other, small_mine, small_other, attn_in, attn_out, feed_in, feed_out, tokens, gains, scales,
                 prompt, cls, adjust_prompt, adjust_cls):
    dp = lax.axis_index("dp")
    for part, l in ((big_mine, dp), (big_other, 1 - dp)):
        for k in range(2):
            attn_in[l, k] = part[:, COL_IN[k] : COL_IN[k] + 384]
            attn_out[l, k] = part[:, COL_OUT[k] : COL_OUT[k] + 128]
        feed_in[l] = part[:, COL_FEED:COL_DOWN]
        for a in range(4):
            feed_out[l, 8 * a : 8 * a + 8, :] = part[:, COL_DOWN + 128 * a : COL_DOWN + 128 * a + 128]
    for c in range(2):
        parts = [slice(256 * k, 256 * k + 256) for k in range(16)]
        tiles = [jnp.where(dp == c, small_mine[:, part], small_other[:, part]) for part in parts]
        blocks = [jnp.concatenate([tile[:, :128], tile[:, 128:]], axis=0) for tile in tiles]
        for k in range(8):
            tokens[c, 16 * k : 16 * k + 16, :] = blocks[k]
        for k in range(4):
            for row in range(10):
                prompt[row, 4 * c + k : 4 * c + k + 1, :] = blocks[8 + k][row : row + 1]
                adjust_prompt[row, 4 * c + k : 4 * c + k + 1, :] = blocks[12 + k][row : row + 1]
            gains[c, k : k + 1, :] = blocks[8 + k][10:11]
            scales[c, k : k + 1, :] = blocks[8 + k][11:12]
        if c == 0:
            cls[...] = blocks[8][12:13]
            adjust_cls[...] = blocks[12][12:13]


def four(first, rest):
    return (first.astype(F32) + rest[0].astype(F32)) + (rest[1].astype(F32) + rest[2].astype(F32))


def reduce_all(big_mine, big_other, small_mine, small_other):
    big = (big_mine.astype(F32) + flip(big_other, "dp", 0, 2).astype(F32)).astype(BF)
    small = (small_mine + flip(small_other, "dp", 0, 2)).astype(BF)
    got = [swap(jnp.concatenate([big[xy], small], axis=2), xy) for xy in range(1, 4)]
    big = four(big[0], [part[:, :, :COLS] for part in got]).astype(BF)
    small = four(small, [part[:, :, COLS:] for part in got]).astype(BF)
    small = jnp.concatenate([small[at] for at in range(4)], axis=1)
    got = [swap(jnp.concatenate([big[z], small], axis=1), 4 * z) for z in range(1, 4)]
    big = four(big[0], [part[:, :COLS] for part in got])
    small = four(small, [part[:, COLS:] for part in got])
    return call(
        final_kernel, "final",
        [shape_of((2, 2, 8, 384)), shape_of((2, 2, 8, 128)), shape_of((2, 8, 1024)), shape_of((2, 32, 128)), shape_of((2, 128, 128)),
         shape_of((2, 4, 128)), shape_of((2, 4, 128)), shape_of((10, 8, 128)), shape_of((1, 128)), shape_of((10, 8, 128)), shape_of((1, 128))],
        "vvvv", [], big, flip(big, "dp", 0, 2), small, flip(small, "dp", 0, 2),
    )


def per_device(shard_count, patches, prompts, cls_token, attn_in, attn_out, feed_in, feed_out, token_operator,
               norm_gains, branch_scales, var_counts, dataset_ids, cotangent, adjust_cotangent):
    fast = shard_count == SHARDS
    turned = call(
        prepare_kernel, "prepare", [shape_of((3, 4, 128, 256), BF)], "svvvvv", [pltpu.VMEM((8, 128, 128), F32)],
        dataset_ids, patches, prompts, cls_token.reshape(1, -1), cotangent, adjust_cotangent,
        cost=pl.CostEstimate(flops=10**6, bytes_accessed=8 * 10**6, transcendentals=0),
    )[0]
    if fast:
        gathered, turned = gather_rows(attn_in, attn_out, feed_in, feed_out, turned)
    else:
        whole_down = lax.all_gather(feed_out, "fsdp", axis=1, tiled=True)
        whole_down = whole_down.reshape(2, SHARDS, 4, 8, 128).transpose(0, 2, 1, 3, 4).reshape(2, 512, 128)
        rows = pack_rows(
            lax.all_gather(attn_in, "fsdp", axis=2, tiled=True),
            lax.all_gather(attn_out, "fsdp", axis=2, tiled=True),
            lax.all_gather(feed_in, "fsdp", axis=1, tiled=True),
            whole_down,
        )
        rows = rows.reshape(2, SHARDS, 8, COLS).transpose(1, 0, 2, 3)
        gathered = [rows[:, l].reshape(4, 4, 8, COLS)[:, xy] for l in range(2) for xy in range(4)]
    output, patch_grad, *sums = run_tower(
        fast, dataset_ids, var_counts, *gathered, token_operator, norm_gains, branch_scales, turned
    )
    if fast:
        (attn_in_g, attn_out_g, feed_in_g, feed_out_g, token_g, gains_g, scales_g, prompt_g, cls_g, adjust_prompt_g,
         adjust_cls_g) = reduce_all(*sums)
        return (output, patch_grad, prompt_g.transpose(1, 0, 2), cls_g[0], attn_in_g, attn_out_g, feed_in_g, feed_out_g, token_g, gains_g,
                scales_g, adjust_prompt_g.transpose(1, 0, 2), adjust_cls_g[0])
    rows = jnp.stack(sums[:2]).transpose(0, 2, 1, 3, 4).astype(F32).reshape(2, 128, COLS)
    attn_in_g, attn_out_g, feed_in_g, feed_out_g = unpack_rows(rows)
    feed_out_g = feed_out_g.reshape(2, 4, SHARDS, 8, 128).transpose(0, 2, 1, 3, 4).reshape(2, 512, 128)
    matrices = (
        lax.psum_scatter(lax.psum(attn_in_g, "dp"), "fsdp", scatter_dimension=2, tiled=True),
        lax.psum_scatter(lax.psum(attn_out_g, "dp"), "fsdp", scatter_dimension=2, tiled=True),
        lax.psum_scatter(lax.psum(feed_in_g, "dp"), "fsdp", scatter_dimension=1, tiled=True),
        lax.psum_scatter(lax.psum(feed_out_g, "dp"), "fsdp", scatter_dimension=1, tiled=True),
    )
    small = lax.psum(jnp.stack(sums[2:]), ("dp", "fsdp"))
    small = small.reshape(2, 4, 8, 4, 2, 128).transpose(0, 1, 3, 4, 2, 5).reshape(2, 16, 16, 128)
    main, adjust = small[:, 8:12].reshape(8, 16, 128), small[:, 12:].reshape(8, 16, 128)
    return (output, patch_grad, main[:, :10], main[0, 12], *matrices, small[:, :8].reshape(2, 128, 128),
            main[:, 10].reshape(2, 4, 128), main[:, 11].reshape(2, 4, 128), adjust[:, :10], adjust[0, 12])


def solution(mesh):
    batch = P(("dp", "fsdp"), None, None, None)
    wide = P(None, None, "fsdp", None)
    tall = P(None, "fsdp", None)
    return jax.shard_map(
        functools.partial(per_device, mesh.shape["fsdp"]),
        mesh=mesh,
        in_specs=(batch, P(), P(), wide, wide, tall, tall, P(), P(), P(), P(), P(("dp", "fsdp")), batch, batch),
        out_specs=(batch, batch, P(), P(), wide, wide, tall, tall, P(), P(), P(), P(), P()),
        check_vma=False,
    )
```

```python
import functools

import jax
import jax.numpy as jnp
from jax import lax
from jax.experimental import pallas as pl
from jax.experimental.pallas import tpu as pltpu
from jax.sharding import PartitionSpec as P

HEADS = 8
EPSILON = 1e-05
NEG_FILL = -1000000000.0
BF = jnp.bfloat16
F32 = jnp.float32

COL_IN = (0, 384)
COL_OUT = (768, 896)
COL_FEED = 1024
COL_DOWN = 2048
COLS = 2560
SHARDS = 16
STEP_BITS = (2, 3, 0, 1)


def dot_nn(a, b):
    return lax.dot_general(a, b, (((1,), (0,)), ((), ())), preferred_element_type=F32)


def dot_nt(a, b):
    return lax.dot_general(a, b, (((1,), (1,)), ((), ())), preferred_element_type=F32)


def norm_cols(x):
    centered = x - jnp.mean(x, axis=0, keepdims=True)
    inv = lax.rsqrt(jnp.mean(centered * centered, axis=0, keepdims=True) + EPSILON)
    return centered * inv, inv


def norm_cols_back(dn, gain, xhat, inv):
    e = dn * gain
    both = e * xhat
    m1 = jnp.mean(e, axis=0, keepdims=True)
    m2 = jnp.mean(both, axis=0, keepdims=True)
    return inv * (e - m1 - xhat * m2), both


def fold(part):
    return part[:, :128] + part[:, 128:]


def pack_kernel(attn_in_ref, attn_out_ref, feed_in_ref, feed_out_ref, out_ref):
    l = lax.axis_index("dp")
    down = feed_out_ref[l].astype(F32)
    parts = [attn_in_ref[l, 0], attn_in_ref[l, 1], attn_out_ref[l, 0], attn_out_ref[l, 1], feed_in_ref[l]]
    parts = [part.astype(F32) for part in parts] + [down[8 * a : 8 * a + 8] for a in range(4)]
    out_ref[0] = jnp.concatenate(parts, axis=1).astype(BF)


def prepare_kernel(ids_ref, patches_ref, prompts_ref, cls_ref, cot_ref, adj_ref, turned_ref, tok_ref):
    for b in range(2):
        ident = ids_ref[b]
        for v in range(4):
            at = 4 * b + v
            lanes = slice(128 * (v % 2), 128 * (v % 2) + 128)
            tok_ref[at, 0:10, :] = prompts_ref[ident].astype(F32)
            tok_ref[at, 10:127, :] = patches_ref[b, v].astype(F32)
            tok_ref[at, 127:128, :] = cls_ref[...].astype(F32)
            turned_ref[0, 2 * b + v // 2, :, lanes] = tok_ref[at].T.astype(BF)
            turned_ref[1, 2 * b + v // 2, :, lanes] = cot_ref[b, v].T
            turned_ref[2, 2 * b + v // 2, :, lanes] = adj_ref[b, v].T


def leave_kernel(last_ref, gradient_ref, out_ref, pgrad_ref, tok_ref):
    for b in range(2):
        for v in range(4):
            lanes = slice(128 * (v % 2), 128 * (v % 2) + 128)
            out_ref[b, v] = last_ref[2 * b + v // 2, :, lanes].T
            tok_ref[4 * b + v] = gradient_ref[2 * b + v // 2, :, lanes].T
            pgrad_ref[b, v] = tok_ref[4 * b + v, 10:127, :]


def tower_kernel(
    split,
    ids_ref, counts_ref, wmine0_ref, wmine1_ref, wmine2_ref, wmine3_ref, wother0_ref, wother1_ref, wother2_ref, wother3_ref,
    tok_ref, gains_ref, scales_ref, turned_ref,
    last_ref, gradient_ref, bigmine_ref, bigother_ref, smallmine_ref, smallother_ref,
    stage_ref, w_ref, wd_ref, wt_ref, wdt_ref, colb_ref, tokscr_ref, h_ref, g_ref, xh_ref, inv_ref,
    qkvt_ref, pb_ref, ot_ref, qkvv_ref, pv_ref, ov_ref, pw_ref, qbd_ref, dob_ref, hid_ref, du_ref, dqkv_ref,
    dov_ref, ga_ref, gd_ref, gt_ref, gacc_ref, gbig_ref, pacc_ref, spread_ref, act_ref, slope_ref, gdt_ref, both_ref,
):
    dp = lax.axis_index("dp") if split else 0
    me = lax.axis_index("fsdp") if split else 0
    layers = 2
    chunks = 4
    items = 2

    for rel in range(SHARDS):
        rows = pl.ds(pl.multiple_of(8 * (me ^ rel), 8), 8)
        mine_ref = (wmine0_ref, wmine1_ref, wmine2_ref, wmine3_ref)[rel % 4]
        other_ref = (wother0_ref, wother1_ref, wother2_ref, wother3_ref)[rel % 4]
        stage_ref[dp, rows, :] = mine_ref[rel // 4].astype(F32)
        stage_ref[1 - dp, rows, :] = other_ref[rel // 4].astype(F32)
    for l in range(layers):
        for pair in range(SHARDS // 2):
            lo = stage_ref[l, 16 * pair : 16 * pair + 8, :]
            hi = stage_ref[l, 16 * pair + 8 : 16 * pair + 16, :]
            w_ref[l, 16 * pair : 16 * pair + 16, :] = jnp.concatenate([lo[:, :COL_DOWN], hi[:, :COL_DOWN]], axis=0).astype(BF)
            for half, part in enumerate((lo, hi)):
                base = 64 * pair + 32 * half
                wd_ref[l, base : base + 32, :] = jnp.concatenate(
                    [part[:, COL_DOWN + 128 * a : COL_DOWN + 128 * a + 128] for a in range(4)], axis=0
                ).astype(BF)
        for block in range(COL_DOWN // 128):
            wt_ref[l, 128 * block : 128 * block + 128, :] = w_ref[l, :, 128 * block : 128 * block + 128].T
        for block in range(4):
            wdt_ref[l, :, 128 * block : 128 * block + 128] = wd_ref[l, 128 * block : 128 * block + 128, :].T
        for k in range(4):
            for offset, rows in ((0, gains_ref), (4, scales_ref)):
                col = jnp.broadcast_to(rows[l, k : k + 1, :], (128, 128)).T
                colb_ref[l * 8 + offset + k, :, 0:128] = col
                colb_ref[l * 8 + offset + k, :, 128:256] = col

    h_ref[...] = turned_ref[0].astype(F32)
    g_ref[...] = turned_ref[1:3].astype(F32)

    head_row = lax.broadcasted_iota(jnp.int32, (8, 128), 0)
    head_col = lax.broadcasted_iota(jnp.int32, (8, 128), 1) // 16
    gather_heads = jnp.where(head_row == head_col, 1.0, 0.0).astype(BF)
    def spread_of(at, j):
        lanes = slice(128 * j, 128 * j + 128)
        return jnp.concatenate([jnp.broadcast_to(spread_ref[at, h : h + 1, lanes], (16, 128)) for h in range(HEADS)], axis=0)

    def head_sums(left, rights):
        return dot_nn(gather_heads, jnp.concatenate([(left * right).astype(BF) for right in rights], axis=1))

    def diag_heads(target_ref, at, rows):
        for head in range(HEADS):
            target_ref[at, 16 * head : 16 * head + 16, 128 * head : 128 * head + 128] = rows[16 * head : 16 * head + 16]

    both_ref[...] = jnp.zeros_like(both_ref)
    for half in range(2):
        both_ref[:, 128 * half : 128 * half + 128, 128 * half : 128 * half + 128] = tok_ref[...]
    qbd_ref[...] = jnp.zeros_like(qbd_ref)
    dob_ref[...] = jnp.zeros_like(dob_ref)

    def gain(l, k):
        return colb_ref[l * 8 + k]

    def scale(l, k):
        return colb_ref[l * 8 + 4 + k]

    def keep_norm(l, k, c, x):
        xhat, inv = norm_cols(x)
        xh_ref[l * 4 + k, c] = xhat
        inv_ref[l * 4 + k, c] = inv
        return (xhat * gain(l, k)).astype(BF)

    def time_forward(l, c):
        x = h_ref[c]
        n = keep_norm(l, 0, c, x)
        qkv = dot_nn(wt_ref[l, 0:384, :], n)
        queries = (qkv[:128] * 0.25).astype(BF)
        keys = qkv[128:256].astype(BF)
        values = qkv[256:].astype(BF)
        qkvt_ref[l, c, 0:128, :] = queries
        qkvt_ref[l, c, 128:256, :] = keys
        qkvt_ref[l, c, 256:384, :] = values
        for s in range(2):
            lanes = slice(128 * s, 128 * s + 128)
            at = 2 * (c % 2) + s
            diag_heads(qbd_ref, at, queries[:, lanes])
            key_rows = keys[:, lanes].T
            for hp in range(4):
                span = slice(256 * hp, 256 * hp + 256)
                rows = slice(32 * hp, 32 * hp + 32)
                scores = dot_nn(key_rows, qbd_ref[at, :, span])
                shifted = jnp.exp(scores - jnp.max(scores, axis=0, keepdims=True))
                prob = (shifted * (1.0 / jnp.sum(shifted, axis=0, keepdims=True))).astype(BF)
                pb_ref[l, 2 * c + s, :, span] = prob
                mixed = dot_nn(values[rows, lanes], prob)
                ot_ref[l, c, 32 * hp : 32 * hp + 16, lanes] = mixed[:16, :128].astype(BF)
                ot_ref[l, c, 32 * hp + 16 : 32 * hp + 32, lanes] = mixed[16:, 128:].astype(BF)
        branch = dot_nn(wt_ref[l, COL_OUT[0] : COL_OUT[0] + 128, :], ot_ref[l, c])
        h_ref[c] = x + scale(l, 0) * branch

    def var_forward(l, b):
        for cc in range(2):
            c = 2 * b + cc
            n = keep_norm(l, 1, c, h_ref[c])
            qkv = dot_nn(wt_ref[l, COL_IN[1] : COL_IN[1] + 384, :], n)
            qkvv_ref[l, c, 0:128, :] = (qkv[:128] * 0.25).astype(BF)
            qkvv_ref[l, c, 128:384, :] = qkv[128:].astype(BF)
        count = counts_ref[ids_ref[b]]

        def slot(first, i):
            lanes = slice(128 * (i % 2), 128 * (i % 2) + 128)
            return qkvv_ref[l, 2 * b + i // 2, first : first + 128, lanes].astype(F32)

        key_slots = [slot(128, j) for j in range(4)]
        value_slots = [slot(256, j) for j in range(4)]
        for i in range(4):
            scores = head_sums(slot(0, i), key_slots)
            parts = [scores[:, 128 * j : 128 * j + 128] for j in range(4)]
            parts = [jnp.where(jnp.full((8, 128), count, jnp.int32) > j, parts[j], NEG_FILL) for j in range(4)]
            top = jnp.maximum(jnp.maximum(parts[0], parts[1]), jnp.maximum(parts[2], parts[3]))
            shifted = [jnp.exp(part - top) for part in parts]
            total = 1.0 / ((shifted[0] + shifted[1]) + (shifted[2] + shifted[3]))
            prob = jnp.concatenate([part * total for part in shifted], axis=1)
            pv_ref[l, b, i] = prob
            spread_ref[4 * b + i] = prob.astype(BF).astype(F32)
            mixed = None
            for j in range(4):
                spread = spread_of(4 * b + i, j)
                pw_ref[l, b, i, :, 128 * j : 128 * j + 128] = spread.astype(BF)
                mixed = spread * value_slots[j] if mixed is None else mixed + spread * value_slots[j]
            lanes = slice(128 * (i % 2), 128 * (i % 2) + 128)
            ov_ref[l, 2 * b + i // 2, :, lanes] = mixed.astype(BF)
        for cc in range(2):
            c = 2 * b + cc
            branch = dot_nn(wt_ref[l, COL_OUT[1] : COL_OUT[1] + 128, :], ov_ref[l, c])
            h_ref[c] = h_ref[c] + scale(l, 1) * branch

    def tail_forward(l, c):
        x = h_ref[c]
        n = keep_norm(l, 2, c, x)
        x = x + scale(l, 2) * dot_nt(n, both_ref[l])
        n = keep_norm(l, 3, c, x)
        for z in range(4):
            rows = slice(128 * z, 128 * z + 128)
            gate = dot_nn(wt_ref[l, COL_FEED + 128 * z : COL_FEED + 128 * z + 128, :], n)
            up = dot_nn(wt_ref[l, COL_FEED + 512 + 128 * z : COL_FEED + 640 + 128 * z, :], n)
            sig = 0.5 * jnp.tanh(0.5 * gate) + 0.5
            act = gate * sig
            hid_ref[l, c, rows, :] = (act * up).astype(BF)
            act_ref[l, c, rows, :] = act.astype(BF)
            slope_ref[l, c, rows, :] = (up * (sig * (1.0 + gate * (1.0 - sig)))).astype(BF)
        h_ref[c] = x + scale(l, 3) * dot_nn(wdt_ref[l], hid_ref[l, c])

    def norm_of(l, k, c):
        xhat = xh_ref[l * 4 + k, c]
        return xhat, inv_ref[l * 4 + k, c], (xhat * gain(l, k)).astype(BF)

    def pass_on(l, k, c, x, dn, xhat, inv):
        back, both = norm_cols_back(dn, gain(l, k), xhat, inv)
        if x == 0:
            gacc_ref[l * 4 + k] += fold(both)
        g_ref[x, c] += back

    def feed_backward(l, c):
        xhat, inv, n = norm_of(l, 3, c)
        dz = [(scale(l, 3) * g_ref[x, c]).astype(BF) for x in range(2)]
        for z in range(4):
            rows = slice(128 * z, 128 * z + 128)
            act = act_ref[l, c, rows, :].astype(F32)
            slope = slope_ref[l, c, rows, :].astype(F32)
            for x in range(2):
                dhid = dot_nn(wd_ref[l, rows, :], dz[x])
                du_ref[2 * (c % 2) + x, 128 * z : 128 * z + 128, :] = (dhid * slope).astype(BF)
                du_ref[2 * (c % 2) + x, 512 + 128 * z : 640 + 128 * z, :] = (dhid * act).astype(BF)
        ga_ref[:, COL_FEED:COL_DOWN] += dot_nt(n, du_ref[2 * (c % 2)])
        gdt_ref[...] += dot_nt(dz[0], hid_ref[l, c])
        for x in range(2):
            dn = dot_nn(w_ref[l, :, COL_FEED:COL_DOWN], du_ref[2 * (c % 2) + x])
            pass_on(l, 3, c, x, dn, xhat, inv)

    def token_backward(l, c):
        xhat, inv, n = norm_of(l, 2, c)
        for x in range(2):
            dy = (scale(l, 2) * g_ref[x, c]).astype(BF)
            if x == 0:
                turned = jnp.concatenate([dy[:, :128].T, dy[:, 128:].T], axis=1)
                gt_ref[l] += dot_nn(turned, jnp.concatenate([n[:, :128], n[:, 128:]], axis=0))
            pass_on(l, 2, c, x, dot_nn(dy, both_ref[l]), xhat, inv)

    def var_backward(l, b):
        def slot(first, i):
            lanes = slice(128 * (i % 2), 128 * (i % 2) + 128)
            return qkvv_ref[l, 2 * b + i // 2, first : first + 128, lanes].astype(F32)

        for x in range(2):
            for cc in range(2):
                c = 2 * b + cc
                dt = (scale(l, 1) * g_ref[x, c]).astype(BF)
                dov_ref[4 * b + 2 * x + cc] = dot_nn(w_ref[l, :, COL_OUT[1] : COL_OUT[1] + 128], dt).astype(BF)
                if x == 0:
                    ga_ref[:, COL_OUT[1] : COL_OUT[1] + 128] += dot_nt(ov_ref[l, c], dt)
            value_slots = [slot(256, j) for j in range(4)]
            dkeys = [0.0] * 4
            dvalues = [0.0] * 4
            for i in range(4):
                lanes = slice(128 * (i % 2), 128 * (i % 2) + 128)
                grad = dov_ref[4 * b + 2 * x + i // 2, :, lanes].astype(F32)
                query = slot(0, i)
                prob = pv_ref[l, b, i]
                weighted = prob * head_sums(grad, value_slots)
                total = (weighted[:, :128] + weighted[:, 128:256]) + (weighted[:, 256:384] + weighted[:, 384:])
                ds = weighted - prob * jnp.concatenate([total] * 4, axis=1)
                spread_ref[8 * b + 4 * x + i] = ds.astype(BF).astype(F32)
                ds_slots = [spread_of(8 * b + 4 * x + i, j) for j in range(4)]
                terms = [ds_slots[j] * slot(128, j) for j in range(4)]
                dquery = (terms[0] + terms[1]) + (terms[2] + terms[3])
                for j in range(4):
                    dkeys[j] = dkeys[j] + ds_slots[j] * query
                    dvalues[j] = dvalues[j] + pw_ref[l, b, i, :, 128 * j : 128 * j + 128].astype(F32) * grad
                dqkv_ref[4 * b + 2 * x + i // 2, 0:128, lanes] = (dquery * 0.25).astype(BF)
            for j in range(4):
                lanes = slice(128 * (j % 2), 128 * (j % 2) + 128)
                dqkv_ref[4 * b + 2 * x + j // 2, 128:256, lanes] = dkeys[j].astype(BF)
                dqkv_ref[4 * b + 2 * x + j // 2, 256:384, lanes] = dvalues[j].astype(BF)
            for cc in range(2):
                c = 2 * b + cc
                xhat, inv, n = norm_of(l, 1, c)
                dqkv = dqkv_ref[4 * b + 2 * x + cc]
                if x == 0:
                    ga_ref[:, COL_IN[1] : COL_IN[1] + 384] += dot_nt(n, dqkv)
                pass_on(l, 1, c, x, dot_nn(w_ref[l, :, COL_IN[1] : COL_IN[1] + 384], dqkv), xhat, inv)

    def time_backward(l, c):
        xhat, inv, n = norm_of(l, 0, c)
        queries = qkvt_ref[l, c, 0:128, :]
        keys = qkvt_ref[l, c, 128:256, :]
        values = qkvt_ref[l, c, 256:384, :]
        grads = []
        for x in range(2):
            dt = (scale(l, 0) * g_ref[x, c]).astype(BF)
            grads.append(dot_nn(w_ref[l, :, COL_OUT[0] : COL_OUT[0] + 128], dt).astype(BF))
            if x == 0:
                ga_ref[:, COL_OUT[0] : COL_OUT[0] + 128] += dot_nt(ot_ref[l, c], dt)
        for s in range(2):
            lanes = slice(128 * s, 128 * s + 128)
            at = 2 * (c % 2) + s
            diag_heads(qbd_ref, at, queries[:, lanes])
            value_rows = values[:, lanes].T
            for x in range(2):
                diag_heads(dob_ref, 2 * at + x, grads[x][:, lanes])
            for hp in range(4):
                span = slice(256 * hp, 256 * hp + 256)
                rows = slice(32 * hp, 32 * hp + 32)
                prob_bf = pb_ref[l, 2 * c + s, :, span]
                prob = prob_bf.astype(F32)
                for x in range(2):
                    weighted = prob * dot_nn(value_rows, dob_ref[2 * at + x, :, span])
                    ds = (weighted - prob * jnp.sum(weighted, axis=0, keepdims=True)).astype(BF)
                    dvalue = dot_nt(dob_ref[2 * at + x, rows, span], prob_bf)
                    dquery = dot_nn(keys[rows, lanes], ds) * 0.25
                    dkey = dot_nt(qbd_ref[at, rows, span], ds)
                    dqkv_ref[2 * c + x, 32 * hp : 32 * hp + 16, lanes] = dquery[:16, :128].astype(BF)
                    dqkv_ref[2 * c + x, 32 * hp + 16 : 32 * hp + 32, lanes] = dquery[16:, 128:].astype(BF)
                    dqkv_ref[2 * c + x, 128 + 32 * hp : 160 + 32 * hp, lanes] = dkey.astype(BF)
                    dqkv_ref[2 * c + x, 256 + 32 * hp : 288 + 32 * hp, lanes] = dvalue.astype(BF)
        ga_ref[:, COL_IN[0] : COL_IN[0] + 384] += dot_nt(n, dqkv_ref[2 * c])
        for x in range(2):
            pass_on(l, 0, c, x, dot_nn(w_ref[l, :, COL_IN[0] : COL_IN[0] + 384], dqkv_ref[2 * c + x]), xhat, inv)

    def each(count, stage, l):
        for i in range(count):
            stage(l, i)

    def forward_layer(l, carry):
        each(chunks, time_forward, l)
        each(items, var_forward, l)
        each(chunks, tail_forward, l)
        return carry

    lax.fori_loop(0, layers, forward_layer, 0)
    last_ref[...] = h_ref[...].astype(BF)

    gacc_ref[...] = jnp.zeros_like(gacc_ref)
    gt_ref[...] = jnp.zeros_like(gt_ref)
    pacc_ref[...] = jnp.zeros_like(pacc_ref)

    def backward_layer(step, carry):
        l = layers - 1 - step
        ga_ref[...] = jnp.zeros_like(ga_ref)
        gdt_ref[...] = jnp.zeros_like(gdt_ref)
        each(chunks, feed_backward, l)
        each(chunks, token_backward, l)
        each(items, var_backward, l)
        each(chunks, time_backward, l)
        for k in range(4):
            gd_ref[128 * k : 128 * k + 128, :] = gdt_ref[:, 128 * k : 128 * k + 128].T
        for f in range(SHARDS):
            down = jnp.concatenate([gd_ref[32 * f + 8 * a : 32 * f + 8 * a + 8, :] for a in range(4)], axis=1)
            block = jnp.concatenate([ga_ref[8 * f : 8 * f + 8, :], down], axis=1)
            gbig_ref[l, f] = block.astype(BF)
        gains_rows = [jnp.sum(gacc_ref[l * 4 + k].T, axis=0, keepdims=True) for k in range(4)]
        sums = [
            jnp.sum(w_ref[l, :, COL_OUT[k] : COL_OUT[k] + 128].astype(F32) * ga_ref[:, COL_OUT[k] : COL_OUT[k] + 128], axis=0, keepdims=True)
            for k in range(2)
        ]
        sums.append(gains_rows[2])
        sums.append(jnp.sum(wd_ref[l].astype(F32) * gd_ref[...], axis=0, keepdims=True))
        for k in range(4):
            pacc_ref[0, l * 4 + k, 10:11, :] = gains_rows[k] / gains_ref[l, k : k + 1, :]
            pacc_ref[0, l * 4 + k, 11:12, :] = sums[k] / scales_ref[l, k : k + 1, :]
        return carry

    lax.fori_loop(0, layers, backward_layer, 0)

    gradient_ref[...] = g_ref[0]
    for x in range(2):
        for b in range(items):
            slots = g_ref[x, 2 * b] + g_ref[x, 2 * b + 1]
            tokscr_ref[2 * x + b] = (slots[:, :128] + slots[:, 128:]).T
            pacc_ref[x, ids_ref[b], 0:10, :] += tokscr_ref[2 * x + b, 0:10, :]
        pacc_ref[x, 0, 12:13, :] = tokscr_ref[2 * x, 127:128, :] + tokscr_ref[2 * x + 1, 127:128, :]

    for big_ref, small_ref, c in ((bigmine_ref, smallmine_ref, dp), (bigother_ref, smallother_ref, 1 - dp)):
        for rel in range(SHARDS):
            big_ref[rel % 4, rel // 4] = gbig_ref[c, me ^ rel]
        for block in range(16):
            if block < 8:
                pair = gt_ref[c, 16 * block : 16 * block + 16, :]
            else:
                pair = pacc_ref[block // 4 - 2, 4 * c + block % 4]
            lanes = slice(256 * (block % 4), 256 * (block % 4) + 256)
            small_ref[block // 4, :, lanes] = jnp.concatenate([pair[:8], pair[8:]], axis=1)


def call(kernel, name, out_shape, in_spaces, scratch, *operands, cost=None):
    spaces = {"v": pltpu.VMEM, "s": pltpu.SMEM}
    return pl.pallas_call(
        kernel,
        out_shape=out_shape,
        in_specs=[pl.BlockSpec(memory_space=spaces[space]) for space in in_spaces],
        out_specs=[pl.BlockSpec(memory_space=pltpu.VMEM)] * len(out_shape),
        scratch_shapes=scratch,
        compiler_params=pltpu.CompilerParams(vmem_limit_bytes=58 * 1024 * 1024),
        cost_estimate=cost,
        name=name,
    )(*operands)


def shape_of(shape, kind=F32):
    return jax.ShapeDtypeStruct(shape, kind)


def run_tower(split, *operands):
    half = [shape_of((4, 4, 8, COLS), BF)] * 2 + [shape_of((4, 8, 1024))] * 2
    return call(
        functools.partial(tower_kernel, split),
        "tower",
        [shape_of((4, 128, 256), BF), shape_of((4, 128, 256))] + half,
        "ss" + "v" * 12,
        [
            pltpu.VMEM((2, 128, COLS), F32),
            pltpu.VMEM((2, 128, COL_DOWN), BF),
            pltpu.VMEM((2, 512, 128), BF),
            pltpu.VMEM((2, COL_DOWN, 128), BF),
            pltpu.VMEM((2, 128, 512), BF),
            pltpu.VMEM((16, 128, 256), F32),
            pltpu.VMEM((8, 128, 128), F32),
            pltpu.VMEM((4, 128, 256), F32),
            pltpu.VMEM((2, 4, 128, 256), F32),
            pltpu.VMEM((8, 4, 128, 256), F32),
            pltpu.VMEM((8, 4, 1, 256), F32),
            pltpu.VMEM((2, 4, 384, 256), BF),
            pltpu.VMEM((2, 8, 128, 1024), BF),
            pltpu.VMEM((2, 4, 128, 256), BF),
            pltpu.VMEM((2, 4, 384, 256), BF),
            pltpu.VMEM((2, 2, 4, 8, 512), F32),
            pltpu.VMEM((2, 4, 128, 256), BF),
            pltpu.VMEM((2, 2, 4, 128, 512), BF),
            pltpu.VMEM((4, 128, 1024), BF),
            pltpu.VMEM((8, 128, 1024), BF),
            pltpu.VMEM((2, 4, 512, 256), BF),
            pltpu.VMEM((4, 1024, 256), BF),
            pltpu.VMEM((8, 384, 256), BF),
            pltpu.VMEM((8, 128, 256), BF),
            pltpu.VMEM((128, COL_DOWN), F32),
            pltpu.VMEM((512, 128), F32),
            pltpu.VMEM((2, 128, 128), F32),
            pltpu.VMEM((8, 128, 128), F32),
            pltpu.VMEM((2, SHARDS, 8, COLS), BF),
            pltpu.VMEM((2, 8, 16, 128), F32),
            pltpu.VMEM((16, 8, 512), F32),
            pltpu.VMEM((2, 4, 512, 256), BF),
            pltpu.VMEM((2, 4, 512, 256), BF),
            pltpu.VMEM((128, 512), F32),
            pltpu.VMEM((2, 256, 256), BF),
        ],
        *operands,
        cost=pl.CostEstimate(flops=10**10, bytes_accessed=20 * 10**6, transcendentals=0),
    )


def pack_rows(attn_in, attn_out, feed_in, feed_out):
    layers, _, rows, _ = attn_in.shape
    down = feed_out.reshape(layers, 4, rows, 128)
    return jnp.concatenate(
        [attn_in[:, 0], attn_in[:, 1], attn_out[:, 0], attn_out[:, 1], feed_in] + [down[:, a] for a in range(4)], axis=2
    )


def unpack_rows(packed):
    layers, rows, _ = packed.shape
    attn_in = jnp.stack([packed[:, :, at : at + 384] for at in COL_IN], axis=1)
    attn_out = jnp.stack([packed[:, :, at : at + 128] for at in COL_OUT], axis=1)
    feed_in = packed[:, :, COL_FEED:COL_DOWN]
    feed_out = jnp.stack([packed[:, :, COL_DOWN + 128 * a : COL_DOWN + 128 * a + 128] for a in range(4)], axis=1)
    return attn_in, attn_out, feed_in, feed_out.reshape(layers, 4 * rows, 128)


def flip(array, axis, bit, size):
    return lax.ppermute(array, axis, [(i, i ^ (1 << bit)) for i in range(size)])


def swap(array, mask):
    return lax.ppermute(array, "fsdp", [(i, i ^ mask) for i in range(SHARDS)])


def gather_rows(attn_in, attn_out, feed_in, feed_out, turned):
    row = call(pack_kernel, "pack", [shape_of((1, 8, COLS), BF)], "vvvv", [], attn_in, attn_out, feed_in, feed_out)[0]
    column = jnp.concatenate([row] + [swap(row, 4 * z) for z in range(1, 4)], axis=0)
    mine = [column] + [swap(column, xy) for xy in range(1, 4)]
    mine, turned = lax.optimization_barrier((mine, turned))
    return mine + [flip(part, "dp", 0, 2) for part in mine], turned


def final_kernel(big_mine, big_other, small_mine, small_other, attn_in, attn_out, feed_in, feed_out, tokens, gains, scales,
                 prompt, cls, adjust_prompt, adjust_cls):
    dp = lax.axis_index("dp")
    for part, l in ((big_mine, dp), (big_other, 1 - dp)):
        for k in range(2):
            attn_in[l, k] = part[:, COL_IN[k] : COL_IN[k] + 384]
            attn_out[l, k] = part[:, COL_OUT[k] : COL_OUT[k] + 128]
        feed_in[l] = part[:, COL_FEED:COL_DOWN]
        for a in range(4):
            feed_out[l, 8 * a : 8 * a + 8, :] = part[:, COL_DOWN + 128 * a : COL_DOWN + 128 * a + 128]
    for c in range(2):
        parts = [slice(256 * k, 256 * k + 256) for k in range(16)]
        tiles = [jnp.where(dp == c, small_mine[:, part], small_other[:, part]) for part in parts]
        blocks = [jnp.concatenate([tile[:, :128], tile[:, 128:]], axis=0) for tile in tiles]
        for k in range(8):
            tokens[c, 16 * k : 16 * k + 16, :] = blocks[k]
        for k in range(4):
            for row in range(10):
                prompt[row, 4 * c + k : 4 * c + k + 1, :] = blocks[8 + k][row : row + 1]
                adjust_prompt[row, 4 * c + k : 4 * c + k + 1, :] = blocks[12 + k][row : row + 1]
            gains[c, k : k + 1, :] = blocks[8 + k][10:11]
            scales[c, k : k + 1, :] = blocks[8 + k][11:12]
        if c == 0:
            cls[...] = blocks[8][12:13]
            adjust_cls[...] = blocks[12][12:13]


def four(first, rest):
    return (first.astype(F32) + rest[0].astype(F32)) + (rest[1].astype(F32) + rest[2].astype(F32))


def leave(last, gradient):
    return call(
        leave_kernel, "leave", [shape_of((2, 4, 128, 128), BF), shape_of((2, 4, 117, 128))], "vv", [pltpu.VMEM((8, 128, 128), F32)],
        last, gradient, cost=pl.CostEstimate(flops=10**6, bytes_accessed=16 * 10**6, transcendentals=0),
    )


def reduce_all(big_mine, big_other, small_mine, small_other, last, gradient):
    big = (big_mine.astype(F32) + flip(big_other, "dp", 0, 2).astype(F32)).astype(BF)
    small = (small_mine + flip(small_other, "dp", 0, 2)).astype(BF)
    big, small, last, gradient = lax.optimization_barrier((big, small, last, gradient))
    local = leave(last, gradient)
    got = [swap(jnp.concatenate([big[xy], small], axis=2), xy) for xy in range(1, 4)]
    big = four(big[0], [part[:, :, :COLS] for part in got]).astype(BF)
    small = four(small, [part[:, :, COLS:] for part in got]).astype(BF)
    small = jnp.concatenate([small[at] for at in range(4)], axis=1)
    big, small, local = lax.optimization_barrier((big, small, local))
    got = [swap(jnp.concatenate([big[z], small], axis=1), 4 * z) for z in range(1, 4)]
    big = four(big[0], [part[:, :COLS] for part in got])
    small = four(small, [part[:, COLS:] for part in got])
    reduced = call(
        final_kernel, "final",
        [shape_of((2, 2, 8, 384)), shape_of((2, 2, 8, 128)), shape_of((2, 8, 1024)), shape_of((2, 32, 128)), shape_of((2, 128, 128)),
         shape_of((2, 4, 128)), shape_of((2, 4, 128)), shape_of((10, 8, 128)), shape_of((1, 128)), shape_of((10, 8, 128)), shape_of((1, 128))],
        "vvvv", [], big, flip(big, "dp", 0, 2), small, flip(small, "dp", 0, 2),
    )
    return local, reduced


def per_device(shard_count, patches, prompts, cls_token, attn_in, attn_out, feed_in, feed_out, token_operator,
               norm_gains, branch_scales, var_counts, dataset_ids, cotangent, adjust_cotangent):
    fast = shard_count == SHARDS
    turned = call(
        prepare_kernel, "prepare", [shape_of((3, 4, 128, 256), BF)], "svvvvv", [pltpu.VMEM((8, 128, 128), F32)],
        dataset_ids, patches, prompts, cls_token.reshape(1, -1), cotangent, adjust_cotangent,
        cost=pl.CostEstimate(flops=10**6, bytes_accessed=8 * 10**6, transcendentals=0),
    )[0]
    if fast:
        gathered, turned = gather_rows(attn_in, attn_out, feed_in, feed_out, turned)
    else:
        whole_down = lax.all_gather(feed_out, "fsdp", axis=1, tiled=True)
        whole_down = whole_down.reshape(2, SHARDS, 4, 8, 128).transpose(0, 2, 1, 3, 4).reshape(2, 512, 128)
        rows = pack_rows(
            lax.all_gather(attn_in, "fsdp", axis=2, tiled=True),
            lax.all_gather(attn_out, "fsdp", axis=2, tiled=True),
            lax.all_gather(feed_in, "fsdp", axis=1, tiled=True),
            whole_down,
        )
        rows = rows.reshape(2, SHARDS, 8, COLS).transpose(1, 0, 2, 3)
        gathered = [rows[:, l].reshape(4, 4, 8, COLS)[:, xy] for l in range(2) for xy in range(4)]
    last, gradient, *sums = run_tower(
        fast, dataset_ids, var_counts, *gathered, token_operator, norm_gains, branch_scales, turned
    )
    if fast:
        (output, patch_grad), reduced = reduce_all(*sums, last, gradient)
        (attn_in_g, attn_out_g, feed_in_g, feed_out_g, token_g, gains_g, scales_g, prompt_g, cls_g, adjust_prompt_g,
         adjust_cls_g) = reduced
        return (output, patch_grad, prompt_g.transpose(1, 0, 2), cls_g[0], attn_in_g, attn_out_g, feed_in_g, feed_out_g, token_g, gains_g,
                scales_g, adjust_prompt_g.transpose(1, 0, 2), adjust_cls_g[0])
    output, patch_grad = leave(last, gradient)
    rows = jnp.stack(sums[:2]).transpose(0, 2, 1, 3, 4).astype(F32).reshape(2, 128, COLS)
    attn_in_g, attn_out_g, feed_in_g, feed_out_g = unpack_rows(rows)
    feed_out_g = feed_out_g.reshape(2, 4, SHARDS, 8, 128).transpose(0, 2, 1, 3, 4).reshape(2, 512, 128)
    matrices = (
        lax.psum_scatter(lax.psum(attn_in_g, "dp"), "fsdp", scatter_dimension=2, tiled=True),
        lax.psum_scatter(lax.psum(attn_out_g, "dp"), "fsdp", scatter_dimension=2, tiled=True),
        lax.psum_scatter(lax.psum(feed_in_g, "dp"), "fsdp", scatter_dimension=1, tiled=True),
        lax.psum_scatter(lax.psum(feed_out_g, "dp"), "fsdp", scatter_dimension=1, tiled=True),
    )
    small = lax.psum(jnp.stack(sums[2:]), ("dp", "fsdp"))
    small = small.reshape(2, 4, 8, 4, 2, 128).transpose(0, 1, 3, 4, 2, 5).reshape(2, 16, 16, 128)
    main, adjust = small[:, 8:12].reshape(8, 16, 128), small[:, 12:].reshape(8, 16, 128)
    return (output, patch_grad, main[:, :10], main[0, 12], *matrices, small[:, :8].reshape(2, 128, 128),
            main[:, 10].reshape(2, 4, 128), main[:, 11].reshape(2, 4, 128), adjust[:, :10], adjust[0, 12])


def solution(mesh):
    batch = P(("dp", "fsdp"), None, None, None)
    wide = P(None, None, "fsdp", None)
    tall = P(None, "fsdp", None)
    return jax.shard_map(
        functools.partial(per_device, mesh.shape["fsdp"]),
        mesh=mesh,
        in_specs=(batch, P(), P(), wide, wide, tall, tall, P(), P(), P(), P(), P(("dp", "fsdp")), batch, batch),
        out_specs=(batch, batch, P(), P(), wide, wide, tall, tall, P(), P(), P(), P(), P()),
        check_vma=False,
    )
```

```python
import functools

import jax
import jax.numpy as jnp
from jax import lax
from jax.experimental import pallas as pl
from jax.experimental.pallas import tpu as pltpu
from jax.sharding import PartitionSpec as P

HEADS = 8
EPSILON = 1e-05
NEG_FILL = -1000000000.0
BF = jnp.bfloat16
F32 = jnp.float32

COL_IN = (0, 384)
COL_OUT = (768, 896)
COL_FEED = 1024
COL_DOWN = 2048
COLS = 2560
SHARDS = 16
STEP_BITS = (2, 3, 0, 1)


def dot_nn(a, b):
    return lax.dot_general(a, b, (((1,), (0,)), ((), ())), preferred_element_type=F32)


def dot_nt(a, b):
    return lax.dot_general(a, b, (((1,), (1,)), ((), ())), preferred_element_type=F32)


def norm_cols(x):
    centered = x - jnp.mean(x, axis=0, keepdims=True)
    inv = lax.rsqrt(jnp.mean(centered * centered, axis=0, keepdims=True) + EPSILON)
    return centered * inv, inv


def norm_cols_back(dn, gain, xhat, inv):
    e = dn * gain
    both = e * xhat
    m1 = jnp.mean(e, axis=0, keepdims=True)
    m2 = jnp.mean(both, axis=0, keepdims=True)
    return inv * (e - m1 - xhat * m2), both


def fold(part):
    return part[:, :128] + part[:, 128:]


def pack_kernel(attn_in_ref, attn_out_ref, feed_in_ref, feed_out_ref, out_ref):
    l = lax.axis_index("dp")
    down = feed_out_ref[l].astype(F32)
    parts = [attn_in_ref[l, 0], attn_in_ref[l, 1], attn_out_ref[l, 0], attn_out_ref[l, 1], feed_in_ref[l]]
    parts = [part.astype(F32) for part in parts] + [down[8 * a : 8 * a + 8] for a in range(4)]
    out_ref[0] = jnp.concatenate(parts, axis=1).astype(BF)


def prepare_kernel(ids_ref, patches_ref, prompts_ref, cls_ref, cot_ref, adj_ref, turned_ref, tok_ref):
    for b in range(2):
        ident = ids_ref[b]
        for v in range(4):
            at = 4 * b + v
            lanes = slice(128 * (v % 2), 128 * (v % 2) + 128)
            tok_ref[at, 0:10, :] = prompts_ref[ident].astype(F32)
            tok_ref[at, 10:127, :] = patches_ref[b, v].astype(F32)
            tok_ref[at, 127:128, :] = cls_ref[...].astype(F32)
            turned_ref[0, 2 * b + v // 2, :, lanes] = tok_ref[at].T.astype(BF)
            turned_ref[1, 2 * b + v // 2, :, lanes] = cot_ref[b, v].T
            turned_ref[2, 2 * b + v // 2, :, lanes] = adj_ref[b, v].T


def tower_kernel(
    split,
    ids_ref, counts_ref, wmine0_ref, wmine1_ref, wmine2_ref, wmine3_ref, wother0_ref, wother1_ref, wother2_ref, wother3_ref,
    tok_ref, gains_ref, scales_ref, turned_ref,
    out_ref, pgrad_ref, bigmine_ref, bigother_ref, smallmine_ref, smallother_ref,
    stage_ref, w_ref, wd_ref, wt_ref, wdt_ref, colb_ref, tokscr_ref, h_ref, g_ref, xh_ref, inv_ref,
    qkvt_ref, pb_ref, ot_ref, qkvv_ref, pv_ref, ov_ref, pw_ref, qbd_ref, dob_ref, hid_ref, du_ref, dqkv_ref,
    dov_ref, ga_ref, gd_ref, gt_ref, gacc_ref, gbig_ref, pacc_ref, spread_ref, act_ref, slope_ref, gdt_ref, both_ref,
):
    dp = lax.axis_index("dp") if split else 0
    me = lax.axis_index("fsdp") if split else 0
    layers = 2
    chunks = 4
    items = 2

    for rel in range(SHARDS):
        rows = pl.ds(pl.multiple_of(8 * (me ^ rel), 8), 8)
        mine_ref = (wmine0_ref, wmine1_ref, wmine2_ref, wmine3_ref)[rel % 4]
        other_ref = (wother0_ref, wother1_ref, wother2_ref, wother3_ref)[rel % 4]
        stage_ref[dp, rows, :] = mine_ref[rel // 4].astype(F32)
        stage_ref[1 - dp, rows, :] = other_ref[rel // 4].astype(F32)
    for l in range(layers):
        for k in range(4):
            for offset, rows in ((0, gains_ref), (4, scales_ref)):
                col = jnp.broadcast_to(rows[l, k : k + 1, :], (128, 128)).T
                colb_ref[l * 8 + offset + k, :, 0:128] = col
                colb_ref[l * 8 + offset + k, :, 128:256] = col

    h_ref[...] = turned_ref[0].astype(F32)
    g_ref[...] = turned_ref[1:3].astype(F32)

    head_row = lax.broadcasted_iota(jnp.int32, (8, 128), 0)
    head_col = lax.broadcasted_iota(jnp.int32, (8, 128), 1) // 16
    gather_heads = jnp.where(head_row == head_col, 1.0, 0.0).astype(BF)
    def spread_of(at, j):
        lanes = slice(128 * j, 128 * j + 128)
        return jnp.concatenate([jnp.broadcast_to(spread_ref[at, h : h + 1, lanes], (16, 128)) for h in range(HEADS)], axis=0)

    def head_sums(left, rights):
        return dot_nn(gather_heads, jnp.concatenate([(left * right).astype(BF) for right in rights], axis=1))

    def diag_heads(target_ref, at, rows):
        for head in range(HEADS):
            target_ref[at, 16 * head : 16 * head + 16, 128 * head : 128 * head + 128] = rows[16 * head : 16 * head + 16]

    both_ref[...] = jnp.zeros_like(both_ref)
    for half in range(2):
        both_ref[:, 128 * half : 128 * half + 128, 128 * half : 128 * half + 128] = tok_ref[...]
    qbd_ref[...] = jnp.zeros_like(qbd_ref)
    dob_ref[...] = jnp.zeros_like(dob_ref)

    def gain(l, k):
        return colb_ref[l * 8 + k]

    def scale(l, k):
        return colb_ref[l * 8 + 4 + k]

    def keep_norm(l, k, c, x):
        xhat, inv = norm_cols(x)
        xh_ref[l * 4 + k, c] = xhat
        inv_ref[l * 4 + k, c] = inv
        return (xhat * gain(l, k)).astype(BF)

    def time_forward(l, c):
        x = h_ref[c]
        n = keep_norm(l, 0, c, x)
        qkv = dot_nn(wt_ref[l, 0:384, :], n)
        queries = (qkv[:128] * 0.25).astype(BF)
        keys = qkv[128:256].astype(BF)
        values = qkv[256:].astype(BF)
        qkvt_ref[l, c, 0:128, :] = queries
        qkvt_ref[l, c, 128:256, :] = keys
        qkvt_ref[l, c, 256:384, :] = values
        for s in range(2):
            lanes = slice(128 * s, 128 * s + 128)
            at = 2 * (c % 2) + s
            diag_heads(qbd_ref, at, queries[:, lanes])
            key_rows = keys[:, lanes].T
            for hp in range(4):
                span = slice(256 * hp, 256 * hp + 256)
                rows = slice(32 * hp, 32 * hp + 32)
                scores = dot_nn(key_rows, qbd_ref[at, :, span])
                shifted = jnp.exp(scores - jnp.max(scores, axis=0, keepdims=True))
                prob = (shifted * (1.0 / jnp.sum(shifted, axis=0, keepdims=True))).astype(BF)
                pb_ref[l, 2 * c + s, :, span] = prob
                mixed = dot_nn(values[rows, lanes], prob)
                ot_ref[l, c, 32 * hp : 32 * hp + 16, lanes] = mixed[:16, :128].astype(BF)
                ot_ref[l, c, 32 * hp + 16 : 32 * hp + 32, lanes] = mixed[16:, 128:].astype(BF)
        branch = dot_nn(wt_ref[l, COL_OUT[0] : COL_OUT[0] + 128, :], ot_ref[l, c])
        h_ref[c] = x + scale(l, 0) * branch

    def var_forward(l, b):
        for cc in range(2):
            c = 2 * b + cc
            n = keep_norm(l, 1, c, h_ref[c])
            qkv = dot_nn(wt_ref[l, COL_IN[1] : COL_IN[1] + 384, :], n)
            qkvv_ref[l, c, 0:128, :] = (qkv[:128] * 0.25).astype(BF)
            qkvv_ref[l, c, 128:384, :] = qkv[128:].astype(BF)
        count = counts_ref[ids_ref[b]]

        def slot(first, i):
            lanes = slice(128 * (i % 2), 128 * (i % 2) + 128)
            return qkvv_ref[l, 2 * b + i // 2, first : first + 128, lanes].astype(F32)

        key_slots = [slot(128, j) for j in range(4)]
        value_slots = [slot(256, j) for j in range(4)]
        for i in range(4):
            scores = head_sums(slot(0, i), key_slots)
            parts = [scores[:, 128 * j : 128 * j + 128] for j in range(4)]
            parts = [jnp.where(jnp.full((8, 128), count, jnp.int32) > j, parts[j], NEG_FILL) for j in range(4)]
            top = jnp.maximum(jnp.maximum(parts[0], parts[1]), jnp.maximum(parts[2], parts[3]))
            shifted = [jnp.exp(part - top) for part in parts]
            total = 1.0 / ((shifted[0] + shifted[1]) + (shifted[2] + shifted[3]))
            prob = jnp.concatenate([part * total for part in shifted], axis=1)
            pv_ref[l, b, i] = prob
            spread_ref[4 * b + i] = prob.astype(BF).astype(F32)
            mixed = None
            for j in range(4):
                spread = spread_of(4 * b + i, j)
                pw_ref[l, b, i, :, 128 * j : 128 * j + 128] = spread.astype(BF)
                mixed = spread * value_slots[j] if mixed is None else mixed + spread * value_slots[j]
            lanes = slice(128 * (i % 2), 128 * (i % 2) + 128)
            ov_ref[l, 2 * b + i // 2, :, lanes] = mixed.astype(BF)
        for cc in range(2):
            c = 2 * b + cc
            branch = dot_nn(wt_ref[l, COL_OUT[1] : COL_OUT[1] + 128, :], ov_ref[l, c])
            h_ref[c] = h_ref[c] + scale(l, 1) * branch

    def tail_forward(l, c):
        x = h_ref[c]
        n = keep_norm(l, 2, c, x)
        x = x + scale(l, 2) * dot_nt(n, both_ref[l])
        n = keep_norm(l, 3, c, x)
        for z in range(4):
            rows = slice(128 * z, 128 * z + 128)
            gate = dot_nn(wt_ref[l, COL_FEED + 128 * z : COL_FEED + 128 * z + 128, :], n)
            up = dot_nn(wt_ref[l, COL_FEED + 512 + 128 * z : COL_FEED + 640 + 128 * z, :], n)
            sig = 0.5 * jnp.tanh(0.5 * gate) + 0.5
            act = gate * sig
            hid_ref[l, c, rows, :] = (act * up).astype(BF)
            act_ref[l, c, rows, :] = act.astype(BF)
            slope_ref[l, c, rows, :] = (up * (sig * (1.0 + gate * (1.0 - sig)))).astype(BF)
        h_ref[c] = x + scale(l, 3) * dot_nn(wdt_ref[l], hid_ref[l, c])

    def norm_of(l, k, c):
        xhat = xh_ref[l * 4 + k, c]
        return xhat, inv_ref[l * 4 + k, c], (xhat * gain(l, k)).astype(BF)

    def pass_on(l, k, c, x, dn, xhat, inv):
        back, both = norm_cols_back(dn, gain(l, k), xhat, inv)
        if x == 0:
            gacc_ref[l * 4 + k] += fold(both)
        g_ref[x, c] += back

    def feed_backward(l, c):
        xhat, inv, n = norm_of(l, 3, c)
        dz = [(scale(l, 3) * g_ref[x, c]).astype(BF) for x in range(2)]
        for z in range(4):
            rows = slice(128 * z, 128 * z + 128)
            act = act_ref[l, c, rows, :].astype(F32)
            slope = slope_ref[l, c, rows, :].astype(F32)
            for x in range(2):
                dhid = dot_nn(wd_ref[l, rows, :], dz[x])
                du_ref[2 * (c % 2) + x, 128 * z : 128 * z + 128, :] = (dhid * slope).astype(BF)
                du_ref[2 * (c % 2) + x, 512 + 128 * z : 640 + 128 * z, :] = (dhid * act).astype(BF)
        ga_ref[:, COL_FEED:COL_DOWN] += dot_nt(n, du_ref[2 * (c % 2)])
        gdt_ref[...] += dot_nt(dz[0], hid_ref[l, c])
        for x in range(2):
            dn = dot_nn(w_ref[l, :, COL_FEED:COL_DOWN], du_ref[2 * (c % 2) + x])
            pass_on(l, 3, c, x, dn, xhat, inv)

    def token_backward(l, c):
        xhat, inv, n = norm_of(l, 2, c)
        for x in range(2):
            dy = (scale(l, 2) * g_ref[x, c]).astype(BF)
            if x == 0:
                turned = jnp.concatenate([dy[:, :128].T, dy[:, 128:].T], axis=1)
                gt_ref[l] += dot_nn(turned, jnp.concatenate([n[:, :128], n[:, 128:]], axis=0))
            pass_on(l, 2, c, x, dot_nn(dy, both_ref[l]), xhat, inv)

    def var_backward(l, b):
        def slot(first, i):
            lanes = slice(128 * (i % 2), 128 * (i % 2) + 128)
            return qkvv_ref[l, 2 * b + i // 2, first : first + 128, lanes].astype(F32)

        for x in range(2):
            for cc in range(2):
                c = 2 * b + cc
                dt = (scale(l, 1) * g_ref[x, c]).astype(BF)
                dov_ref[4 * b + 2 * x + cc] = dot_nn(w_ref[l, :, COL_OUT[1] : COL_OUT[1] + 128], dt).astype(BF)
                if x == 0:
                    ga_ref[:, COL_OUT[1] : COL_OUT[1] + 128] += dot_nt(ov_ref[l, c], dt)
            value_slots = [slot(256, j) for j in range(4)]
            dkeys = [0.0] * 4
            dvalues = [0.0] * 4
            for i in range(4):
                lanes = slice(128 * (i % 2), 128 * (i % 2) + 128)
                grad = dov_ref[4 * b + 2 * x + i // 2, :, lanes].astype(F32)
                query = slot(0, i)
                prob = pv_ref[l, b, i]
                weighted = prob * head_sums(grad, value_slots)
                total = (weighted[:, :128] + weighted[:, 128:256]) + (weighted[:, 256:384] + weighted[:, 384:])
                ds = weighted - prob * jnp.concatenate([total] * 4, axis=1)
                spread_ref[8 * b + 4 * x + i] = ds.astype(BF).astype(F32)
                ds_slots = [spread_of(8 * b + 4 * x + i, j) for j in range(4)]
                terms = [ds_slots[j] * slot(128, j) for j in range(4)]
                dquery = (terms[0] + terms[1]) + (terms[2] + terms[3])
                for j in range(4):
                    dkeys[j] = dkeys[j] + ds_slots[j] * query
                    dvalues[j] = dvalues[j] + pw_ref[l, b, i, :, 128 * j : 128 * j + 128].astype(F32) * grad
                dqkv_ref[4 * b + 2 * x + i // 2, 0:128, lanes] = (dquery * 0.25).astype(BF)
            for j in range(4):
                lanes = slice(128 * (j % 2), 128 * (j % 2) + 128)
                dqkv_ref[4 * b + 2 * x + j // 2, 128:256, lanes] = dkeys[j].astype(BF)
                dqkv_ref[4 * b + 2 * x + j // 2, 256:384, lanes] = dvalues[j].astype(BF)
            for cc in range(2):
                c = 2 * b + cc
                xhat, inv, n = norm_of(l, 1, c)
                dqkv = dqkv_ref[4 * b + 2 * x + cc]
                if x == 0:
                    ga_ref[:, COL_IN[1] : COL_IN[1] + 384] += dot_nt(n, dqkv)
                pass_on(l, 1, c, x, dot_nn(w_ref[l, :, COL_IN[1] : COL_IN[1] + 384], dqkv), xhat, inv)

    def time_backward(l, c):
        xhat, inv, n = norm_of(l, 0, c)
        queries = qkvt_ref[l, c, 0:128, :]
        keys = qkvt_ref[l, c, 128:256, :]
        values = qkvt_ref[l, c, 256:384, :]
        grads = []
        for x in range(2):
            dt = (scale(l, 0) * g_ref[x, c]).astype(BF)
            grads.append(dot_nn(w_ref[l, :, COL_OUT[0] : COL_OUT[0] + 128], dt).astype(BF))
            if x == 0:
                ga_ref[:, COL_OUT[0] : COL_OUT[0] + 128] += dot_nt(ot_ref[l, c], dt)
        for s in range(2):
            lanes = slice(128 * s, 128 * s + 128)
            at = 2 * (c % 2) + s
            diag_heads(qbd_ref, at, queries[:, lanes])
            value_rows = values[:, lanes].T
            for x in range(2):
                diag_heads(dob_ref, 2 * at + x, grads[x][:, lanes])
            for hp in range(4):
                span = slice(256 * hp, 256 * hp + 256)
                rows = slice(32 * hp, 32 * hp + 32)
                prob_bf = pb_ref[l, 2 * c + s, :, span]
                prob = prob_bf.astype(F32)
                for x in range(2):
                    weighted = prob * dot_nn(value_rows, dob_ref[2 * at + x, :, span])
                    ds = (weighted - prob * jnp.sum(weighted, axis=0, keepdims=True)).astype(BF)
                    dvalue = dot_nt(dob_ref[2 * at + x, rows, span], prob_bf)
                    dquery = dot_nn(keys[rows, lanes], ds) * 0.25
                    dkey = dot_nt(qbd_ref[at, rows, span], ds)
                    dqkv_ref[2 * c + x, 32 * hp : 32 * hp + 16, lanes] = dquery[:16, :128].astype(BF)
                    dqkv_ref[2 * c + x, 32 * hp + 16 : 32 * hp + 32, lanes] = dquery[16:, 128:].astype(BF)
                    dqkv_ref[2 * c + x, 128 + 32 * hp : 160 + 32 * hp, lanes] = dkey.astype(BF)
                    dqkv_ref[2 * c + x, 256 + 32 * hp : 288 + 32 * hp, lanes] = dvalue.astype(BF)
        ga_ref[:, COL_IN[0] : COL_IN[0] + 384] += dot_nt(n, dqkv_ref[2 * c])
        for x in range(2):
            pass_on(l, 0, c, x, dot_nn(w_ref[l, :, COL_IN[0] : COL_IN[0] + 384], dqkv_ref[2 * c + x]), xhat, inv)

    def each(count, stage, l):
        for i in range(count):
            stage(l, i)

    def forward_layer(l, carry):
        for pair in range(SHARDS // 2):
            lo = stage_ref[l, 16 * pair : 16 * pair + 8, :]
            hi = stage_ref[l, 16 * pair + 8 : 16 * pair + 16, :]
            w_ref[l, 16 * pair : 16 * pair + 16, :] = jnp.concatenate([lo[:, :COL_DOWN], hi[:, :COL_DOWN]], axis=0).astype(BF)
            for half, part in enumerate((lo, hi)):
                base = 64 * pair + 32 * half
                wd_ref[l, base : base + 32, :] = jnp.concatenate(
                    [part[:, COL_DOWN + 128 * a : COL_DOWN + 128 * a + 128] for a in range(4)], axis=0
                ).astype(BF)
        for block in range(COL_DOWN // 128):
            wt_ref[l, 128 * block : 128 * block + 128, :] = w_ref[l, :, 128 * block : 128 * block + 128].T
        for block in range(4):
            wdt_ref[l, :, 128 * block : 128 * block + 128] = wd_ref[l, 128 * block : 128 * block + 128, :].T
        each(chunks, time_forward, l)
        each(items, var_forward, l)
        each(chunks, tail_forward, l)
        return carry

    lax.fori_loop(0, layers, forward_layer, 0)
    for b in range(items):
        for v in range(4):
            lanes = slice(128 * (v % 2), 128 * (v % 2) + 128)
            out_ref[b, v] = h_ref[2 * b + v // 2, :, lanes].T.astype(BF)

    gacc_ref[...] = jnp.zeros_like(gacc_ref)
    gt_ref[...] = jnp.zeros_like(gt_ref)
    pacc_ref[...] = jnp.zeros_like(pacc_ref)

    def backward_layer(step, carry):
        l = layers - 1 - step
        ga_ref[...] = jnp.zeros_like(ga_ref)
        gdt_ref[...] = jnp.zeros_like(gdt_ref)
        each(chunks, feed_backward, l)
        each(chunks, token_backward, l)
        each(items, var_backward, l)
        each(chunks, time_backward, l)
        for k in range(4):
            gd_ref[128 * k : 128 * k + 128, :] = gdt_ref[:, 128 * k : 128 * k + 128].T
        for f in range(SHARDS):
            down = jnp.concatenate([gd_ref[32 * f + 8 * a : 32 * f + 8 * a + 8, :] for a in range(4)], axis=1)
            block = jnp.concatenate([ga_ref[8 * f : 8 * f + 8, :], down], axis=1)
            gbig_ref[l, f] = block.astype(BF)
        gains_rows = [jnp.sum(gacc_ref[l * 4 + k].T, axis=0, keepdims=True) for k in range(4)]
        sums = [
            jnp.sum(w_ref[l, :, COL_OUT[k] : COL_OUT[k] + 128].astype(F32) * ga_ref[:, COL_OUT[k] : COL_OUT[k] + 128], axis=0, keepdims=True)
            for k in range(2)
        ]
        sums.append(gains_rows[2])
        sums.append(jnp.sum(wd_ref[l].astype(F32) * gd_ref[...], axis=0, keepdims=True))
        for k in range(4):
            pacc_ref[0, l * 4 + k, 10:11, :] = gains_rows[k] / gains_ref[l, k : k + 1, :]
            pacc_ref[0, l * 4 + k, 11:12, :] = sums[k] / scales_ref[l, k : k + 1, :]
        return carry

    lax.fori_loop(0, layers, backward_layer, 0)

    for x in range(2):
        cls_sum = None
        for b in range(items):
            prompt_sum = None
            for v in range(4):
                lanes = slice(128 * (v % 2), 128 * (v % 2) + 128)
                tokscr_ref[4 * b + v] = g_ref[x, 2 * b + v // 2, :, lanes].T
                head = tokscr_ref[4 * b + v, 0:10, :]
                last = tokscr_ref[4 * b + v, 127:128, :]
                prompt_sum = head if prompt_sum is None else prompt_sum + head
                cls_sum = last if cls_sum is None else cls_sum + last
                if x == 0:
                    pgrad_ref[b, v] = tokscr_ref[4 * b + v, 10:127, :]
            pacc_ref[x, ids_ref[b], 0:10, :] += prompt_sum
        pacc_ref[x, 0, 12:13, :] = cls_sum

    for big_ref, small_ref, c in ((bigmine_ref, smallmine_ref, dp), (bigother_ref, smallother_ref, 1 - dp)):
        for rel in range(SHARDS):
            big_ref[rel % 4, rel // 4] = gbig_ref[c, me ^ rel]
        for block in range(16):
            if block < 8:
                pair = gt_ref[c, 16 * block : 16 * block + 16, :]
            else:
                pair = pacc_ref[block // 4 - 2, 4 * c + block % 4]
            lanes = slice(256 * (block % 4), 256 * (block % 4) + 256)
            small_ref[block // 4, :, lanes] = jnp.concatenate([pair[:8], pair[8:]], axis=1)


def call(kernel, name, out_shape, in_spaces, scratch, *operands, cost=None):
    spaces = {"v": pltpu.VMEM, "s": pltpu.SMEM}
    return pl.pallas_call(
        kernel,
        out_shape=out_shape,
        in_specs=[pl.BlockSpec(memory_space=spaces[space]) for space in in_spaces],
        out_specs=[pl.BlockSpec(memory_space=pltpu.VMEM)] * len(out_shape),
        scratch_shapes=scratch,
        compiler_params=pltpu.CompilerParams(vmem_limit_bytes=58 * 1024 * 1024),
        cost_estimate=cost,
        name=name,
    )(*operands)


def shape_of(shape, kind=F32):
    return jax.ShapeDtypeStruct(shape, kind)


def run_tower(split, *operands):
    half = [shape_of((4, 4, 8, COLS), BF)] * 2 + [shape_of((4, 8, 1024))] * 2
    return call(
        functools.partial(tower_kernel, split),
        "tower",
        [shape_of((2, 4, 128, 128), BF), shape_of((2, 4, 117, 128))] + half,
        "ss" + "v" * 12,
        [
            pltpu.VMEM((2, 128, COLS), F32),
            pltpu.VMEM((2, 128, COL_DOWN), BF),
            pltpu.VMEM((2, 512, 128), BF),
            pltpu.VMEM((2, COL_DOWN, 128), BF),
            pltpu.VMEM((2, 128, 512), BF),
            pltpu.VMEM((16, 128, 256), F32),
            pltpu.VMEM((8, 128, 128), F32),
            pltpu.VMEM((4, 128, 256), F32),
            pltpu.VMEM((2, 4, 128, 256), F32),
            pltpu.VMEM((8, 4, 128, 256), F32),
            pltpu.VMEM((8, 4, 1, 256), F32),
            pltpu.VMEM((2, 4, 384, 256), BF),
            pltpu.VMEM((2, 8, 128, 1024), BF),
            pltpu.VMEM((2, 4, 128, 256), BF),
            pltpu.VMEM((2, 4, 384, 256), BF),
            pltpu.VMEM((2, 2, 4, 8, 512), F32),
            pltpu.VMEM((2, 4, 128, 256), BF),
            pltpu.VMEM((2, 2, 4, 128, 512), BF),
            pltpu.VMEM((4, 128, 1024), BF),
            pltpu.VMEM((8, 128, 1024), BF),
            pltpu.VMEM((2, 4, 512, 256), BF),
            pltpu.VMEM((4, 1024, 256), BF),
            pltpu.VMEM((8, 384, 256), BF),
            pltpu.VMEM((8, 128, 256), BF),
            pltpu.VMEM((128, COL_DOWN), F32),
            pltpu.VMEM((512, 128), F32),
            pltpu.VMEM((2, 128, 128), F32),
            pltpu.VMEM((8, 128, 128), F32),
            pltpu.VMEM((2, SHARDS, 8, COLS), BF),
            pltpu.VMEM((2, 8, 16, 128), F32),
            pltpu.VMEM((16, 8, 512), F32),
            pltpu.VMEM((2, 4, 512, 256), BF),
            pltpu.VMEM((2, 4, 512, 256), BF),
            pltpu.VMEM((128, 512), F32),
            pltpu.VMEM((2, 256, 256), BF),
        ],
        *operands,
        cost=pl.CostEstimate(flops=10**10, bytes_accessed=20 * 10**6, transcendentals=0),
    )


def pack_rows(attn_in, attn_out, feed_in, feed_out):
    layers, _, rows, _ = attn_in.shape
    down = feed_out.reshape(layers, 4, rows, 128)
    return jnp.concatenate(
        [attn_in[:, 0], attn_in[:, 1], attn_out[:, 0], attn_out[:, 1], feed_in] + [down[:, a] for a in range(4)], axis=2
    )


def unpack_rows(packed):
    layers, rows, _ = packed.shape
    attn_in = jnp.stack([packed[:, :, at : at + 384] for at in COL_IN], axis=1)
    attn_out = jnp.stack([packed[:, :, at : at + 128] for at in COL_OUT], axis=1)
    feed_in = packed[:, :, COL_FEED:COL_DOWN]
    feed_out = jnp.stack([packed[:, :, COL_DOWN + 128 * a : COL_DOWN + 128 * a + 128] for a in range(4)], axis=1)
    return attn_in, attn_out, feed_in, feed_out.reshape(layers, 4 * rows, 128)


def flip(array, axis, bit, size):
    return lax.ppermute(array, axis, [(i, i ^ (1 << bit)) for i in range(size)])


def swap(array, mask):
    return lax.ppermute(array, "fsdp", [(i, i ^ mask) for i in range(SHARDS)])


def gather_rows(attn_in, attn_out, feed_in, feed_out, turned):
    row = call(pack_kernel, "pack", [shape_of((1, 8, COLS), BF)], "vvvv", [], attn_in, attn_out, feed_in, feed_out)[0]
    column = jnp.concatenate([row] + [swap(row, 4 * z) for z in range(1, 4)], axis=0)
    mine = [column] + [swap(column, xy) for xy in range(1, 4)]
    mine, turned = lax.optimization_barrier((mine, turned))
    return mine + [flip(part, "dp", 0, 2) for part in mine], turned


def final_kernel(big_mine, big_other, small_mine, small_other, attn_in, attn_out, feed_in, feed_out, tokens, gains, scales,
                 prompt, cls, adjust_prompt, adjust_cls):
    dp = lax.axis_index("dp")
    for part, l in ((big_mine, dp), (big_other, 1 - dp)):
        for k in range(2):
            attn_in[l, k] = part[:, COL_IN[k] : COL_IN[k] + 384]
            attn_out[l, k] = part[:, COL_OUT[k] : COL_OUT[k] + 128]
        feed_in[l] = part[:, COL_FEED:COL_DOWN]
        for a in range(4):
            feed_out[l, 8 * a : 8 * a + 8, :] = part[:, COL_DOWN + 128 * a : COL_DOWN + 128 * a + 128]
    for c in range(2):
        parts = [slice(256 * k, 256 * k + 256) for k in range(16)]
        tiles = [jnp.where(dp == c, small_mine[:, part], small_other[:, part]) for part in parts]
        blocks = [jnp.concatenate([tile[:, :128], tile[:, 128:]], axis=0) for tile in tiles]
        for k in range(8):
            tokens[c, 16 * k : 16 * k + 16, :] = blocks[k]
        for k in range(4):
            for row in range(10):
                prompt[row, 4 * c + k : 4 * c + k + 1, :] = blocks[8 + k][row : row + 1]
                adjust_prompt[row, 4 * c + k : 4 * c + k + 1, :] = blocks[12 + k][row : row + 1]
            gains[c, k : k + 1, :] = blocks[8 + k][10:11]
            scales[c, k : k + 1, :] = blocks[8 + k][11:12]
        if c == 0:
            cls[...] = blocks[8][12:13]
            adjust_cls[...] = blocks[12][12:13]


def four(first, rest):
    return (first.astype(F32) + rest[0].astype(F32)) + (rest[1].astype(F32) + rest[2].astype(F32))


def reduce_all(big_mine, big_other, small_mine, small_other):
    big = (big_mine.astype(F32) + flip(big_other, "dp", 0, 2).astype(F32)).astype(BF)
    small = (small_mine + flip(small_other, "dp", 0, 2)).astype(BF)
    got = [swap(jnp.concatenate([big[xy], small], axis=2), xy) for xy in range(1, 4)]
    big = four(big[0], [part[:, :, :COLS] for part in got]).astype(BF)
    small = four(small, [part[:, :, COLS:] for part in got]).astype(BF)
    small = jnp.concatenate([small[at] for at in range(4)], axis=1)
    got = [swap(jnp.concatenate([big[z], small], axis=1), 4 * z) for z in range(1, 4)]
    big = four(big[0], [part[:, :COLS] for part in got])
    small = four(small, [part[:, COLS:] for part in got])
    return call(
        final_kernel, "final",
        [shape_of((2, 2, 8, 384)), shape_of((2, 2, 8, 128)), shape_of((2, 8, 1024)), shape_of((2, 32, 128)), shape_of((2, 128, 128)),
         shape_of((2, 4, 128)), shape_of((2, 4, 128)), shape_of((10, 8, 128)), shape_of((1, 128)), shape_of((10, 8, 128)), shape_of((1, 128))],
        "vvvv", [], big, flip(big, "dp", 0, 2), small, flip(small, "dp", 0, 2),
    )


def per_device(shard_count, patches, prompts, cls_token, attn_in, attn_out, feed_in, feed_out, token_operator,
               norm_gains, branch_scales, var_counts, dataset_ids, cotangent, adjust_cotangent):
    fast = shard_count == SHARDS
    turned = call(
        prepare_kernel, "prepare", [shape_of((3, 4, 128, 256), BF)], "svvvvv", [pltpu.VMEM((8, 128, 128), F32)],
        dataset_ids, patches, prompts, cls_token.reshape(1, -1), cotangent, adjust_cotangent,
        cost=pl.CostEstimate(flops=10**6, bytes_accessed=8 * 10**6, transcendentals=0),
    )[0]
    if fast:
        gathered, turned = gather_rows(attn_in, attn_out, feed_in, feed_out, turned)
    else:
        whole_down = lax.all_gather(feed_out, "fsdp", axis=1, tiled=True)
        whole_down = whole_down.reshape(2, SHARDS, 4, 8, 128).transpose(0, 2, 1, 3, 4).reshape(2, 512, 128)
        rows = pack_rows(
            lax.all_gather(attn_in, "fsdp", axis=2, tiled=True),
            lax.all_gather(attn_out, "fsdp", axis=2, tiled=True),
            lax.all_gather(feed_in, "fsdp", axis=1, tiled=True),
            whole_down,
        )
        rows = rows.reshape(2, SHARDS, 8, COLS).transpose(1, 0, 2, 3)
        gathered = [rows[:, l].reshape(4, 4, 8, COLS)[:, xy] for l in range(2) for xy in range(4)]
    output, patch_grad, *sums = run_tower(
        fast, dataset_ids, var_counts, *gathered, token_operator, norm_gains, branch_scales, turned
    )
    if fast:
        (attn_in_g, attn_out_g, feed_in_g, feed_out_g, token_g, gains_g, scales_g, prompt_g, cls_g, adjust_prompt_g,
         adjust_cls_g) = reduce_all(*sums)
        return (output, patch_grad, prompt_g.transpose(1, 0, 2), cls_g[0], attn_in_g, attn_out_g, feed_in_g, feed_out_g, token_g, gains_g,
                scales_g, adjust_prompt_g.transpose(1, 0, 2), adjust_cls_g[0])
    rows = jnp.stack(sums[:2]).transpose(0, 2, 1, 3, 4).astype(F32).reshape(2, 128, COLS)
    attn_in_g, attn_out_g, feed_in_g, feed_out_g = unpack_rows(rows)
    feed_out_g = feed_out_g.reshape(2, 4, SHARDS, 8, 128).transpose(0, 2, 1, 3, 4).reshape(2, 512, 128)
    matrices = (
        lax.psum_scatter(lax.psum(attn_in_g, "dp"), "fsdp", scatter_dimension=2, tiled=True),
        lax.psum_scatter(lax.psum(attn_out_g, "dp"), "fsdp", scatter_dimension=2, tiled=True),
        lax.psum_scatter(lax.psum(feed_in_g, "dp"), "fsdp", scatter_dimension=1, tiled=True),
        lax.psum_scatter(lax.psum(feed_out_g, "dp"), "fsdp", scatter_dimension=1, tiled=True),
    )
    small = lax.psum(jnp.stack(sums[2:]), ("dp", "fsdp"))
    small = small.reshape(2, 4, 8, 4, 2, 128).transpose(0, 1, 3, 4, 2, 5).reshape(2, 16, 16, 128)
    main, adjust = small[:, 8:12].reshape(8, 16, 128), small[:, 12:].reshape(8, 16, 128)
    return (output, patch_grad, main[:, :10], main[0, 12], *matrices, small[:, :8].reshape(2, 128, 128),
            main[:, 10].reshape(2, 4, 128), main[:, 11].reshape(2, 4, 128), adjust[:, :10], adjust[0, 12])


def solution(mesh):
    batch = P(("dp", "fsdp"), None, None, None)
    wide = P(None, None, "fsdp", None)
    tall = P(None, "fsdp", None)
    return jax.shard_map(
        functools.partial(per_device, mesh.shape["fsdp"]),
        mesh=mesh,
        in_specs=(batch, P(), P(), wide, wide, tall, tall, P(), P(), P(), P(), P(("dp", "fsdp")), batch, batch),
        out_specs=(batch, batch, P(), P(), wide, wide, tall, tall, P(), P(), P(), P(), P()),
        check_vma=False,
    )
```

```python
import functools

import jax
import jax.numpy as jnp
from jax import lax
from jax.experimental import pallas as pl
from jax.experimental.pallas import tpu as pltpu
from jax.sharding import PartitionSpec as P

HEADS = 8
EPSILON = 1e-05
NEG_FILL = -1000000000.0
BF = jnp.bfloat16
F32 = jnp.float32

COL_IN = (0, 384)
COL_OUT = (768, 896)
COL_FEED = 1024
COL_DOWN = 2048
COLS = 2560
SHARDS = 16
STEP_BITS = (2, 3, 0, 1)


def dot_nn(a, b):
    return lax.dot_general(a, b, (((1,), (0,)), ((), ())), preferred_element_type=F32)


def dot_nt(a, b):
    return lax.dot_general(a, b, (((1,), (1,)), ((), ())), preferred_element_type=F32)


def norm_cols(x):
    centered = x - jnp.mean(x, axis=0, keepdims=True)
    inv = lax.rsqrt(jnp.mean(centered * centered, axis=0, keepdims=True) + EPSILON)
    return centered * inv, inv


def norm_cols_back(dn, gain, xhat, inv):
    e = dn * gain
    both = e * xhat
    m1 = jnp.mean(e, axis=0, keepdims=True)
    m2 = jnp.mean(both, axis=0, keepdims=True)
    return inv * (e - m1 - xhat * m2), both


def fold(part):
    return part[:, :128] + part[:, 128:]


def pack_kernel(attn_in_ref, attn_out_ref, feed_in_ref, feed_out_ref, out_ref):
    l = lax.axis_index("dp")
    down = feed_out_ref[l].astype(F32)
    parts = [attn_in_ref[l, 0], attn_in_ref[l, 1], attn_out_ref[l, 0], attn_out_ref[l, 1], feed_in_ref[l]]
    parts = [part.astype(F32) for part in parts] + [down[8 * a : 8 * a + 8] for a in range(4)]
    out_ref[0] = jnp.concatenate(parts, axis=1).astype(BF)


def prepare_kernel(ids_ref, patches_ref, prompts_ref, cls_ref, cot_ref, adj_ref, turned_ref, tok_ref):
    for b in range(2):
        ident = ids_ref[b]
        for v in range(4):
            at = 4 * b + v
            lanes = slice(128 * (v % 2), 128 * (v % 2) + 128)
            tok_ref[at, 0:10, :] = prompts_ref[ident].astype(F32)
            tok_ref[at, 10:127, :] = patches_ref[b, v].astype(F32)
            tok_ref[at, 127:128, :] = cls_ref[...].astype(F32)
            turned_ref[0, 2 * b + v // 2, :, lanes] = tok_ref[at].T.astype(BF)
            turned_ref[1, 2 * b + v // 2, :, lanes] = cot_ref[b, v].T
            turned_ref[2, 2 * b + v // 2, :, lanes] = adj_ref[b, v].T


def tower_kernel(
    split,
    ids_ref, counts_ref, wmine0_ref, wmine1_ref, wmine2_ref, wmine3_ref, wother0_ref, wother1_ref, wother2_ref, wother3_ref,
    tok_ref, gains_ref, scales_ref, turned_ref,
    out_ref, pgrad_ref, bigmine_ref, bigother_ref, smallmine_ref, smallother_ref,
    stage_ref, w_ref, wd_ref, wt_ref, wdt_ref, colb_ref, tokscr_ref, h_ref, g_ref, xh_ref, inv_ref,
    qkvt_ref, pb_ref, ot_ref, qkvv_ref, pv_ref, ov_ref, pw_ref, qbd_ref, dob_ref, hid_ref, du_ref, dqkv_ref,
    dov_ref, ga_ref, gd_ref, gt_ref, gacc_ref, gbig_ref, pacc_ref, spread_ref, act_ref, slope_ref, gdt_ref, both_ref, dop_ref,
):
    dp = lax.axis_index("dp") if split else 0
    me = lax.axis_index("fsdp") if split else 0
    layers = 2
    chunks = 4
    items = 2

    for rel in range(SHARDS):
        rows = pl.ds(pl.multiple_of(8 * (me ^ rel), 8), 8)
        mine_ref = (wmine0_ref, wmine1_ref, wmine2_ref, wmine3_ref)[rel % 4]
        other_ref = (wother0_ref, wother1_ref, wother2_ref, wother3_ref)[rel % 4]
        stage_ref[dp, rows, :] = mine_ref[rel // 4].astype(F32)
        stage_ref[1 - dp, rows, :] = other_ref[rel // 4].astype(F32)
    for l in range(layers):
        for k in range(4):
            for offset, rows in ((0, gains_ref), (4, scales_ref)):
                col = jnp.broadcast_to(rows[l, k : k + 1, :], (128, 128)).T
                colb_ref[l * 8 + offset + k, :, 0:128] = col
                colb_ref[l * 8 + offset + k, :, 128:256] = col

    h_ref[...] = turned_ref[0].astype(F32)
    g_ref[...] = turned_ref[1:3].astype(F32)

    head_row = lax.broadcasted_iota(jnp.int32, (8, 128), 0)
    head_col = lax.broadcasted_iota(jnp.int32, (8, 128), 1) // 16
    gather_heads = jnp.where(head_row == head_col, 1.0, 0.0).astype(BF)
    def spread_of(at, j):
        lanes = slice(128 * j, 128 * j + 128)
        return jnp.concatenate([jnp.broadcast_to(spread_ref[at, h : h + 1, lanes], (16, 128)) for h in range(HEADS)], axis=0)

    def head_sums(left, rights):
        return dot_nn(gather_heads, jnp.concatenate([(left * right).astype(BF) for right in rights], axis=1))

    def diag_heads(target_ref, at, rows):
        for head in range(HEADS):
            target_ref[at, 16 * head : 16 * head + 16, 128 * head : 128 * head + 128] = rows[16 * head : 16 * head + 16]

    both_ref[...] = jnp.zeros_like(both_ref)
    for half in range(2):
        both_ref[:, 128 * half : 128 * half + 128, 128 * half : 128 * half + 128] = tok_ref[...]
    dop_ref[...] = jnp.zeros_like(dop_ref)
    qbd_ref[...] = jnp.zeros_like(qbd_ref)
    dob_ref[...] = jnp.zeros_like(dob_ref)

    def gain(l, k):
        return colb_ref[l * 8 + k]

    def scale(l, k):
        return colb_ref[l * 8 + 4 + k]

    def keep_norm(l, k, c, x):
        xhat, inv = norm_cols(x)
        xh_ref[l * 4 + k, c] = xhat
        inv_ref[l * 4 + k, c] = inv
        return (xhat * gain(l, k)).astype(BF)

    def time_forward(l, c):
        x = h_ref[c]
        n = keep_norm(l, 0, c, x)
        qkv = dot_nn(wt_ref[l, 0:384, :], n)
        queries = (qkv[:128] * 0.25).astype(BF)
        keys = qkv[128:256].astype(BF)
        values = qkv[256:].astype(BF)
        qkvt_ref[l, c, 0:128, :] = queries
        qkvt_ref[l, c, 128:256, :] = keys
        qkvt_ref[l, c, 256:384, :] = values
        for s in range(2):
            lanes = slice(128 * s, 128 * s + 128)
            at = 2 * (c % 2) + s
            diag_heads(qbd_ref, at, queries[:, lanes])
            key_rows = keys[:, lanes].T
            for hp in range(4):
                span = slice(256 * hp, 256 * hp + 256)
                rows = slice(32 * hp, 32 * hp + 32)
                scores = dot_nn(key_rows, qbd_ref[at, :, span])
                shifted = jnp.exp(scores - jnp.max(scores, axis=0, keepdims=True))
                prob = (shifted * (1.0 / jnp.sum(shifted, axis=0, keepdims=True))).astype(BF)
                pb_ref[l, 2 * c + s, :, span] = prob
                mixed = dot_nn(values[rows, lanes], prob)
                ot_ref[l, c, 32 * hp : 32 * hp + 16, lanes] = mixed[:16, :128].astype(BF)
                ot_ref[l, c, 32 * hp + 16 : 32 * hp + 32, lanes] = mixed[16:, 128:].astype(BF)
        branch = dot_nn(wt_ref[l, COL_OUT[0] : COL_OUT[0] + 128, :], ot_ref[l, c])
        h_ref[c] = x + scale(l, 0) * branch

    def var_forward(l, b):
        for cc in range(2):
            c = 2 * b + cc
            n = keep_norm(l, 1, c, h_ref[c])
            qkv = dot_nn(wt_ref[l, COL_IN[1] : COL_IN[1] + 384, :], n)
            qkvv_ref[l, c, 0:128, :] = (qkv[:128] * 0.25).astype(BF)
            qkvv_ref[l, c, 128:384, :] = qkv[128:].astype(BF)
        count = counts_ref[ids_ref[b]]

        def slot(first, i):
            lanes = slice(128 * (i % 2), 128 * (i % 2) + 128)
            return qkvv_ref[l, 2 * b + i // 2, first : first + 128, lanes].astype(F32)

        key_slots = [slot(128, j) for j in range(4)]
        value_slots = [slot(256, j) for j in range(4)]
        for i in range(4):
            scores = head_sums(slot(0, i), key_slots)
            parts = [scores[:, 128 * j : 128 * j + 128] for j in range(4)]
            parts = [jnp.where(jnp.full((8, 128), count, jnp.int32) > j, parts[j], NEG_FILL) for j in range(4)]
            top = jnp.maximum(jnp.maximum(parts[0], parts[1]), jnp.maximum(parts[2], parts[3]))
            shifted = [jnp.exp(part - top) for part in parts]
            total = 1.0 / ((shifted[0] + shifted[1]) + (shifted[2] + shifted[3]))
            prob = jnp.concatenate([part * total for part in shifted], axis=1)
            pv_ref[l, b, i] = prob
            spread_ref[4 * b + i] = prob.astype(BF).astype(F32)
            mixed = None
            for j in range(4):
                spread = spread_of(4 * b + i, j)
                pw_ref[l, b, i, :, 128 * j : 128 * j + 128] = spread.astype(BF)
                mixed = spread * value_slots[j] if mixed is None else mixed + spread * value_slots[j]
            lanes = slice(128 * (i % 2), 128 * (i % 2) + 128)
            ov_ref[l, 2 * b + i // 2, :, lanes] = mixed.astype(BF)
        for cc in range(2):
            c = 2 * b + cc
            branch = dot_nn(wt_ref[l, COL_OUT[1] : COL_OUT[1] + 128, :], ov_ref[l, c])
            h_ref[c] = h_ref[c] + scale(l, 1) * branch

    def tail_forward(l, c):
        x = h_ref[c]
        n = keep_norm(l, 2, c, x)
        x = x + scale(l, 2) * dot_nt(n, both_ref[l])
        n = keep_norm(l, 3, c, x)
        for z in range(4):
            rows = slice(128 * z, 128 * z + 128)
            gate = dot_nn(wt_ref[l, COL_FEED + 128 * z : COL_FEED + 128 * z + 128, :], n)
            up = dot_nn(wt_ref[l, COL_FEED + 512 + 128 * z : COL_FEED + 640 + 128 * z, :], n)
            sig = 0.5 * jnp.tanh(0.5 * gate) + 0.5
            act = gate * sig
            hid_ref[l, c, rows, :] = (act * up).astype(BF)
            act_ref[l, c, rows, :] = act.astype(BF)
            slope_ref[l, c, rows, :] = (up * (sig * (1.0 + gate * (1.0 - sig)))).astype(BF)
        h_ref[c] = x + scale(l, 3) * dot_nn(wdt_ref[l], hid_ref[l, c])

    def norm_of(l, k, c):
        xhat = xh_ref[l * 4 + k, c]
        return xhat, inv_ref[l * 4 + k, c], (xhat * gain(l, k)).astype(BF)

    def pass_on(l, k, c, x, dn, xhat, inv):
        back, both = norm_cols_back(dn, gain(l, k), xhat, inv)
        if x == 0:
            gacc_ref[l * 4 + k] += fold(both)
        g_ref[x, c] += back

    def feed_backward(l, c):
        xhat, inv, n = norm_of(l, 3, c)
        dz = [(scale(l, 3) * g_ref[x, c]).astype(BF) for x in range(2)]
        for z in range(4):
            rows = slice(128 * z, 128 * z + 128)
            act = act_ref[l, c, rows, :].astype(F32)
            slope = slope_ref[l, c, rows, :].astype(F32)
            for x in range(2):
                dhid = dot_nn(wd_ref[l, rows, :], dz[x])
                du_ref[2 * (c % 2) + x, 128 * z : 128 * z + 128, :] = (dhid * slope).astype(BF)
                du_ref[2 * (c % 2) + x, 512 + 128 * z : 640 + 128 * z, :] = (dhid * act).astype(BF)
        ga_ref[:, COL_FEED:COL_DOWN] += dot_nt(n, du_ref[2 * (c % 2)])
        gdt_ref[...] += dot_nt(dz[0], hid_ref[l, c])
        for x in range(2):
            dn = dot_nn(w_ref[l, :, COL_FEED:COL_DOWN], du_ref[2 * (c % 2) + x])
            pass_on(l, 3, c, x, dn, xhat, inv)

    def token_backward(l, c):
        xhat, inv, n = norm_of(l, 2, c)
        for x in range(2):
            dy = (scale(l, 2) * g_ref[x, c]).astype(BF)
            if x == 0:
                turned = jnp.concatenate([dy[:, :128].T, dy[:, 128:].T], axis=1)
                gt_ref[l] += dot_nn(turned, jnp.concatenate([n[:, :128], n[:, 128:]], axis=0))
            pass_on(l, 2, c, x, dot_nn(dy, both_ref[l]), xhat, inv)

    def var_backward(l, b):
        def slot(first, i):
            lanes = slice(128 * (i % 2), 128 * (i % 2) + 128)
            return qkvv_ref[l, 2 * b + i // 2, first : first + 128, lanes].astype(F32)

        for x in range(2):
            for cc in range(2):
                c = 2 * b + cc
                dt = (scale(l, 1) * g_ref[x, c]).astype(BF)
                dov_ref[4 * b + 2 * x + cc] = dot_nn(w_ref[l, :, COL_OUT[1] : COL_OUT[1] + 128], dt).astype(BF)
                if x == 0:
                    ga_ref[:, COL_OUT[1] : COL_OUT[1] + 128] += dot_nt(ov_ref[l, c], dt)
            value_slots = [slot(256, j) for j in range(4)]
            dkeys = [0.0] * 4
            dvalues = [0.0] * 4
            for i in range(4):
                lanes = slice(128 * (i % 2), 128 * (i % 2) + 128)
                grad = dov_ref[4 * b + 2 * x + i // 2, :, lanes].astype(F32)
                query = slot(0, i)
                prob = pv_ref[l, b, i]
                weighted = prob * head_sums(grad, value_slots)
                total = (weighted[:, :128] + weighted[:, 128:256]) + (weighted[:, 256:384] + weighted[:, 384:])
                ds = weighted - prob * jnp.concatenate([total] * 4, axis=1)
                spread_ref[8 * b + 4 * x + i] = ds.astype(BF).astype(F32)
                ds_slots = [spread_of(8 * b + 4 * x + i, j) for j in range(4)]
                terms = [ds_slots[j] * slot(128, j) for j in range(4)]
                dquery = (terms[0] + terms[1]) + (terms[2] + terms[3])
                for j in range(4):
                    dkeys[j] = dkeys[j] + ds_slots[j] * query
                    dvalues[j] = dvalues[j] + pw_ref[l, b, i, :, 128 * j : 128 * j + 128].astype(F32) * grad
                dqkv_ref[4 * b + 2 * x + i // 2, 0:128, lanes] = (dquery * 0.25).astype(BF)
            for j in range(4):
                lanes = slice(128 * (j % 2), 128 * (j % 2) + 128)
                dqkv_ref[4 * b + 2 * x + j // 2, 128:256, lanes] = dkeys[j].astype(BF)
                dqkv_ref[4 * b + 2 * x + j // 2, 256:384, lanes] = dvalues[j].astype(BF)
            for cc in range(2):
                c = 2 * b + cc
                xhat, inv, n = norm_of(l, 1, c)
                dqkv = dqkv_ref[4 * b + 2 * x + cc]
                if x == 0:
                    ga_ref[:, COL_IN[1] : COL_IN[1] + 384] += dot_nt(n, dqkv)
                pass_on(l, 1, c, x, dot_nn(w_ref[l, :, COL_IN[1] : COL_IN[1] + 384], dqkv), xhat, inv)

    def time_backward(l, c):
        xhat, inv, n = norm_of(l, 0, c)
        queries = qkvt_ref[l, c, 0:128, :]
        keys = qkvt_ref[l, c, 128:256, :]
        values = qkvt_ref[l, c, 256:384, :]
        grads = []
        for x in range(2):
            dt = (scale(l, 0) * g_ref[x, c]).astype(BF)
            grads.append(dot_nn(w_ref[l, :, COL_OUT[0] : COL_OUT[0] + 128], dt).astype(BF))
            if x == 0:
                ga_ref[:, COL_OUT[0] : COL_OUT[0] + 128] += dot_nt(ot_ref[l, c], dt)
        for s in range(2):
            lanes = slice(128 * s, 128 * s + 128)
            at = 2 * (c % 2) + s
            diag_heads(qbd_ref, at, queries[:, lanes])
            value_rows = values[:, lanes].T
            for x in range(2):
                diag_heads(dob_ref, 2 * at + x, grads[x][:, lanes])
                for head in range(HEADS):
                    first = 64 * (head // 2) + 32 * x + 16 * (head % 2)
                    half = slice(128 * (head % 2), 128 * (head % 2) + 128)
                    dop_ref[at, first : first + 16, half] = grads[x][16 * head : 16 * head + 16, lanes]
            for hp in range(4):
                span = slice(256 * hp, 256 * hp + 256)
                rows = slice(32 * hp, 32 * hp + 32)
                prob_bf = pb_ref[l, 2 * c + s, :, span]
                prob = prob_bf.astype(F32)
                dvalue = dot_nt(dop_ref[at, 64 * hp : 64 * hp + 64, :], prob_bf).astype(BF)
                for x in range(2):
                    weighted = prob * dot_nn(value_rows, dob_ref[2 * at + x, :, span])
                    ds = (weighted - prob * jnp.sum(weighted, axis=0, keepdims=True)).astype(BF)
                    dquery = dot_nn(keys[rows, lanes], ds) * 0.25
                    dkey = dot_nt(qbd_ref[at, rows, span], ds)
                    dqkv_ref[2 * c + x, 32 * hp : 32 * hp + 16, lanes] = dquery[:16, :128].astype(BF)
                    dqkv_ref[2 * c + x, 32 * hp + 16 : 32 * hp + 32, lanes] = dquery[16:, 128:].astype(BF)
                    dqkv_ref[2 * c + x, 128 + 32 * hp : 160 + 32 * hp, lanes] = dkey.astype(BF)
                    dqkv_ref[2 * c + x, 256 + 32 * hp : 288 + 32 * hp, lanes] = dvalue[32 * x : 32 * x + 32]
        ga_ref[:, COL_IN[0] : COL_IN[0] + 384] += dot_nt(n, dqkv_ref[2 * c])
        for x in range(2):
            pass_on(l, 0, c, x, dot_nn(w_ref[l, :, COL_IN[0] : COL_IN[0] + 384], dqkv_ref[2 * c + x]), xhat, inv)

    def each(count, stage, l):
        for i in range(count):
            stage(l, i)

    def forward_layer(l, carry):
        for pair in range(SHARDS // 2):
            lo = stage_ref[l, 16 * pair : 16 * pair + 8, :]
            hi = stage_ref[l, 16 * pair + 8 : 16 * pair + 16, :]
            w_ref[l, 16 * pair : 16 * pair + 16, :] = jnp.concatenate([lo[:, :COL_DOWN], hi[:, :COL_DOWN]], axis=0).astype(BF)
            for half, part in enumerate((lo, hi)):
                base = 64 * pair + 32 * half
                wd_ref[l, base : base + 32, :] = jnp.concatenate(
                    [part[:, COL_DOWN + 128 * a : COL_DOWN + 128 * a + 128] for a in range(4)], axis=0
                ).astype(BF)
        for block in range(COL_DOWN // 128):
            wt_ref[l, 128 * block : 128 * block + 128, :] = w_ref[l, :, 128 * block : 128 * block + 128].T
        for block in range(4):
            wdt_ref[l, :, 128 * block : 128 * block + 128] = wd_ref[l, 128 * block : 128 * block + 128, :].T
        each(chunks, time_forward, l)
        each(items, var_forward, l)
        each(chunks, tail_forward, l)
        return carry

    lax.fori_loop(0, layers, forward_layer, 0)
    for b in range(items):
        for v in range(4):
            lanes = slice(128 * (v % 2), 128 * (v % 2) + 128)
            out_ref[b, v] = h_ref[2 * b + v // 2, :, lanes].T.astype(BF)

    gacc_ref[...] = jnp.zeros_like(gacc_ref)
    gt_ref[...] = jnp.zeros_like(gt_ref)
    pacc_ref[...] = jnp.zeros_like(pacc_ref)

    def backward_layer(step, carry):
        l = layers - 1 - step
        ga_ref[...] = jnp.zeros_like(ga_ref)
        gdt_ref[...] = jnp.zeros_like(gdt_ref)
        each(chunks, feed_backward, l)
        each(chunks, token_backward, l)
        each(items, var_backward, l)
        each(chunks, time_backward, l)
        for k in range(4):
            gd_ref[128 * k : 128 * k + 128, :] = gdt_ref[:, 128 * k : 128 * k + 128].T
        for f in range(SHARDS):
            down = jnp.concatenate([gd_ref[32 * f + 8 * a : 32 * f + 8 * a + 8, :] for a in range(4)], axis=1)
            block = jnp.concatenate([ga_ref[8 * f : 8 * f + 8, :], down], axis=1)
            gbig_ref[l, f] = block.astype(BF)
        gains_rows = [jnp.sum(gacc_ref[l * 4 + k].T, axis=0, keepdims=True) for k in range(4)]
        sums = [
            jnp.sum(w_ref[l, :, COL_OUT[k] : COL_OUT[k] + 128].astype(F32) * ga_ref[:, COL_OUT[k] : COL_OUT[k] + 128], axis=0, keepdims=True)
            for k in range(2)
        ]
        sums.append(gains_rows[2])
        sums.append(jnp.sum(wd_ref[l].astype(F32) * gd_ref[...], axis=0, keepdims=True))
        for k in range(4):
            pacc_ref[0, l * 4 + k, 10:11, :] = gains_rows[k] / gains_ref[l, k : k + 1, :]
            pacc_ref[0, l * 4 + k, 11:12, :] = sums[k] / scales_ref[l, k : k + 1, :]
        return carry

    lax.fori_loop(0, layers, backward_layer, 0)

    for x in range(2):
        cls_sum = None
        for b in range(items):
            prompt_sum = None
            for v in range(4):
                lanes = slice(128 * (v % 2), 128 * (v % 2) + 128)
                tokscr_ref[4 * b + v] = g_ref[x, 2 * b + v // 2, :, lanes].T
                head = tokscr_ref[4 * b + v, 0:10, :]
                last = tokscr_ref[4 * b + v, 127:128, :]
                prompt_sum = head if prompt_sum is None else prompt_sum + head
                cls_sum = last if cls_sum is None else cls_sum + last
                if x == 0:
                    pgrad_ref[b, v] = tokscr_ref[4 * b + v, 10:127, :]
            pacc_ref[x, ids_ref[b], 0:10, :] += prompt_sum
        pacc_ref[x, 0, 12:13, :] = cls_sum

    for big_ref, small_ref, c in ((bigmine_ref, smallmine_ref, dp), (bigother_ref, smallother_ref, 1 - dp)):
        for rel in range(SHARDS):
            big_ref[rel % 4, rel // 4] = gbig_ref[c, me ^ rel]
        for block in range(16):
            if block < 8:
                pair = gt_ref[c, 16 * block : 16 * block + 16, :]
            else:
                pair = pacc_ref[block // 4 - 2, 4 * c + block % 4]
            lanes = slice(256 * (block % 4), 256 * (block % 4) + 256)
            small_ref[block // 4, :, lanes] = jnp.concatenate([pair[:8], pair[8:]], axis=1)


def call(kernel, name, out_shape, in_spaces, scratch, *operands, cost=None):
    spaces = {"v": pltpu.VMEM, "s": pltpu.SMEM}
    return pl.pallas_call(
        kernel,
        out_shape=out_shape,
        in_specs=[pl.BlockSpec(memory_space=spaces[space]) for space in in_spaces],
        out_specs=[pl.BlockSpec(memory_space=pltpu.VMEM)] * len(out_shape),
        scratch_shapes=scratch,
        compiler_params=pltpu.CompilerParams(vmem_limit_bytes=58 * 1024 * 1024),
        cost_estimate=cost,
        name=name,
    )(*operands)


def shape_of(shape, kind=F32):
    return jax.ShapeDtypeStruct(shape, kind)


def run_tower(split, *operands):
    half = [shape_of((4, 4, 8, COLS), BF)] * 2 + [shape_of((4, 8, 1024))] * 2
    return call(
        functools.partial(tower_kernel, split),
        "tower",
        [shape_of((2, 4, 128, 128), BF), shape_of((2, 4, 117, 128))] + half,
        "ss" + "v" * 12,
        [
            pltpu.VMEM((2, 128, COLS), F32),
            pltpu.VMEM((2, 128, COL_DOWN), BF),
            pltpu.VMEM((2, 512, 128), BF),
            pltpu.VMEM((2, COL_DOWN, 128), BF),
            pltpu.VMEM((2, 128, 512), BF),
            pltpu.VMEM((16, 128, 256), F32),
            pltpu.VMEM((8, 128, 128), F32),
            pltpu.VMEM((4, 128, 256), F32),
            pltpu.VMEM((2, 4, 128, 256), F32),
            pltpu.VMEM((8, 4, 128, 256), F32),
            pltpu.VMEM((8, 4, 1, 256), F32),
            pltpu.VMEM((2, 4, 384, 256), BF),
            pltpu.VMEM((2, 8, 128, 1024), BF),
            pltpu.VMEM((2, 4, 128, 256), BF),
            pltpu.VMEM((2, 4, 384, 256), BF),
            pltpu.VMEM((2, 2, 4, 8, 512), F32),
            pltpu.VMEM((2, 4, 128, 256), BF),
            pltpu.VMEM((2, 2, 4, 128, 512), BF),
            pltpu.VMEM((4, 128, 1024), BF),
            pltpu.VMEM((8, 128, 1024), BF),
            pltpu.VMEM((2, 4, 512, 256), BF),
            pltpu.VMEM((4, 1024, 256), BF),
            pltpu.VMEM((8, 384, 256), BF),
            pltpu.VMEM((8, 128, 256), BF),
            pltpu.VMEM((128, COL_DOWN), F32),
            pltpu.VMEM((512, 128), F32),
            pltpu.VMEM((2, 128, 128), F32),
            pltpu.VMEM((8, 128, 128), F32),
            pltpu.VMEM((2, SHARDS, 8, COLS), BF),
            pltpu.VMEM((2, 8, 16, 128), F32),
            pltpu.VMEM((16, 8, 512), F32),
            pltpu.VMEM((2, 4, 512, 256), BF),
            pltpu.VMEM((2, 4, 512, 256), BF),
            pltpu.VMEM((128, 512), F32),
            pltpu.VMEM((2, 256, 256), BF),
            pltpu.VMEM((4, 256, 256), BF),
        ],
        *operands,
        cost=pl.CostEstimate(flops=10**10, bytes_accessed=20 * 10**6, transcendentals=0),
    )


def pack_rows(attn_in, attn_out, feed_in, feed_out):
    layers, _, rows, _ = attn_in.shape
    down = feed_out.reshape(layers, 4, rows, 128)
    return jnp.concatenate(
        [attn_in[:, 0], attn_in[:, 1], attn_out[:, 0], attn_out[:, 1], feed_in] + [down[:, a] for a in range(4)], axis=2
    )


def unpack_rows(packed):
    layers, rows, _ = packed.shape
    attn_in = jnp.stack([packed[:, :, at : at + 384] for at in COL_IN], axis=1)
    attn_out = jnp.stack([packed[:, :, at : at + 128] for at in COL_OUT], axis=1)
    feed_in = packed[:, :, COL_FEED:COL_DOWN]
    feed_out = jnp.stack([packed[:, :, COL_DOWN + 128 * a : COL_DOWN + 128 * a + 128] for a in range(4)], axis=1)
    return attn_in, attn_out, feed_in, feed_out.reshape(layers, 4 * rows, 128)


def flip(array, axis, bit, size):
    return lax.ppermute(array, axis, [(i, i ^ (1 << bit)) for i in range(size)])


def swap(array, mask):
    return lax.ppermute(array, "fsdp", [(i, i ^ mask) for i in range(SHARDS)])


def gather_rows(attn_in, attn_out, feed_in, feed_out, turned):
    row = call(pack_kernel, "pack", [shape_of((1, 8, COLS), BF)], "vvvv", [], attn_in, attn_out, feed_in, feed_out)[0]
    column = jnp.concatenate([row] + [swap(row, 4 * z) for z in range(1, 4)], axis=0)
    mine = [column] + [swap(column, xy) for xy in range(1, 4)]
    mine, turned = lax.optimization_barrier((mine, turned))
    return mine + [flip(part, "dp", 0, 2) for part in mine], turned


def final_kernel(big_mine, big_other, small_mine, small_other, attn_in, attn_out, feed_in, feed_out, tokens, gains, scales,
                 prompt, cls, adjust_prompt, adjust_cls):
    dp = lax.axis_index("dp")
    for part, l in ((big_mine, dp), (big_other, 1 - dp)):
        for k in range(2):
            attn_in[l, k] = part[:, COL_IN[k] : COL_IN[k] + 384]
            attn_out[l, k] = part[:, COL_OUT[k] : COL_OUT[k] + 128]
        feed_in[l] = part[:, COL_FEED:COL_DOWN]
        for a in range(4):
            feed_out[l, 8 * a : 8 * a + 8, :] = part[:, COL_DOWN + 128 * a : COL_DOWN + 128 * a + 128]
    for c in range(2):
        parts = [slice(256 * k, 256 * k + 256) for k in range(16)]
        tiles = [jnp.where(dp == c, small_mine[:, part], small_other[:, part]) for part in parts]
        blocks = [jnp.concatenate([tile[:, :128], tile[:, 128:]], axis=0) for tile in tiles]
        for k in range(8):
            tokens[c, 16 * k : 16 * k + 16, :] = blocks[k]
        for k in range(4):
            for row in range(10):
                prompt[row, 4 * c + k : 4 * c + k + 1, :] = blocks[8 + k][row : row + 1]
                adjust_prompt[row, 4 * c + k : 4 * c + k + 1, :] = blocks[12 + k][row : row + 1]
            gains[c, k : k + 1, :] = blocks[8 + k][10:11]
            scales[c, k : k + 1, :] = blocks[8 + k][11:12]
        if c == 0:
            cls[...] = blocks[8][12:13]
            adjust_cls[...] = blocks[12][12:13]


def four(first, rest):
    return (first.astype(F32) + rest[0].astype(F32)) + (rest[1].astype(F32) + rest[2].astype(F32))


def reduce_all(big_mine, big_other, small_mine, small_other):
    big = (big_mine.astype(F32) + flip(big_other, "dp", 0, 2).astype(F32)).astype(BF)
    small = (small_mine + flip(small_other, "dp", 0, 2)).astype(BF)
    got = [swap(jnp.concatenate([big[xy], small], axis=2), xy) for xy in range(1, 4)]
    big = four(big[0], [part[:, :, :COLS] for part in got]).astype(BF)
    small = four(small, [part[:, :, COLS:] for part in got]).astype(BF)
    small = jnp.concatenate([small[at] for at in range(4)], axis=1)
    got = [swap(jnp.concatenate([big[z], small], axis=1), 4 * z) for z in range(1, 4)]
    big = four(big[0], [part[:, :COLS] for part in got])
    small = four(small, [part[:, COLS:] for part in got])
    return call(
        final_kernel, "final",
        [shape_of((2, 2, 8, 384)), shape_of((2, 2, 8, 128)), shape_of((2, 8, 1024)), shape_of((2, 32, 128)), shape_of((2, 128, 128)),
         shape_of((2, 4, 128)), shape_of((2, 4, 128)), shape_of((10, 8, 128)), shape_of((1, 128)), shape_of((10, 8, 128)), shape_of((1, 128))],
        "vvvv", [], big, flip(big, "dp", 0, 2), small, flip(small, "dp", 0, 2),
    )


def per_device(shard_count, patches, prompts, cls_token, attn_in, attn_out, feed_in, feed_out, token_operator,
               norm_gains, branch_scales, var_counts, dataset_ids, cotangent, adjust_cotangent):
    fast = shard_count == SHARDS
    turned = call(
        prepare_kernel, "prepare", [shape_of((3, 4, 128, 256), BF)], "svvvvv", [pltpu.VMEM((8, 128, 128), F32)],
        dataset_ids, patches, prompts, cls_token.reshape(1, -1), cotangent, adjust_cotangent,
        cost=pl.CostEstimate(flops=10**6, bytes_accessed=8 * 10**6, transcendentals=0),
    )[0]
    if fast:
        gathered, turned = gather_rows(attn_in, attn_out, feed_in, feed_out, turned)
    else:
        whole_down = lax.all_gather(feed_out, "fsdp", axis=1, tiled=True)
        whole_down = whole_down.reshape(2, SHARDS, 4, 8, 128).transpose(0, 2, 1, 3, 4).reshape(2, 512, 128)
        rows = pack_rows(
            lax.all_gather(attn_in, "fsdp", axis=2, tiled=True),
            lax.all_gather(attn_out, "fsdp", axis=2, tiled=True),
            lax.all_gather(feed_in, "fsdp", axis=1, tiled=True),
            whole_down,
        )
        rows = rows.reshape(2, SHARDS, 8, COLS).transpose(1, 0, 2, 3)
        gathered = [rows[:, l].reshape(4, 4, 8, COLS)[:, xy] for l in range(2) for xy in range(4)]
    output, patch_grad, *sums = run_tower(
        fast, dataset_ids, var_counts, *gathered, token_operator, norm_gains, branch_scales, turned
    )
    if fast:
        (attn_in_g, attn_out_g, feed_in_g, feed_out_g, token_g, gains_g, scales_g, prompt_g, cls_g, adjust_prompt_g,
         adjust_cls_g) = reduce_all(*sums)
        return (output, patch_grad, prompt_g.transpose(1, 0, 2), cls_g[0], attn_in_g, attn_out_g, feed_in_g, feed_out_g, token_g, gains_g,
                scales_g, adjust_prompt_g.transpose(1, 0, 2), adjust_cls_g[0])
    rows = jnp.stack(sums[:2]).transpose(0, 2, 1, 3, 4).astype(F32).reshape(2, 128, COLS)
    attn_in_g, attn_out_g, feed_in_g, feed_out_g = unpack_rows(rows)
    feed_out_g = feed_out_g.reshape(2, 4, SHARDS, 8, 128).transpose(0, 2, 1, 3, 4).reshape(2, 512, 128)
    matrices = (
        lax.psum_scatter(lax.psum(attn_in_g, "dp"), "fsdp", scatter_dimension=2, tiled=True),
        lax.psum_scatter(lax.psum(attn_out_g, "dp"), "fsdp", scatter_dimension=2, tiled=True),
        lax.psum_scatter(lax.psum(feed_in_g, "dp"), "fsdp", scatter_dimension=1, tiled=True),
        lax.psum_scatter(lax.psum(feed_out_g, "dp"), "fsdp", scatter_dimension=1, tiled=True),
    )
    small = lax.psum(jnp.stack(sums[2:]), ("dp", "fsdp"))
    small = small.reshape(2, 4, 8, 4, 2, 128).transpose(0, 1, 3, 4, 2, 5).reshape(2, 16, 16, 128)
    main, adjust = small[:, 8:12].reshape(8, 16, 128), small[:, 12:].reshape(8, 16, 128)
    return (output, patch_grad, main[:, :10], main[0, 12], *matrices, small[:, :8].reshape(2, 128, 128),
            main[:, 10].reshape(2, 4, 128), main[:, 11].reshape(2, 4, 128), adjust[:, :10], adjust[0, 12])


def solution(mesh):
    batch = P(("dp", "fsdp"), None, None, None)
    wide = P(None, None, "fsdp", None)
    tall = P(None, "fsdp", None)
    return jax.shard_map(
        functools.partial(per_device, mesh.shape["fsdp"]),
        mesh=mesh,
        in_specs=(batch, P(), P(), wide, wide, tall, tall, P(), P(), P(), P(), P(("dp", "fsdp")), batch, batch),
        out_specs=(batch, batch, P(), P(), wide, wide, tall, tall, P(), P(), P(), P(), P()),
        check_vma=False,
    )
```
